128 devices in a mesh: bin: 8 (over x, z_hi), tile: 16 (over z_lo, y, core).
Axes of the slice: x: 4, y: 4, z: 4 (z_hi: 2, z_lo: 2; z = z_hi * 2 + z_lo), core: 2. Of those that a mesh axis runs over, the one named last changes fastest.
Arguments:
- embeddings: bfloat16 [8192, 512], P('bin'), may hold values from -6 to 6
- w_left: bfloat16 [512, 128], replicated, may hold values from -0.25 to 0.25
- w_right: bfloat16 [512, 128], replicated, may hold values from -0.25 to 0.25
- pair_bias: float32 [5, 128], replicated, may hold values from -3 to 3
- w_pair: bfloat16 [128, 128], replicated, may hold values from -0.5 to 0.5
- b_pair: float32 [128], replicated, may hold values from -3 to 3
- w_out: float32 [128], replicated, may hold values from -0.5 to 0.5
- tile_list: int32 [8, 16, 6, 3], P('bin', 'tile'), may hold values from -1 to 63, as said below
- target: bfloat16 [8, 16, 6, 128, 128], P('bin', 'tile'), may hold values from -6 to 6
Outputs:
- predicted: bfloat16 [8, 16, 6, 128, 128], P('bin', 'tile')
- grad_emb: bfloat16 [8192, 512], P('bin')
- grad_wleft: float32 [512, 128], replicated
- grad_wright: float32 [512, 128], replicated
- grad_bias: float32 [5, 128], replicated
- grad_wpair: float32 [128, 128], replicated
- grad_bpair: float32 [128], replicated
- grad_wout: float32 [128], replicated
The draws below stay inside these ranges and needn't reach their ends.
Inputs may be any that keep to these rules, and one draw needn't show every extreme that they name: `tile_list`: each device's listed tiles come first, then empty slots with -1 in all three fields. A listed tile of a device in bin block b has its row block among b*8 .. (b+1)*8 - 1, offset 0..4, column block = row block + offset, below 64; no tile is listed twice. In every draw one device of each bin block lists 6 tiles.
All inputs are finite; a program needn't handle non-finite values.
Results may differ from the reference program's by a relative error of at most 0.011.
Values may be sent and summed in bfloat16 or wider, within the bound.
No kernel may reach another device: no remote copies, remote signals or barrier semaphores. Data moves between devices by JAX's collectives and lax.ppermute only.
A program may use at most 64 MiB of HBM per device.

```python
import jax
import jax.numpy as jnp
from jax import lax

C = 512
H = 128
TB = 128
BPB = 8
NDIAG = 5
TPD = 6
NB = 8192
N_BIN = 8
N_TILE = 16


def group_lists(group_key, group_index):
    cand_count = BPB * NDIAG
    block_total = BPB * N_BIN
    cand_ids = jnp.arange(cand_count, dtype=jnp.int32)
    cand_rows = group_index * BPB + cand_ids // NDIAG
    cand_offsets = cand_ids % NDIAG
    cand_cols = cand_rows + cand_offsets
    cand_valid = cand_cols < block_total
    key_order, key_counts, key_first = jax.random.split(group_key, 3)
    shuffled = jax.random.permutation(key_order, cand_count).astype(jnp.int32)
    scores = jnp.where(cand_valid, 0, cand_count) + shuffled
    ordering = jnp.argsort(scores)
    valid_total = jnp.sum(cand_valid.astype(jnp.int32))
    device_loads = jnp.minimum(jax.random.randint(key_counts, (N_TILE,), 1, 4), TPD)
    device_loads = device_loads.at[0].set(TPD)
    starts = jnp.cumsum(device_loads) - device_loads
    first_device = jax.random.randint(key_first, (), 0, N_TILE)
    position = (jnp.arange(N_TILE) - first_device) % N_TILE
    dev_start = starts[position]
    dev_load = device_loads[position]
    slot_ids = jnp.arange(TPD)
    flat_pos = dev_start[:, None] + slot_ids[None, :]
    slot_used = (slot_ids[None, :] < dev_load[:, None]) & (flat_pos < valid_total)
    chosen = ordering[jnp.clip(flat_pos, 0, cand_count - 1)]
    listing = jnp.stack([cand_rows[chosen], cand_cols[chosen], cand_offsets[chosen]], axis=-1)
    return jnp.where(slot_used[:, :, None], listing, -1).astype(jnp.int32)


def draw_tile_list(key, part):
    key = jax.random.fold_in(key, 11)
    group_keys = jax.random.split(key, N_BIN)
    return jax.vmap(group_lists)(group_keys, jnp.arange(N_BIN, dtype=jnp.int32))


def shard_levels(key, dims, cuts, least, high):
    factor_of, own = 1.0, jax.random.fold_in(key, 6)
    for dim, blocks in cuts:
        draws = jnp.exp(jax.random.uniform(jax.random.fold_in(own, dim), (blocks,), jnp.float32, least / len(cuts), high / len(cuts)))
        factor_of = factor_of * jnp.repeat(draws, dims[dim] // blocks).reshape([-1 if axis == dim else 1 for axis in range(len(dims))])
    return factor_of


def noise(key, dims, scale, limit, shards=(), kind=jnp.bfloat16):
    result = jax.random.normal(key, dims, jnp.float32) * scale
    if len(shards) > 0:
        result = shard_levels(key, dims, shards, -0.22, 0.18) * result
    return jnp.clip(result, min=-limit, max=limit).astype(kind)


def setup_inputs(seed: int = 0) -> dict:
    streams_of = jax.random.split(jax.random.key(seed), 10)
    return {
        "embeddings": noise(streams_of[0], (NB, C), 1.0, 6.0, ((0, 8),)),
        "w_left": noise(streams_of[1], (C, H), C ** -0.5, 0.25),
        "w_right": noise(streams_of[2], (C, H), C ** -0.5, 0.25),
        "pair_bias": noise(streams_of[3], (NDIAG, H), 0.5, 3.0, (), jnp.float32),
        "w_pair": noise(streams_of[4], (H, H), H ** -0.5, 0.5),
        "b_pair": noise(streams_of[5], (H,), 0.5, 3.0, (), jnp.float32),
        "w_out": noise(streams_of[6], (H,), H ** -0.5, 0.5, (), jnp.float32),
        "tile_list": draw_tile_list(jax.random.fold_in(streams_of[9], 71), 0),
        "target": noise(streams_of[8], (N_BIN, N_TILE, TPD, TB, TB), 1.0, 6.0, ((0, 8), (1, 16))),
    }


def tile_pass(row_panel, col_panel, bias_row, target_tile, w_pair, b_pair, w_out):
    tile_width = row_panel.shape[0]
    feature_count = row_panel.shape[1]
    pre_one = row_panel.astype(jnp.float32)[:, None, :] + col_panel.astype(jnp.float32)[None, :, :] + bias_row
    first_act = jnp.maximum(pre_one, 0.0).astype(jnp.bfloat16).reshape(tile_width * tile_width, feature_count)
    pre_two = jnp.dot(first_act, w_pair, preferred_element_type=jnp.float32) + b_pair
    second_act = jnp.maximum(pre_two, 0.0)
    contact = jnp.sum(second_act * w_out, axis=1)
    residual_slope = (contact - target_tile.reshape(-1).astype(jnp.float32)) / tile_width
    back_two = (residual_slope[:, None] * w_out * (pre_two > 0)).astype(jnp.bfloat16)
    grad_out = jnp.sum(residual_slope[:, None] * second_act, axis=0)
    grad_bpair = jnp.sum(back_two.astype(jnp.float32), axis=0)
    grad_wpair = jnp.dot(first_act.T, back_two, preferred_element_type=jnp.float32)
    back_one = jnp.dot(back_two, w_pair.T, preferred_element_type=jnp.float32).reshape(tile_width, tile_width, feature_count)
    back_one = jnp.where(pre_one > 0, back_one, 0.0)
    return (contact.reshape(tile_width, tile_width).astype(jnp.bfloat16), jnp.sum(back_one, axis=1),
            jnp.sum(back_one, axis=0), jnp.sum(back_one, axis=(0, 1)), grad_wpair, grad_bpair, grad_out)


def reference(embeddings, w_left, w_right, pair_bias, w_pair, b_pair, w_out, tile_list, target):
    left_proj = jnp.dot(embeddings, w_left, preferred_element_type=jnp.float32).astype(jnp.bfloat16)
    right_proj = jnp.dot(embeddings, w_right, preferred_element_type=jnp.float32).astype(jnp.bfloat16)
    flat_list = tile_list.reshape(-1, 3)
    flat_target = target.reshape(-1, TB, TB)
    initial = (jnp.zeros(left_proj.shape, jnp.float32), jnp.zeros(right_proj.shape, jnp.float32),
               jnp.zeros(pair_bias.shape, jnp.float32), jnp.zeros(w_pair.shape, jnp.float32),
               jnp.zeros(b_pair.shape, jnp.float32), jnp.zeros(w_out.shape, jnp.float32))

    def visit_slot(running, scan_item):
        slot_entry, target_tile = scan_item

        def active(running):
            row_grad, col_grad, bias_grad, wpair_grad, bpair_grad, out_grad = running
            start_row = (jnp.maximum(slot_entry[0], 0) * TB).astype(jnp.int32)
            start_col = (jnp.maximum(slot_entry[1], 0) * TB).astype(jnp.int32)
            offset_now = jnp.maximum(slot_entry[2], 0).astype(jnp.int32)
            panel_row = lax.dynamic_slice_in_dim(left_proj, start_row, TB, 0)
            panel_col = lax.dynamic_slice_in_dim(right_proj, start_col, TB, 0)
            bias_row = lax.dynamic_index_in_dim(pair_bias, offset_now, 0, keepdims=False)
            pass_out = tile_pass(panel_row, panel_col, bias_row, target_tile, w_pair, b_pair, w_out)
            row_grad = lax.dynamic_update_slice_in_dim(row_grad, lax.dynamic_slice_in_dim(row_grad, start_row, TB, 0) + pass_out[1], start_row, 0)
            col_grad = lax.dynamic_update_slice_in_dim(col_grad, lax.dynamic_slice_in_dim(col_grad, start_col, TB, 0) + pass_out[2], start_col, 0)
            hits = (jnp.arange(NDIAG).astype(jnp.int32) == offset_now).astype(jnp.float32)
            bias_grad = bias_grad + hits[:, None] * pass_out[3]
            return (row_grad, col_grad, bias_grad, wpair_grad + pass_out[4], bpair_grad + pass_out[5],
                    out_grad + pass_out[6]), pass_out[0]

        def skipped(running):
            return running, jnp.zeros((TB, TB), jnp.bfloat16)

        return lax.cond(slot_entry[2] >= 0, active, skipped, running)

    running, predicted = lax.scan(visit_slot, initial, (flat_list, flat_target))
    row_grad, col_grad, bias_grad, wpair_grad, bpair_grad, out_grad = running
    row_low = row_grad.astype(jnp.bfloat16)
    col_low = col_grad.astype(jnp.bfloat16)
    grad_emb = (jnp.dot(row_low, w_left.T, preferred_element_type=jnp.float32)
                + jnp.dot(col_low, w_right.T, preferred_element_type=jnp.float32)).astype(jnp.bfloat16)
    grad_wleft = jnp.dot(embeddings.T, row_low, preferred_element_type=jnp.float32)
    grad_wright = jnp.dot(embeddings.T, col_low, preferred_element_type=jnp.float32)
    predicted = predicted.reshape(N_BIN, N_TILE, TPD, TB, TB)
    return (predicted, grad_emb, grad_wleft, grad_wright, bias_grad, wpair_grad, bpair_grad, out_grad)
```

```python
import jax
import jax.numpy as jnp
from jax import lax
from jax.experimental import pallas as pl
from jax.experimental.pallas import tpu as pltpu
from jax.sharding import PartitionSpec as P

F32 = jnp.float32
BF16 = jnp.bfloat16
GROUP = 16
SHARE = 4
VMEM = pl.BlockSpec(memory_space=pltpu.VMEM)
SMEM = pl.BlockSpec(memory_space=pltpu.SMEM)
LIMIT = pltpu.CompilerParams(vmem_limit_bytes=32 * 1024 * 1024)


def place():
    tile = lax.axis_index("tile")
    return lax.rem(tile, 2), lax.div(tile, 8)


def project_kernel(
    emb_hbm, left_hbm, right_hbm, left_ref, right_ref, full_ref, emb_ref, left_w_ref, right_w_ref, sems
):
    copies = [
        pltpu.make_async_copy(source, target, sems.at[k])
        for k, (source, target) in enumerate(
            ((left_hbm, left_w_ref), (right_hbm, right_w_ref), (emb_hbm, emb_ref))
        )
    ]
    for copy in copies:
        copy.start()
    for copy in copies:
        copy.wait()
    core, z_lo = place()
    width = left_w_ref.shape[1]
    half = width // 2
    step = width // SHARE
    blocks = emb_ref.shape[0] // width
    weights = jnp.concatenate([left_w_ref[...], right_w_ref[...]], axis=1)
    for block in range(0, blocks, 2):
        both = jnp.dot(
            emb_ref[block * width : (block + 2) * width, :],
            weights,
            preferred_element_type=F32,
        ).astype(BF16).astype(F32)
        for k in range(2):
            left = both[k * width : (k + 1) * width, :width]
            at = (block + k) * half
            left_ref[at : at + half, :width] = left[:half]
            left_ref[at : at + half, width:] = left[half:]
        full_ref[block * width : (block + 2) * width, :] = both[:, width:]
    quarter = (core * 2 + z_lo) * step
    for block in range(blocks):
        at = pl.multiple_of(block * width + quarter, step)
        right_ref[block * step : (block + 1) * step, :] = full_ref[pl.ds(at, step), :]


def split_kernel(list_mine, list_other, mine_ref, other_ref, keep_ref, send_ref, list_ref, flip_ref):
    core, z_lo = place()
    for ref, owner in ((list_mine, core), (list_other, 1 - core)):
        for slot in range(ref.shape[0]):
            for k in range(3):
                list_ref[owner * ref.shape[0] + slot, k] = ref[slot, k]
    slots, width, _ = mine_ref.shape
    step = width // SHARE
    keep_at = pl.multiple_of((core * 2 + z_lo) * step, step)
    send_at = pl.multiple_of((core * 2 + 1 - z_lo) * step, step)
    for ref, owner in ((mine_ref, core), (other_ref, 1 - core)):
        for slot in range(slots):
            flip_ref[slot] = (ref[slot].astype(F32) * (1.0 / width)).T
            keep_ref[owner * slots + slot] = flip_ref[slot, pl.ds(keep_at, step), :].astype(BF16)
            send_ref[owner * slots + slot] = flip_ref[slot, pl.ds(send_at, step), :].astype(BF16)


def join_kernel(keep_ref, back_ref, other_ref, pred_ref, flip_ref):
    core, z_lo = place()
    slots, width, _ = pred_ref.shape
    step = width // SHARE
    spots = [
        pl.multiple_of((side * 2 + deep) * step, step)
        for side in (core, 1 - core)
        for deep in (z_lo, 1 - z_lo)
    ]
    for slot in range(slots):
        flip_ref[slot, pl.ds(spots[0], step), :] = keep_ref[core * slots + slot].astype(F32)
        flip_ref[slot, pl.ds(spots[1], step), :] = back_ref[core * slots + slot].astype(F32)
        flip_ref[slot, pl.ds(spots[2], step), :] = other_ref[slot, :step].astype(F32)
        flip_ref[slot, pl.ds(spots[3], step), :] = other_ref[slot, step:].astype(F32)
        pred_ref[slot] = flip_ref[slot].T.astype(BF16)


def pair_kernel(
    list_a, list_b,
    left_ref, right_ref, emb_ref, next_ref, right_w_ref, bias_ref, target_a, target_b,
    w_ref, b_ref, out_ref,
    pred_a, pred_b, sum_ref, col_ref, edge_ref,
    table, right_all, target_all, pred_all, row_all, col_all, outer_all, bias_all,
    w_two, out_two, back_two, b_two, first_0, first_1, slope_0, slope_1,
):
    core, z_lo = place()
    chip_slots, step, width = target_a.shape
    pairs = width // 2
    blocks = left_ref.shape[0] // pairs
    chunks = pairs // GROUP

    count = jnp.int32(0)
    for source, ref in enumerate((list_a, list_b)):
        for slot in range(chip_slots):
            offset = ref[slot, 2]
            table[3 * count] = lax.rem(ref[slot, 0], blocks)
            table[3 * count + 1] = offset
            table[3 * count + 2] = source * chip_slots + slot
            count = count + jnp.where(offset >= 0, 1, 0)

    w = w_ref[...].astype(F32)
    w_out = out_ref[...]
    back = (w * w_out).T.astype(BF16)
    spread = jnp.broadcast_to(w_out * (1.0 / width), (width, width)).T.astype(BF16)
    for ref, block in ((w_two, w_ref[...]), (out_two, spread), (back_two, back)):
        ref[...] = jnp.zeros_like(ref)
        ref[:width, :width] = block
        ref[width:, width:] = block
    b_two[:, :width] = b_ref[...]
    b_two[:, width:] = b_ref[...]
    own = right_ref.shape[0]
    right_all[:own, :] = right_ref[...]
    right_next = jnp.dot(next_ref[...], right_w_ref[...], preferred_element_type=F32)
    right_all[own:, :] = right_next.astype(BF16).astype(F32)
    target_all[:chip_slots] = target_a[...].astype(F32)
    target_all[chip_slots:] = target_b[...].astype(F32)
    for ref in (pred_all, row_all, col_all, outer_all, bias_all, first_1, slope_1):
        ref[...] = jnp.zeros_like(ref)
    lane = lax.broadcasted_iota(jnp.int32, (step, width), 1)
    spot = lax.rem(lane, pairs)
    ones = jnp.ones((8, GROUP * step), BF16)

    def forward(turn, first_ref, slope_ref):
        job = lax.div(turn, chunks)
        chunk = lax.rem(turn, chunks)
        block, offset, slot = table[3 * job], table[3 * job + 1], table[3 * job + 2]
        at = block * pairs + chunk * GROUP
        shift = chunk * GROUP
        right = right_all[pl.ds(pl.multiple_of((block + offset) * step, step), step), :]
        right = right + bias_ref[pl.ds(offset, 1), :]
        right = jnp.concatenate([right, right], axis=1)
        target = pltpu.roll(target_all[slot], lax.rem(width - shift, width), 1)
        pre = jnp.concatenate(
            [left_ref[pl.ds(at + p, 1), :] + right for p in range(GROUP)], axis=0
        )
        first = jnp.maximum(pre, 0.0).astype(BF16)
        first_ref[...] = first
        act = jnp.dot(first, w_two[...], preferred_element_type=F32) + b_two[...]
        second = jnp.maximum(act, 0.0).astype(BF16)
        contact = jnp.dot(second, out_two[...], preferred_element_type=F32)
        found = jnp.zeros((step, width), F32)
        wanted = []
        for p in range(GROUP):
            pair = []
            for s in range(2):
                k = p + s * pairs
                here = contact[p * step : (p + 1) * step, s * width : (s + 1) * width]
                found = jnp.where(lane == k, here, found)
                pair.append(jnp.broadcast_to(target[:, k : k + 1], (step, width)))
            wanted.append(jnp.concatenate(pair, axis=1))
        slope = (contact - jnp.concatenate(wanted, axis=0)).astype(BF16)
        slope_ref[...] = jnp.where(second > 0, slope, jnp.zeros_like(slope))
        mine = (spot >= shift) & (spot < shift + GROUP)
        pred_all[slot] = jnp.where(mine, pltpu.roll(found, shift, 1), pred_all[slot])

    def backward(turn, first_ref, slope_ref):
        job = lax.div(turn, chunks)
        chunk = lax.rem(turn, chunks)
        block, offset = table[3 * job], table[3 * job + 1]
        at = pl.multiple_of(block * pairs + chunk * GROUP, GROUP)
        first = first_ref[...]
        slope = slope_ref[...]
        back = jnp.dot(slope, back_two[...], preferred_element_type=F32)
        back = jnp.where(first.astype(F32) > 0.0, back, 0.0)
        rows = []
        cols = jnp.zeros((step, 2 * width), F32)
        for p in range(GROUP):
            here = back[p * step : (p + 1) * step]
            rows.append(jnp.sum(here, axis=0, keepdims=True))
            cols = cols + here
        row_all[pl.ds(at, GROUP), :] += jnp.concatenate(rows, axis=0)
        cols = cols[:, :width] + cols[:, width:]
        col_at = pl.multiple_of((block + offset) * step, step)
        col_all[pl.ds(col_at, step), :] += cols
        bias_all[pl.ds(offset, 1), :] += jnp.sum(cols, axis=0, keepdims=True)
        outer = jnp.zeros((width + 8, width), F32)
        for s in range(2):
            lhs = jnp.concatenate([first[:, s * width : (s + 1) * width].T, ones], axis=0)
            outer = outer + jnp.dot(
                lhs, slope[:, s * width : (s + 1) * width], preferred_element_type=F32
            )
        outer_all[...] += outer

    def body(pass_at, _):
        turn = 2 * pass_at
        backward(jnp.maximum(turn - 1, 0), first_1, slope_1)
        forward(turn, first_0, slope_0)
        backward(turn, first_0, slope_0)
        forward(turn + 1, first_1, slope_1)
        return 0

    turns = count * chunks
    lax.fori_loop(0, lax.div(turns, 2), body, 0)

    @pl.when(count > 0)
    def _():
        backward(turns - 1, first_1, slope_1)

    pred = (pred_all[...] * float(width)).astype(BF16)
    pred_a[...] = pred[:chip_slots]
    pred_b[...] = pred[chip_slots:]
    outer = outer_all[:width]
    sum_d = outer_all[width : width + 1]
    bias = bias_all[...]
    line = lax.broadcasted_iota(jnp.int32, bias.shape, 0)
    sum_out = jnp.sum(w * outer, axis=0, keepdims=True) + b_ref[...] * sum_d
    vectors = jnp.where(line == 5, sum_d * w_out, bias)
    vectors = jnp.where(line == 6, sum_out, vectors)
    outer = outer * w_out
    high = vectors.astype(BF16).astype(F32)
    rest = (high, vectors - high)
    col = col_all[...].astype(BF16)
    quarter = (core * 2 + z_lo) * step
    rows = []
    embs = []
    for block in range(blocks):
        here = row_all[block * pairs : (block + 1) * pairs, :].astype(BF16)
        rows += [here[:, :width], here[:, width:]]
        embs.append(emb_ref[pl.ds(pl.multiple_of(block * width + quarter, step), step), :])
    embs.append(next_ref[...])
    contract = (((0,), (0,)), ((), ()))
    grads = (
        lax.dot_general(
            jnp.concatenate(rows, axis=0), emb_ref[...], contract, preferred_element_type=F32
        ).astype(BF16),
        lax.dot_general(
            col, jnp.concatenate(embs, axis=0), contract, preferred_element_type=F32
        ).astype(BF16),
    )
    chips = sum_ref.shape[1]
    for side in range(2):
        for chip in range(chips):
            share = side * chips + chip
            sum_ref[side, chip, :pairs, :] = rows[share]
            grad = grads[side][:, chip // 2 * width : (chip // 2 + 1) * width]
            sum_ref[side, chip, pairs:width, :] = grad[chip % 2 * pairs : (chip % 2 + 1) * pairs]
            more = rest[share] if share < 2 else jnp.zeros_like(high)
            sum_ref[side, chip, width:, :] = jnp.concatenate(
                [outer[8 * share : 8 * share + 8], more], axis=0
            ).astype(BF16)
    col_ref[...] = col_all[:own]
    edge_ref[...] = col[own:]


def last_kernel(
    mine_ref, other_ref, left_w_ref, right_w_ref,
    emb_ref, left_ref, right_ref, bias_ref, w_ref, b_ref, out_ref,
    both_ref, flat_ref,
):
    core, _ = place()
    width = left_w_ref.shape[1]
    pairs = width // 2
    step = width // SHARE
    chips = mine_ref.shape[0]
    lows = []
    for side, grad_ref in enumerate((left_ref, right_ref)):
        for chip in range(chips):
            share = side * chips + chip
            block = jnp.where(core == side, mine_ref[chip], other_ref[chip])
            both_ref[share * pairs : (share + 1) * pairs, :width] = block[:pairs]
            z_lo, y = chip // SHARE, chip % SHARE
            for k in range(2):
                to = (2 * y + k) * width + (side * 2 + z_lo) * step
                at = width + 16 + k * step
                both_ref[to : to + step, width:] = block[at : at + step]
            flat_ref[chip * pairs : (chip + 1) * pairs, :] = block[pairs:width].astype(F32)
            small = block[width : width + 16].astype(F32)
            w_ref[8 * share : 8 * share + 8, :] = small[:8]
            lows.append(small[8:])
        for k in range(chips // 2):
            grad_ref[k * width : (k + 1) * width, :] = flat_ref[k * width : (k + 1) * width, :].T
    vectors = lows[0] + lows[1]
    bias_ref[...] = vectors[:5]
    b_ref[...] = vectors[5:6]
    out_ref[...] = vectors[6:7]
    weights = jnp.concatenate([left_w_ref[...], right_w_ref[...]], axis=1)
    part = 2 * width
    for k in range(both_ref.shape[0] // part):
        emb_ref[k * part : (k + 1) * part, :] = lax.dot_general(
            both_ref[k * part : (k + 1) * part, :],
            weights,
            (((1,), (1,)), ((), ())),
            preferred_element_type=F32,
        ).astype(BF16)


def shape(*dims, dtype=F32):
    return jax.ShapeDtypeStruct(dims, dtype)


def call(kernel, outs, scratch, *args, lists=0, space=VMEM, list_out=0):
    return pl.pallas_call(
        kernel,
        out_shape=outs,
        in_specs=[SMEM] * lists + [space] * (len(args) - lists),
        out_specs=(VMEM,) * (len(outs) - list_out) + (SMEM,) * list_out,
        scratch_shapes=scratch,
        compiler_params=LIMIT,
    )(*args)


def shifted(block, axis, distance):
    devices = range(lax.axis_size(axis))
    route = [(i - distance, i) for i in devices if i - distance in devices]
    return lax.ppermute(block, axis, route)


def swapped(block, axis, bits):
    return lax.ppermute(block, axis, [(i, i ^ bits) for i in range(lax.axis_size(axis))])


def chosen(block, index, size):
    return lax.dynamic_slice_in_dim(block, index * size, size, 0)


def across(block, axis, groups=None):
    return lax.all_to_all(block, axis, 0, 0, axis_index_groups=groups, tiled=True)


def summed(blocks):
    return jnp.sum(blocks.astype(F32), axis=0).astype(BF16)


def per_device(embeddings, w_left, w_right, pair_bias, w_pair, b_pair, w_out, tile_list, target):
    core, z_lo = place()
    slots, width = target.shape[2:4]
    rows, features = embeddings.shape
    blocks = rows // width
    pairs = width // 2
    part = rows // SHARE
    step = width // SHARE
    edge = part // 2
    chip = 2 * slots
    chips = lax.axis_size("tile") // 2
    target = target[0, 0]
    lists = tile_list[0, 0]

    target_other = swapped(target, "tile", 1)
    list_other = swapped(lists, "tile", 1)
    emb_edge = lax.dynamic_slice_in_dim(
        embeddings.reshape(blocks, SHARE, step, features)[: blocks // 2], core * 2 + z_lo, 1, 1
    ).reshape(edge, features)
    emb_next = shifted(emb_edge, "bin", -1)
    left, right = call(
        project_kernel,
        (shape(rows // 2, 2 * width), shape(part, width)),
        [
            pltpu.VMEM((rows, width), F32),
            pltpu.VMEM((rows, features), BF16),
            pltpu.VMEM((features, width), BF16),
            pltpu.VMEM((features, width), BF16),
            pltpu.SemaphoreType.DMA((3,)),
        ],
        embeddings, w_left, w_right, space=pl.BlockSpec(memory_space=pl.ANY),
    )
    quarter = shape(chip, step, width, dtype=BF16)
    target_keep, target_send, list_chip = call(
        split_kernel, (quarter, quarter, shape(chip, 3, dtype=jnp.int32)),
        [pltpu.VMEM((slots, width, width), F32)],
        lists, list_other, target, target_other, lists=2, list_out=1,
    )
    target_deep = swapped(target_send, "tile", 8)
    list_deep = swapped(list_chip, "tile", 8)

    chunk = (GROUP * step, 2 * width)
    pred_keep, pred_send, sums, col, col_edge = call(
        pair_kernel,
        (
            quarter,
            quarter,
            shape(2, chips, width + 16, width, dtype=BF16),
            shape(part, width),
            shape(edge, width, dtype=BF16),
        ),
        [
            pltpu.SMEM((3 * 2 * chip + 8,), jnp.int32),
            pltpu.VMEM((part + edge, width), F32),
            pltpu.VMEM((2 * chip, step, width), F32),
            pltpu.VMEM((2 * chip, step, width), F32),
            pltpu.VMEM((rows // 2, 2 * width), F32),
            pltpu.VMEM((part + edge, width), F32),
            pltpu.VMEM((width + 8, width), F32),
            pltpu.VMEM((8, width), F32),
            pltpu.VMEM((2 * width, 2 * width), BF16),
            pltpu.VMEM((2 * width, 2 * width), BF16),
            pltpu.VMEM((2 * width, 2 * width), BF16),
            pltpu.VMEM((1, 2 * width), F32),
            pltpu.VMEM(chunk, BF16),
            pltpu.VMEM(chunk, BF16),
            pltpu.VMEM(chunk, BF16),
            pltpu.VMEM(chunk, BF16),
        ],
        list_chip, list_deep, left, right, embeddings, emb_next, w_right, pair_bias,
        target_keep, target_deep, w_pair, b_pair[None], w_out[None], lists=2,
    )
    sums_other = swapped(lax.dynamic_index_in_dim(sums, 1 - core, 0, keepdims=False), "tile", 1)
    col_before = shifted(col_edge, "bin", 1)
    sums = lax.dynamic_index_in_dim(sums, core, 0, keepdims=False)
    sums = (sums.astype(F32) + sums_other.astype(F32)).astype(BF16)
    col = jnp.concatenate([col[:edge] + col_before.astype(F32), col[edge:]], axis=0).astype(BF16)
    col = col.reshape(1, chips // 2, 2 * step, width)
    here = (jnp.arange(2) == z_lo).reshape(2, 1, 1, 1)
    col = jnp.where(here, col, jnp.zeros_like(col)).reshape(chips, 2 * step, width)
    groups = [list(range(k, 2 * chips, 2)) for k in range(2)]
    share = summed(across(jnp.concatenate([sums, col], axis=1), "tile", groups))
    weight = share[pairs : width + 16]
    weight = jnp.broadcast_to(weight[None], (lax.axis_size("bin"), *weight.shape))
    weight = summed(across(weight, "bin"))
    share = jnp.concatenate([share[:pairs], weight, share[width + 16 :]], axis=0)
    mine = across(jnp.broadcast_to(share[None], (chips, *share.shape)), "tile", groups)
    other = swapped(mine, "tile", 1)

    pred_back = swapped(pred_send, "tile", 8)
    pred_other = swapped(
        jnp.concatenate(
            [chosen(pred_keep, 1 - core, slots), chosen(pred_back, 1 - core, slots)], axis=1
        ),
        "tile",
        1,
    )
    (predicted,) = call(
        join_kernel, (shape(slots, width, width, dtype=BF16),),
        [pltpu.VMEM((slots, width, width), F32)],
        pred_keep, pred_back, pred_other,
    )
    grads = call(
        last_kernel,
        (
            shape(rows, features, dtype=BF16),
            shape(features, width),
            shape(features, width),
            shape(5, width),
            shape(width, width),
            shape(1, width),
            shape(1, width),
        ),
        [pltpu.VMEM((rows, 2 * width), BF16), pltpu.VMEM((features, width), F32)],
        mine, other, w_left, w_right,
    )
    return (predicted[None, None], *grads[:5], grads[5][0], grads[6][0])


def solution(mesh):
    return jax.shard_map(
        per_device,
        mesh=mesh,
        in_specs=(
            P("bin", None),
            P(),
            P(),
            P(),
            P(),
            P(),
            P(),
            P("bin", "tile", None, None),
            P("bin", "tile", None, None, None),
        ),
        out_specs=(
            P("bin", "tile", None, None, None),
            P("bin", None),
            P(),
            P(),
            P(),
            P(),
            P(),
            P(),
        ),
        check_vma=False,
    )
```

```python
import jax
import jax.numpy as jnp
from jax import lax
from jax.experimental import pallas as pl
from jax.experimental.pallas import tpu as pltpu
from jax.sharding import PartitionSpec as P

F32 = jnp.float32
BF16 = jnp.bfloat16
BATCH = 2
NEVER = -1e38
VMEM = pl.BlockSpec(memory_space=pltpu.VMEM)
SMEM = pl.BlockSpec(memory_space=pltpu.SMEM)
HBM = pl.BlockSpec(memory_space=pl.ANY)
LIMIT = pltpu.CompilerParams(vmem_limit_bytes=32 * 1024 * 1024)


def place():
    return lax.axis_index("tile")


def project_kernel(
    emb_hbm, left_hbm, right_hbm, left_ref, right_ref, full_ref, emb_ref, left_w_ref, right_w_ref, sems
):
    copies = [
        pltpu.make_async_copy(source, target, sems.at[k])
        for k, (source, target) in enumerate(
            ((left_hbm, left_w_ref), (right_hbm, right_w_ref), (emb_hbm, emb_ref))
        )
    ]
    for copy in copies:
        copy.start()
    for copy in copies:
        copy.wait()
    tile = place()
    width = left_w_ref.shape[1]
    half = width // 2
    blocks = emb_ref.shape[0] // width
    step = right_ref.shape[0] // blocks
    weights = jnp.concatenate([left_w_ref[...], right_w_ref[...]], axis=1)
    for block in range(0, blocks, 2):
        both = jnp.dot(
            emb_ref[block * width : (block + 2) * width, :],
            weights,
            preferred_element_type=F32,
        ).astype(BF16).astype(F32)
        for k in range(2):
            left = both[k * width : (k + 1) * width, :width]
            at = (block + k) * half
            left_ref[at : at + half, :width] = left[:half]
            left_ref[at : at + half, width:] = left[half:]
        full_ref[block * width : (block + 2) * width, :] = both[:, width:]
    for block in range(blocks):
        at = pl.multiple_of(block * width + tile * step, step)
        right_ref[block * step : (block + 1) * step, :] = full_ref[pl.ds(at, step), :]


def split_kernel(list_ref, target_hbm, send_ref, target_ref, flip_ref, sem):
    copy = pltpu.make_async_copy(target_hbm, target_ref, sem)
    copy.start()
    slots, width, _ = target_ref.shape
    shares = send_ref.shape[0]
    step = width // shares
    line = lax.broadcasted_iota(jnp.int32, (step, width), 0)
    lane = lax.broadcasted_iota(jnp.int32, (step, width), 1)
    listed = jnp.zeros((step, width), jnp.int32)
    for slot in range(slots):
        for k in range(3):
            listed = jnp.where((line == 0) & (lane == 3 * slot + k), list_ref[k, 0, slot], listed)
    listed = listed.astype(F32)
    copy.wait()
    for slot in range(slots):
        flip_ref[slot] = (target_ref[slot].astype(F32) * (1.0 / width)).T
    spare = send_ref.shape[1] - (slots + 1) * step
    for share in range(shares):
        pieces = [flip_ref[slot, share * step : (share + 1) * step, :] for slot in range(slots)]
        pieces += [listed, jnp.zeros((spare, width), F32)]
        send_ref[share] = jnp.concatenate(pieces, axis=0).astype(BF16)


def join_kernel(back_ref, pred_ref, flip_ref):
    slots, width, _ = pred_ref.shape
    shares = back_ref.shape[0]
    step = width // shares
    at = back_ref.shape[1] - slots * step
    for share in range(shares):
        block = back_ref[share, at:, :].astype(F32)
        for slot in range(slots):
            flip_ref[slot, share * step : (share + 1) * step, :] = block[
                slot * step : (slot + 1) * step
            ]
    for slot in range(slots):
        pred_ref[slot] = flip_ref[slot].T.astype(BF16)


def pair_kernel(
    left_ref, right_ref, emb_ref, cols_ref, next_ref, right_w_ref, bias_ref, target_ref,
    w_ref, b_ref, out_ref,
    sum_ref, col_ref, edge_ref,
    table, lists, list_sem, list_all, right_all, target_all, pred_all, row_all, col_all,
    outer_all, bias_all, w_two, out_two, back_two, b_two, first_0, first_1, slope_0, slope_1,
):
    width = w_ref.shape[0]
    pairs = width // 2
    blocks = left_ref.shape[0] // pairs
    shares = target_ref.shape[0]
    step = width // shares
    slots = target_ref.shape[1] // step - 2
    groups = target_all.shape[0] - 1
    spread_bits = (width // step).bit_length() - 1

    for share in range(shares):
        rows = target_ref[share].astype(F32)
        list_all[share : share + 1] = rows[slots * step : slots * step + 1].astype(jnp.int32)
    copy = pltpu.make_async_copy(list_all, lists, list_sem)
    copy.start()

    w = w_ref[...].astype(F32)
    w_out = out_ref[...]
    back = (w * w_out).T.astype(BF16)
    spread = jnp.broadcast_to(w_out * (1.0 / width), (width, width)).T.astype(BF16)
    for ref, block in ((w_two, w_ref[...]), (out_two, spread), (back_two, back)):
        ref[...] = jnp.zeros_like(ref)
        ref[:width, :width] = block
        ref[width:, width:] = block
    b_two[:, :width] = b_ref[...]
    b_two[:, width:] = b_ref[...]
    own = right_ref.shape[0]
    right_all[:own, :] = right_ref[...]
    right_next = jnp.dot(next_ref[...], right_w_ref[...], preferred_element_type=F32)
    right_all[own:, :] = right_next.astype(BF16).astype(F32)
    rows = [target_ref[share].astype(F32)[: slots * step] for share in range(shares)]
    rows = jnp.concatenate(rows, axis=0)
    for group in range(groups):
        target_all[group] = rows[group * width : (group + 1) * width].T
    target_all[groups] = jnp.zeros((width, width), F32)
    for ref in (pred_all, row_all, col_all, outer_all, bias_all, first_1, slope_1):
        ref[...] = jnp.zeros_like(ref)
    lane = lax.broadcasted_iota(jnp.int32, (width, width), 1)
    ones = jnp.ones((16, BATCH * step * pairs), BF16)

    copy.wait()
    count = jnp.int32(0)
    for share in range(shares):
        for slot in range(slots):
            offset = lists[share, 3 * slot + 2]
            table[0, count] = lists[share, 3 * slot] & (blocks - 1)
            table[1, count] = offset
            table[2, count] = share * slots + slot
            count = count + jnp.where(offset >= 0, 1, 0)
    for spare in range(2 * BATCH):
        table[0, count + spare] = 0
        table[1, count + spare] = 0
        table[2, count + spare] = shares * slots

    def forward(turn, first_ref, slope_ref):
        pre = []
        wanted = []
        shifts = []
        floors = []
        for k in range(BATCH):
            job = turn * BATCH + k
            block, offset, slot = table[0, job], table[1, job], table[2, job]
            shift = (slot & (width // step - 1)) * step
            shifts.append((slot >> spread_bits, shift))
            at = pl.multiple_of(block * pairs, pairs)
            col_at = pl.multiple_of((block + offset) * step, step)
            right = right_all[pl.ds(col_at, step), :] + bias_ref[pl.ds(offset, 1), :]
            right = jnp.concatenate([right, right], axis=1)
            left = left_ref[pl.ds(at, pairs), :]
            pre += [left + right[j : j + 1, :] for j in range(step)]
            target = pltpu.roll(
                target_all[slot >> spread_bits], (width - shift) & (width - 1), 1
            )
            for j in range(step):
                want = jnp.broadcast_to(target[:, j : j + 1], (width, width))
                wanted.append(jnp.concatenate([want[:pairs], want[pairs:]], axis=1))
            floor = jnp.where(job < count, b_two[...], jnp.full((1, 2 * width), NEVER, F32))
            floors.append(jnp.broadcast_to(floor, (step * pairs, 2 * width)))
        first = jnp.maximum(jnp.concatenate(pre, axis=0), 0.0).astype(BF16)
        first_ref[...] = first
        act = jnp.dot(first, w_two[...], preferred_element_type=F32)
        act = act + jnp.concatenate(floors, axis=0)
        second = jnp.maximum(act, 0.0).astype(BF16)
        contact = jnp.dot(second, out_two[...], preferred_element_type=F32)
        slope = (contact - jnp.concatenate(wanted, axis=0)).astype(BF16)
        slope_ref[...] = jnp.where(second > 0, slope, jnp.zeros_like(slope))
        for k, (group, shift) in enumerate(shifts):
            found = jnp.zeros((width, width), F32)
            for j in range(step):
                here = contact[(k * step + j) * pairs : (k * step + j + 1) * pairs]
                here = jnp.concatenate([here[:, :width], here[:, width:]], axis=0)
                found = jnp.where(lane == j, here, found)
            mine = (lane >= shift) & (lane < shift + step)
            pred_all[group] = jnp.where(mine, pltpu.roll(found, shift, 1), pred_all[group])

    def backward(turn, first_ref, slope_ref):
        first = first_ref[...]
        slope = slope_ref[...]
        back = jnp.dot(slope, back_two[...], preferred_element_type=F32)
        back = jnp.where(first.astype(F32) > 0.0, back, 0.0)
        for k in range(BATCH):
            job = turn * BATCH + k
            block, offset = table[0, job], table[1, job]
            at = pl.multiple_of(block * pairs, pairs)
            rows = jnp.zeros((pairs, 2 * width), F32)
            cols = []
            for j in range(step):
                here = back[(k * step + j) * pairs : (k * step + j + 1) * pairs]
                rows = rows + here
                col = jnp.sum(here, axis=0, keepdims=True)
                cols.append(col[:, :width] + col[:, width:])
            row_all[pl.ds(at, pairs), :] += rows
            cols = jnp.concatenate(cols, axis=0)
            col_at = pl.multiple_of((block + offset) * step, step)
            col_all[pl.ds(col_at, step), :] += cols
            bias_all[pl.ds(offset, 1), :] += jnp.sum(cols, axis=0, keepdims=True)
        lhs = jnp.concatenate([first.T, ones], axis=0)
        outer_all[...] += jnp.dot(lhs, slope, preferred_element_type=F32)

    def body(pass_at, _):
        turn = 2 * pass_at
        backward(jnp.maximum(turn - 1, 0), first_1, slope_1)
        forward(turn, first_0, slope_0)
        backward(turn, first_0, slope_0)
        forward(turn + 1, first_1, slope_1)
        return 0

    passes = lax.div(count + 2 * BATCH - 1, 2 * BATCH)
    lax.fori_loop(0, passes, body, 0)
    backward(jnp.maximum(2 * passes - 1, 0), first_1, slope_1)

    flat = [(pred_all[group] * float(width)).T for group in range(groups)]
    flat = jnp.concatenate(flat, axis=0).astype(BF16)
    for share in range(shares):
        sum_ref[share, width + 16 :, :] = flat[share * slots * step : (share + 1) * slots * step]
    outer = outer_all[:width, :width] + outer_all[width : 2 * width, width:]
    sum_d = outer_all[2 * width : 2 * width + 1, :width] + outer_all[2 * width : 2 * width + 1, width:]
    bias = bias_all[...]
    line = lax.broadcasted_iota(jnp.int32, bias.shape, 0)
    sum_out = jnp.sum(w * outer, axis=0, keepdims=True) + b_ref[...] * sum_d
    vectors = jnp.where(line == 5, sum_d * w_out, bias)
    vectors = jnp.where(line == 6, sum_out, vectors)
    outer = outer * w_out
    high = vectors.astype(BF16).astype(F32)
    rest = (high, vectors - high)
    col = col_all[...].astype(BF16)
    rows = []
    for block in range(blocks):
        here = row_all[block * pairs : (block + 1) * pairs, :].astype(BF16)
        rows += [here[:, :width], here[:, width:]]
    embs = [cols_ref[...], next_ref[...]]
    contract = (((0,), (0,)), ((), ()))
    grads = (
        lax.dot_general(
            jnp.concatenate(rows, axis=0), emb_ref[...], contract, preferred_element_type=F32
        ).astype(BF16),
        lax.dot_general(
            col, jnp.concatenate(embs, axis=0), contract, preferred_element_type=F32
        ).astype(BF16),
    )
    half = shares // 2
    for share in range(shares):
        side, at = share // half, share % half
        sum_ref[share, :pairs, :] = rows[share]
        grad = grads[side][:, at // 2 * width : (at // 2 + 1) * width]
        sum_ref[share, pairs:width, :] = grad[at % 2 * pairs : (at % 2 + 1) * pairs]
        more = rest[share] if share < 2 else jnp.zeros_like(high)
        sum_ref[share, width : width + 16, :] = jnp.concatenate(
            [outer[8 * share : 8 * share + 8], more], axis=0
        ).astype(BF16)
    col_ref[...] = col_all[:own]
    edge_ref[...] = col[own:]


def last_kernel(
    mine_ref, other_ref, left_w_ref, right_w_ref,
    emb_ref, left_ref, right_ref, bias_ref, w_ref, b_ref, out_ref,
    both_ref, flat_ref, col_ref,
):
    core = lax.rem(place(), 2)
    width = left_w_ref.shape[1]
    pairs = width // 2
    chips = mine_ref.shape[0]
    step = width // (2 * chips)
    lows = []
    for share in range(2 * chips):
        block = jnp.where(core == share % 2, mine_ref[share // 2], other_ref[share // 2])
        both_ref[share * pairs : (share + 1) * pairs, :width] = block[:pairs]
        block = block.astype(F32)
        for k in range(col_ref.shape[0] // width):
            to = k * width + share * step
            at = width + 16 + k * step
            col_ref[to : to + step, :] = block[at : at + step]
        flat_ref[share * pairs : (share + 1) * pairs, :] = block[pairs:width]
        small = block[width : width + 16]
        w_ref[8 * share : 8 * share + 8, :] = small[:8]
        lows.append(small[8:])
    for side, grad_ref in enumerate((left_ref, right_ref)):
        for k in range(chips // 2):
            at = (side * chips // 2 + k) * width
            grad_ref[k * width : (k + 1) * width, :] = flat_ref[at : at + width, :].T
    both_ref[:, width:] = col_ref[...].astype(BF16)
    vectors = lows[0] + lows[1]
    bias_ref[...] = vectors[:5]
    b_ref[...] = vectors[5:6]
    out_ref[...] = vectors[6:7]
    weights = jnp.concatenate([left_w_ref[...], right_w_ref[...]], axis=1)
    part = 2 * width
    for k in range(both_ref.shape[0] // part):
        emb_ref[k * part : (k + 1) * part, :] = lax.dot_general(
            both_ref[k * part : (k + 1) * part, :],
            weights,
            (((1,), (1,)), ((), ())),
            preferred_element_type=F32,
        ).astype(BF16)


def shape(*dims, dtype=F32):
    return jax.ShapeDtypeStruct(dims, dtype)


def call(kernel, outs, scratch, *args, lists=0, space=VMEM):
    return pl.pallas_call(
        kernel,
        out_shape=outs,
        in_specs=[SMEM] * lists + [space] * (len(args) - lists),
        out_specs=(VMEM,) * len(outs),
        scratch_shapes=scratch,
        compiler_params=LIMIT,
    )(*args)


def shifted(block, axis, distance):
    devices = range(lax.axis_size(axis))
    route = [(i - distance, i) for i in devices if i - distance in devices]
    return lax.ppermute(block, axis, route)


def swapped(block, axis, bits):
    return lax.ppermute(block, axis, [(i, i ^ bits) for i in range(lax.axis_size(axis))])


def across(block, axis, groups=None):
    return lax.all_to_all(block, axis, 0, 0, axis_index_groups=groups, tiled=True)


def per_device(embeddings, w_left, w_right, pair_bias, w_pair, b_pair, w_out, tile_list, target):
    tile = place()
    core = lax.rem(tile, 2)
    slots, width = target.shape[2:4]
    rows, features = embeddings.shape
    blocks = rows // width
    pairs = width // 2
    shares = lax.axis_size("tile")
    chips = shares // 2
    step = width // shares
    part = rows // shares
    edge = part // 2
    target = target[0, 0]
    lists = jnp.transpose(tile_list, (0, 3, 1, 2)).reshape(3, 1, slots)

    emb_cols = lax.dynamic_slice_in_dim(
        embeddings.reshape(blocks, shares, step, features), tile, 1, 1
    ).reshape(part, features)
    emb_next = shifted(emb_cols[:edge], "bin", -1)
    (target_send,) = call(
        split_kernel, (shape(shares, (slots + 2) * step, width, dtype=BF16),),
        [
            pltpu.VMEM((slots, width, width), BF16),
            pltpu.VMEM((slots, width, width), F32),
            pltpu.SemaphoreType.DMA,
        ],
        lists, target, lists=1, space=HBM,
    )
    left, right = call(
        project_kernel,
        (shape(rows // 2, 2 * width), shape(part, width)),
        [
            pltpu.VMEM((rows, width), F32),
            pltpu.VMEM((rows, features), BF16),
            pltpu.VMEM((features, width), BF16),
            pltpu.VMEM((features, width), BF16),
            pltpu.SemaphoreType.DMA((3,)),
        ],
        embeddings, w_left, w_right, space=HBM,
    )
    target_send, emb_next = lax.optimization_barrier((target_send, emb_next))
    target_all = across(target_send, "tile")

    chunk = (BATCH * step * pairs, 2 * width)
    grouped = (slots * shares * step // width + 1, width, width)
    sums, col, col_edge = call(
        pair_kernel,
        (
            shape(shares, width + 16 + slots * step, width, dtype=BF16),
            shape(part, width),
            shape(edge, width, dtype=BF16),
        ),
        [
            pltpu.SMEM((3, slots * shares + 2 * BATCH), jnp.int32),
            pltpu.SMEM((shares, width), jnp.int32),
            pltpu.SemaphoreType.DMA,
            pltpu.VMEM((shares, width), jnp.int32),
            pltpu.VMEM((part + edge, width), F32),
            pltpu.VMEM(grouped, F32),
            pltpu.VMEM(grouped, F32),
            pltpu.VMEM((rows // 2, 2 * width), F32),
            pltpu.VMEM((part + edge, width), F32),
            pltpu.VMEM((2 * width + 16, 2 * width), F32),
            pltpu.VMEM((8, width), F32),
            pltpu.VMEM((2 * width, 2 * width), BF16),
            pltpu.VMEM((2 * width, 2 * width), BF16),
            pltpu.VMEM((2 * width, 2 * width), BF16),
            pltpu.VMEM((1, 2 * width), F32),
            pltpu.VMEM(chunk, BF16),
            pltpu.VMEM(chunk, BF16),
            pltpu.VMEM(chunk, BF16),
            pltpu.VMEM(chunk, BF16),
        ],
        left, right, embeddings, emb_cols, emb_next, w_right, pair_bias,
        target_all, w_pair, b_pair[None], w_out[None],
    )
    sums = across(sums, "tile")
    share = jnp.sum(sums[:, : width + 16].astype(F32), axis=0).astype(BF16)
    weight = share[pairs:]
    bins = lax.axis_size("bin")
    here = lax.axis_index("bin")
    before = jnp.zeros((edge, width), F32)
    mask = 1
    while mask < bins:
        met = swapped(jnp.concatenate([weight, col_edge], axis=0), "bin", mask).astype(F32)
        weight = (weight.astype(F32) + met[: weight.shape[0]]).astype(BF16)
        before = jnp.where((here ^ mask) + 1 == here, met[weight.shape[0] :], before)
        mask = 2 * mask + 1
    col = jnp.concatenate([col[:edge] + before, col[edge:]], axis=0).astype(BF16)
    share = jnp.concatenate([share[:pairs], weight, col], axis=0)
    groups = [list(range(k, shares, 2)) for k in range(2)]
    mine = across(jnp.broadcast_to(share[None], (chips, *share.shape)), "tile", groups)
    other = swapped(mine, "tile", 1)
    (predicted,) = call(
        join_kernel, (shape(slots, width, width, dtype=BF16),),
        [pltpu.VMEM((slots, width, width), F32)],
        sums,
    )
    grads = call(
        last_kernel,
        (
            shape(rows, features, dtype=BF16),
            shape(features, width),
            shape(features, width),
            shape(5, width),
            shape(width, width),
            shape(1, width),
            shape(1, width),
        ),
        [
            pltpu.VMEM((rows, 2 * width), BF16),
            pltpu.VMEM((2 * features, width), F32),
            pltpu.VMEM((rows, width), F32),
        ],
        mine, other, w_left, w_right,
    )
    return (predicted[None, None], *grads[:5], grads[5][0], grads[6][0])


def solution(mesh):
    return jax.shard_map(
        per_device,
        mesh=mesh,
        in_specs=(
            P("bin", None),
            P(),
            P(),
            P(),
            P(),
            P(),
            P(),
            P("bin", "tile", None, None),
            P("bin", "tile", None, None, None),
        ),
        out_specs=(
            P("bin", "tile", None, None, None),
            P("bin", None),
            P(),
            P(),
            P(),
            P(),
            P(),
            P(),
        ),
        check_vma=False,
    )
```

```python
import jax
import jax.numpy as jnp
from jax import lax
from jax.experimental import pallas as pl
from jax.experimental.pallas import tpu as pltpu
from jax.sharding import PartitionSpec as P

F32 = jnp.float32
BF16 = jnp.bfloat16
BATCH = 2
NEVER = -1e38
BIN_MASKS = (2, 6, 4)
VMEM = pl.BlockSpec(memory_space=pltpu.VMEM)
HBM = pl.BlockSpec(memory_space=pl.ANY)


def place():
    return lax.axis_index("tile")


def prepare_kernel(
    list_hbm, target_hbm, emb_hbm, left_hbm, right_hbm,
    send_ref, left_ref, right_ref, cols_ref, edge_ref,
    list_ref, target_ref, emb_ref, left_w_ref, right_w_ref, flip_ref, listed_ref, full_ref, sems,
):
    copies = [
        pltpu.make_async_copy(source, target, sems.at[k])
        for k, (source, target) in enumerate(
            (
                (target_hbm, target_ref),
                (list_hbm, list_ref),
                (left_hbm, left_w_ref),
                (right_hbm, right_w_ref),
                (emb_hbm, emb_ref),
            )
        )
    ]
    for copy in copies:
        copy.start()
    slots, width, _ = target_ref.shape
    shares = send_ref.shape[0]
    step = width // shares
    half = width // 2
    blocks = emb_ref.shape[0] // width
    listed_ref[...] = jnp.zeros_like(listed_ref)
    copies[0].wait()
    for slot in range(slots):
        flip_ref[slot] = (target_ref[slot].astype(F32) * (1.0 / width)).T
    copies[1].wait()
    for k in range(3):
        listed_ref[k : k + 1, :slots] = list_ref[k].astype(F32)
    listed = listed_ref[...]
    spare = send_ref.shape[1] - (slots + 1) * step
    for share in range(shares):
        pieces = [flip_ref[slot, share * step : (share + 1) * step, :] for slot in range(slots)]
        pieces += [listed, jnp.zeros((spare, width), F32)]
        send_ref[share] = jnp.concatenate(pieces, axis=0).astype(BF16)
    for copy in copies[2:]:
        copy.wait()
    tile = place()
    weights = jnp.concatenate([left_w_ref[...], right_w_ref[...]], axis=1)
    for block in range(0, blocks, 2):
        both = jnp.dot(
            emb_ref[block * width : (block + 2) * width, :],
            weights,
            preferred_element_type=F32,
        ).astype(BF16).astype(F32)
        for k in range(2):
            left = both[k * width : (k + 1) * width, :width]
            at = (block + k) * half
            left_ref[at : at + half, :width] = left[:half]
            left_ref[at : at + half, width:] = left[half:]
        full_ref[block * width : (block + 2) * width, :] = both[:, width:]
    rows = []
    for block in range(blocks):
        at = pl.multiple_of(block * width + tile * step, step)
        right_ref[block * step : (block + 1) * step, :] = full_ref[pl.ds(at, step), :]
        at = pl.multiple_of(block * width + (tile >> 1) * (2 * step), 2 * step)
        near = emb_ref[pl.ds(at, 2 * step), :].astype(F32)
        rows.append(jnp.where((tile & 1) == 0, near[:step], near[step:]))
    rows = jnp.concatenate(rows, axis=0).astype(BF16)
    cols_ref[...] = rows
    edge_ref[...] = rows[: edge_ref.shape[0]]


def join_kernel(back_ref, pred_ref, flip_ref):
    slots, width, _ = pred_ref.shape
    shares = back_ref.shape[0]
    step = width // shares
    at = back_ref.shape[1] - slots * step
    for share in range(shares):
        block = back_ref[share, at:, :].astype(F32)
        for slot in range(slots):
            flip_ref[slot, share * step : (share + 1) * step, :] = block[
                slot * step : (slot + 1) * step
            ]
    for slot in range(slots):
        pred_ref[slot] = flip_ref[slot].T.astype(BF16)


def pair_kernel(
    left_ref, right_ref, emb_ref, cols_ref, next_ref, right_w_ref, bias_ref, target_ref,
    w_ref, b_ref, out_ref,
    sum_ref, col_ref, edge_ref,
    table, lists, list_sem, list_all, right_all, target_all, pred_all, row_all, col_all,
    outer_all, bias_all, w_two, out_two, back_two, b_two, first_0, first_1, slope_0, slope_1,
):
    width = w_ref.shape[0]
    pairs = width // 2
    blocks = left_ref.shape[0] // pairs
    shares = target_ref.shape[0]
    step = width // shares
    slots = target_ref.shape[1] // step - 2
    groups = target_all.shape[0] - 1
    spread_bits = (width // step).bit_length() - 1

    for share in range(shares):
        rows = target_ref[share].astype(F32)
        for k in range(3):
            at = slots * step + k
            list_all[k, share : share + 1] = rows[at : at + 1].astype(jnp.int32)
    copy = pltpu.make_async_copy(list_all, lists, list_sem)
    copy.start()

    w = w_ref[...].astype(F32)
    w_out = out_ref[...]
    back = (w * w_out).T.astype(BF16)
    spread = jnp.broadcast_to(w_out * (1.0 / width), (width, width)).T.astype(BF16)
    for ref, block in ((w_two, w_ref[...]), (out_two, spread), (back_two, back)):
        ref[...] = jnp.zeros_like(ref)
        ref[:width, :width] = block
        ref[width:, width:] = block
    b_two[:, :width] = b_ref[...]
    b_two[:, width:] = b_ref[...]
    own = right_ref.shape[0]
    right_all[:own, :] = right_ref[...]
    right_next = jnp.dot(next_ref[...], right_w_ref[...], preferred_element_type=F32)
    right_all[own:, :] = right_next.astype(BF16).astype(F32)
    rows = [target_ref[share].astype(F32)[: slots * step] for share in range(shares)]
    rows = jnp.concatenate(rows, axis=0)
    for group in range(groups):
        target_all[group] = rows[group * width : (group + 1) * width].T
    target_all[groups] = jnp.zeros((width, width), F32)
    for ref in (pred_all, row_all, col_all, outer_all, bias_all, first_1, slope_1):
        ref[...] = jnp.zeros_like(ref)
    lane = lax.broadcasted_iota(jnp.int32, (width, width), 1)
    ones = jnp.ones((16, BATCH * step * pairs), BF16)

    copy.wait()
    count = jnp.int32(0)
    for share in range(shares):
        for slot in range(slots):
            offset = lists[2, share, slot]
            table[0, count] = lists[0, share, slot] & (blocks - 1)
            table[1, count] = offset
            table[2, count] = share * slots + slot
            count = count + jnp.where(offset >= 0, 1, 0)
    for spare in range(2 * BATCH):
        table[0, count + spare] = 0
        table[1, count + spare] = 0
        table[2, count + spare] = shares * slots

    def forward(turn, first_ref, slope_ref):
        pre = []
        wanted = []
        shifts = []
        floors = []
        for k in range(BATCH):
            job = turn * BATCH + k
            block, offset, slot = table[0, job], table[1, job], table[2, job]
            shift = (slot & (width // step - 1)) * step
            shifts.append((slot >> spread_bits, shift))
            at = pl.multiple_of(block * pairs, pairs)
            col_at = pl.multiple_of((block + offset) * step, step)
            right = right_all[pl.ds(col_at, step), :] + bias_ref[pl.ds(offset, 1), :]
            right = jnp.concatenate([right, right], axis=1)
            left = left_ref[pl.ds(at, pairs), :]
            pre += [left + right[j : j + 1, :] for j in range(step)]
            target = pltpu.roll(
                target_all[slot >> spread_bits], (width - shift) & (width - 1), 1
            )
            for j in range(step):
                want = jnp.broadcast_to(target[:, j : j + 1], (width, width))
                wanted.append(jnp.concatenate([want[:pairs], want[pairs:]], axis=1))
            floor = jnp.where(job < count, b_two[...], jnp.full((1, 2 * width), NEVER, F32))
            floors.append(jnp.broadcast_to(floor, (step * pairs, 2 * width)))
        first = jnp.maximum(jnp.concatenate(pre, axis=0), 0.0).astype(BF16)
        first_ref[...] = first
        act = jnp.dot(first, w_two[...], preferred_element_type=F32)
        act = act + jnp.concatenate(floors, axis=0)
        second = jnp.maximum(act, 0.0).astype(BF16)
        contact = jnp.dot(second, out_two[...], preferred_element_type=F32)
        slope = (contact - jnp.concatenate(wanted, axis=0)).astype(BF16)
        slope_ref[...] = jnp.where(second > 0, slope, jnp.zeros_like(slope))
        for k, (group, shift) in enumerate(shifts):
            found = jnp.zeros((width, width), F32)
            for j in range(step):
                here = contact[(k * step + j) * pairs : (k * step + j + 1) * pairs]
                here = jnp.concatenate([here[:, :width], here[:, width:]], axis=0)
                found = jnp.where(lane == j, here, found)
            mine = (lane >= shift) & (lane < shift + step)
            pred_all[group] = jnp.where(mine, pltpu.roll(found, shift, 1), pred_all[group])

    def backward(turn, first_ref, slope_ref):
        first = first_ref[...]
        slope = slope_ref[...]
        back = jnp.dot(slope, back_two[...], preferred_element_type=F32)
        back = jnp.where(first.astype(F32) > 0.0, back, 0.0)
        for k in range(BATCH):
            job = turn * BATCH + k
            block, offset = table[0, job], table[1, job]
            at = pl.multiple_of(block * pairs, pairs)
            rows = jnp.zeros((pairs, 2 * width), F32)
            cols = []
            for j in range(step):
                here = back[(k * step + j) * pairs : (k * step + j + 1) * pairs]
                rows = rows + here
                col = jnp.sum(here, axis=0, keepdims=True)
                cols.append(col[:, :width] + col[:, width:])
            row_all[pl.ds(at, pairs), :] += rows
            cols = jnp.concatenate(cols, axis=0)
            col_at = pl.multiple_of((block + offset) * step, step)
            col_all[pl.ds(col_at, step), :] += cols
            bias_all[pl.ds(offset, 1), :] += jnp.sum(cols, axis=0, keepdims=True)
        lhs = jnp.concatenate([first.T, ones], axis=0)
        outer_all[...] += jnp.dot(lhs, slope, preferred_element_type=F32)

    def body(pass_at, _):
        turn = 2 * pass_at
        backward(jnp.maximum(turn - 1, 0), first_1, slope_1)
        forward(turn, first_0, slope_0)
        backward(turn, first_0, slope_0)
        forward(turn + 1, first_1, slope_1)
        return 0

    passes = lax.div(count + 2 * BATCH - 1, 2 * BATCH)
    lax.fori_loop(0, passes, body, 0)
    backward(jnp.maximum(2 * passes - 1, 0), first_1, slope_1)

    flat = [(pred_all[group] * float(width)).T for group in range(groups)]
    flat = jnp.concatenate(flat, axis=0).astype(BF16)
    for share in range(shares):
        sum_ref[share, width + 16 :, :] = flat[share * slots * step : (share + 1) * slots * step]
    outer = outer_all[:width, :width] + outer_all[width : 2 * width, width:]
    sum_d = outer_all[2 * width : 2 * width + 1, :width] + outer_all[2 * width : 2 * width + 1, width:]
    bias = bias_all[...]
    line = lax.broadcasted_iota(jnp.int32, bias.shape, 0)
    sum_out = jnp.sum(w * outer, axis=0, keepdims=True) + b_ref[...] * sum_d
    vectors = jnp.where(line == 5, sum_d * w_out, bias)
    vectors = jnp.where(line == 6, sum_out, vectors)
    outer = outer * w_out
    high = vectors.astype(BF16).astype(F32)
    rest = (high, vectors - high)
    col = col_all[...].astype(BF16)
    rows = []
    for block in range(blocks):
        here = row_all[block * pairs : (block + 1) * pairs, :].astype(BF16)
        rows += [here[:, :width], here[:, width:]]
    embs = [cols_ref[...], next_ref[...]]
    contract = (((0,), (0,)), ((), ()))
    grads = (
        lax.dot_general(
            jnp.concatenate(rows, axis=0), emb_ref[...], contract, preferred_element_type=F32
        ).astype(BF16),
        lax.dot_general(
            col, jnp.concatenate(embs, axis=0), contract, preferred_element_type=F32
        ).astype(BF16),
    )
    half = shares // 2
    for share in range(shares):
        side, at = share // half, share % half
        sum_ref[share, :pairs, :] = rows[share]
        grad = grads[side][:, at // 2 * width : (at // 2 + 1) * width]
        sum_ref[share, pairs:width, :] = grad[at % 2 * pairs : (at % 2 + 1) * pairs]
        more = rest[share] if share < 2 else jnp.zeros_like(high)
        sum_ref[share, width : width + 16, :] = jnp.concatenate(
            [outer[8 * share : 8 * share + 8], more], axis=0
        ).astype(BF16)
    col_ref[...] = col_all[:own]
    edge_ref[...] = col[own:]


def last_kernel(
    mine_ref, other_ref, left_w_ref, right_w_ref,
    emb_ref, left_ref, right_ref, bias_ref, w_ref, b_ref, out_ref,
    both_ref, flat_ref, col_ref,
):
    core = lax.rem(place(), 2)
    width = left_w_ref.shape[1]
    pairs = width // 2
    chips = mine_ref.shape[0]
    step = width // (2 * chips)
    lows = []
    for share in range(2 * chips):
        block = jnp.where(core == share % 2, mine_ref[share // 2], other_ref[share // 2])
        both_ref[share * pairs : (share + 1) * pairs, :width] = block[:pairs]
        block = block.astype(F32)
        for k in range(col_ref.shape[0] // width):
            to = k * width + share * step
            at = width + 16 + k * step
            col_ref[to : to + step, :] = block[at : at + step]
        flat_ref[share * pairs : (share + 1) * pairs, :] = block[pairs:width]
        small = block[width : width + 16]
        w_ref[8 * share : 8 * share + 8, :] = small[:8]
        lows.append(small[8:])
    for side, grad_ref in enumerate((left_ref, right_ref)):
        for k in range(chips // 2):
            at = (side * chips // 2 + k) * width
            grad_ref[k * width : (k + 1) * width, :] = flat_ref[at : at + width, :].T
    both_ref[:, width:] = col_ref[...].astype(BF16)
    vectors = lows[0] + lows[1]
    bias_ref[...] = vectors[:5]
    b_ref[...] = vectors[5:6]
    out_ref[...] = vectors[6:7]
    weights = jnp.concatenate([left_w_ref[...], right_w_ref[...]], axis=1)
    part = 2 * width
    for k in range(both_ref.shape[0] // part):
        emb_ref[k * part : (k + 1) * part, :] = lax.dot_general(
            both_ref[k * part : (k + 1) * part, :],
            weights,
            (((1,), (1,)), ((), ())),
            preferred_element_type=F32,
        ).astype(BF16)


def shape(*dims, dtype=F32):
    return jax.ShapeDtypeStruct(dims, dtype)


def call(kernel, outs, scratch, *args, space=VMEM, limit=32):
    return pl.pallas_call(
        kernel,
        out_shape=outs,
        in_specs=[space] * len(args),
        out_specs=(VMEM,) * len(outs),
        scratch_shapes=scratch,
        compiler_params=pltpu.CompilerParams(vmem_limit_bytes=limit * 1024 * 1024),
    )(*args)


def shifted(block, axis, distance):
    devices = range(lax.axis_size(axis))
    route = [(i - distance, i) for i in devices if i - distance in devices]
    return lax.ppermute(block, axis, route)


def swapped(block, axis, bits):
    return lax.ppermute(block, axis, [(i, i ^ bits) for i in range(lax.axis_size(axis))])


def across(block, axis, groups=None):
    return lax.all_to_all(block, axis, 0, 0, axis_index_groups=groups, tiled=True)


def per_device(embeddings, w_left, w_right, pair_bias, w_pair, b_pair, w_out, tile_list, target):
    tile = place()
    core = lax.rem(tile, 2)
    slots, width = target.shape[2:4]
    rows, features = embeddings.shape
    blocks = rows // width
    pairs = width // 2
    shares = lax.axis_size("tile")
    chips = shares // 2
    step = width // shares
    part = rows // shares
    edge = part // 2
    target = target[0, 0]
    lists = jnp.transpose(tile_list, (0, 3, 1, 2)).reshape(3, 1, slots)

    target_send, left, right, emb_cols, emb_edge = call(
        prepare_kernel,
        (
            shape(shares, (slots + 2) * step, width, dtype=BF16),
            shape(rows // 2, 2 * width),
            shape(part, width),
            shape(part, features, dtype=BF16),
            shape(edge, features, dtype=BF16),
        ),
        [
            pltpu.VMEM(lists.shape, jnp.int32),
            pltpu.VMEM((slots, width, width), BF16),
            pltpu.VMEM((rows, features), BF16),
            pltpu.VMEM((features, width), BF16),
            pltpu.VMEM((features, width), BF16),
            pltpu.VMEM((slots, width, width), F32),
            pltpu.VMEM((step, width), F32),
            pltpu.VMEM((rows, width), F32),
            pltpu.SemaphoreType.DMA((5,)),
        ],
        lists, target, embeddings, w_left, w_right, space=HBM, limit=56,
    )
    target_all = across(target_send, "tile")
    emb_next = shifted(emb_edge, "bin", -1)

    chunk = (BATCH * step * pairs, 2 * width)
    grouped = (slots * shares * step // width + 1, width, width)
    sums, col, col_edge = call(
        pair_kernel,
        (
            shape(shares, width + 16 + slots * step, width, dtype=BF16),
            shape(part, width),
            shape(edge, width, dtype=BF16),
        ),
        [
            pltpu.SMEM((3, slots * shares + 2 * BATCH), jnp.int32),
            pltpu.SMEM((3, shares, width), jnp.int32),
            pltpu.SemaphoreType.DMA,
            pltpu.VMEM((3, shares, width), jnp.int32),
            pltpu.VMEM((part + edge, width), F32),
            pltpu.VMEM(grouped, F32),
            pltpu.VMEM(grouped, F32),
            pltpu.VMEM((rows // 2, 2 * width), F32),
            pltpu.VMEM((part + edge, width), F32),
            pltpu.VMEM((2 * width + 16, 2 * width), F32),
            pltpu.VMEM((8, width), F32),
            pltpu.VMEM((2 * width, 2 * width), BF16),
            pltpu.VMEM((2 * width, 2 * width), BF16),
            pltpu.VMEM((2 * width, 2 * width), BF16),
            pltpu.VMEM((1, 2 * width), F32),
            pltpu.VMEM(chunk, BF16),
            pltpu.VMEM(chunk, BF16),
            pltpu.VMEM(chunk, BF16),
            pltpu.VMEM(chunk, BF16),
        ],
        left, right, embeddings, emb_cols, emb_next, w_right, pair_bias,
        target_all, w_pair, b_pair[None], w_out[None],
    )
    sums = across(sums, "tile")
    share = jnp.sum(sums[:, : width + 16].astype(F32), axis=0).astype(BF16)
    weight = share[pairs:]
    here = lax.axis_index("bin")
    count = weight.shape[0]
    met = swapped(jnp.concatenate([weight, col_edge], axis=0), "bin", 1)
    weight = (weight.astype(F32) + met[:count].astype(F32)).astype(BF16)
    passed = met[count:]
    before = jnp.where(here % 2 == 1, passed.astype(F32), jnp.zeros((edge, width), F32))
    message = jnp.concatenate([weight, passed], axis=0)
    mets = [swapped(message, "bin", mask).astype(F32) for mask in BIN_MASKS]
    near, wrapped, far = [met[:count] for met in mets]
    weight = ((weight.astype(F32) + near) + (far + wrapped)).astype(BF16)
    for mask, met in zip(BIN_MASKS[:2], mets):
        before = jnp.where((here % 2 == 0) & ((here ^ mask) + 2 == here), met[count:], before)
    col = jnp.concatenate([col[:edge] + before, col[edge:]], axis=0).astype(BF16)
    share = jnp.concatenate([share[:pairs], weight, col], axis=0)
    groups = [list(range(k, shares, 2)) for k in range(2)]
    mine = across(jnp.broadcast_to(share[None], (chips, *share.shape)), "tile", groups)
    other = swapped(mine, "tile", 1)
    (predicted,) = call(
        join_kernel, (shape(slots, width, width, dtype=BF16),),
        [pltpu.VMEM((slots, width, width), F32)],
        sums,
    )
    grads = call(
        last_kernel,
        (
            shape(rows, features, dtype=BF16),
            shape(features, width),
            shape(features, width),
            shape(5, width),
            shape(width, width),
            shape(1, width),
            shape(1, width),
        ),
        [
            pltpu.VMEM((rows, 2 * width), BF16),
            pltpu.VMEM((2 * features, width), F32),
            pltpu.VMEM((rows, width), F32),
        ],
        mine, other, w_left, w_right,
    )
    return (predicted[None, None], *grads[:5], grads[5][0], grads[6][0])


def solution(mesh):
    return jax.shard_map(
        per_device,
        mesh=mesh,
        in_specs=(
            P("bin", None),
            P(),
            P(),
            P(),
            P(),
            P(),
            P(),
            P("bin", "tile", None, None),
            P("bin", "tile", None, None, None),
        ),
        out_specs=(
            P("bin", "tile", None, None, None),
            P("bin", None),
            P(),
            P(),
            P(),
            P(),
            P(),
            P(),
        ),
        check_vma=False,
    )
```

```python
import jax
import jax.numpy as jnp
from jax import lax
from jax.experimental import pallas as pl
from jax.experimental.pallas import tpu as pltpu
from jax.sharding import PartitionSpec as P

F32 = jnp.float32
BF16 = jnp.bfloat16
BATCH = 2
NEVER = -1e38
BIN_MASKS = (2, 6, 4)
VMEM = pl.BlockSpec(memory_space=pltpu.VMEM)
HBM = pl.BlockSpec(memory_space=pl.ANY)


def place():
    return lax.axis_index("tile")


def project_kernel(
    emb_hbm, left_hbm, right_hbm,
    left_ref, right_ref, cols_ref, edge_ref,
    emb_ref, left_w_ref, right_w_ref, full_ref, sems,
):
    copies = [
        pltpu.make_async_copy(source, target, sems.at[k])
        for k, (source, target) in enumerate(
            ((left_hbm, left_w_ref), (right_hbm, right_w_ref), (emb_hbm, emb_ref))
        )
    ]
    for copy in copies:
        copy.start()
    for copy in copies:
        copy.wait()
    tile = place()
    width = left_w_ref.shape[1]
    half = width // 2
    blocks = emb_ref.shape[0] // width
    step = right_ref.shape[0] // blocks
    weights = jnp.concatenate([left_w_ref[...], right_w_ref[...]], axis=1)
    for block in range(0, blocks, 2):
        both = jnp.dot(
            emb_ref[block * width : (block + 2) * width, :],
            weights,
            preferred_element_type=F32,
        ).astype(BF16).astype(F32)
        for k in range(2):
            left = both[k * width : (k + 1) * width, :width]
            at = (block + k) * half
            left_ref[at : at + half, :width] = left[:half]
            left_ref[at : at + half, width:] = left[half:]
        full_ref[block * width : (block + 2) * width, :] = both[:, width:]
    rows = []
    for block in range(blocks):
        at = pl.multiple_of(block * width + tile * step, step)
        right_ref[block * step : (block + 1) * step, :] = full_ref[pl.ds(at, step), :]
        at = pl.multiple_of(block * width + (tile >> 1) * (2 * step), 2 * step)
        near = emb_ref[pl.ds(at, 2 * step), :].astype(F32)
        rows.append(jnp.where((tile & 1) == 0, near[:step], near[step:]))
    rows = jnp.concatenate(rows, axis=0).astype(BF16)
    cols_ref[...] = rows
    edge_ref[...] = rows[: edge_ref.shape[0]]


def split_kernel(
    list_mine, list_other, target_mine, target_other, send_ref, flip_ref, listed_ref
):
    core = place() & 1
    slots, width, _ = target_mine.shape
    chips = send_ref.shape[0]
    step = width // (2 * chips)
    listed_ref[...] = jnp.zeros_like(listed_ref)
    for side in range(2):
        mine = core == side
        for k in range(3):
            listed_ref[3 * side + k : 3 * side + k + 1, :slots] = jnp.where(
                mine, list_mine[k], list_other[k]
            ).astype(F32)
        for slot in range(slots):
            block = jnp.where(mine, target_mine[slot], target_other[slot]).astype(F32)
            flip_ref[side * slots + slot] = (block * (1.0 / width)).T
    listed = listed_ref[...].astype(BF16)
    for chip in range(chips):
        for side in range(2):
            at = (2 * chip + core) * step
            at = pl.multiple_of(at, step)
            pieces = [
                flip_ref[side * slots + slot, pl.ds(at, step), :] for slot in range(slots)
            ]
            send_ref[chip, side * slots * step : (side + 1) * slots * step, :] = jnp.concatenate(
                pieces, axis=0
            ).astype(BF16)
        send_ref[chip, 2 * slots * step :, :] = listed


def join_kernel(mine_ref, other_ref, pred_ref, flip_ref):
    core = place() & 1
    slots, width, _ = pred_ref.shape
    chips = mine_ref.shape[0]
    step = width // (2 * chips)
    for chip in range(chips):
        for ref, side in ((mine_ref, core), (other_ref, 1 - core)):
            block = ref[chip].astype(F32)
            to = pl.multiple_of((2 * chip + side) * step, step)
            for slot in range(slots):
                flip_ref[slot, pl.ds(to, step), :] = block[slot * step : (slot + 1) * step]
    for slot in range(slots):
        pred_ref[slot] = flip_ref[slot].T.astype(BF16)


def pair_kernel(
    left_ref, right_ref, emb_ref, cols_ref, next_ref, right_w_ref, bias_ref, target_ref,
    w_ref, b_ref, out_ref,
    keep_ref, send_ref, pred_ref, col_ref, edge_ref,
    table, lists, list_sem, list_all, right_all, target_all, pred_all, row_all, col_all,
    outer_all, bias_all, w_two, out_two, back_two, b_two, first_0, first_1, slope_0, slope_1,
):
    width = w_ref.shape[0]
    pairs = width // 2
    blocks = left_ref.shape[0] // pairs
    chips = target_ref.shape[0]
    shares = 2 * chips
    step = width // shares
    slots = target_ref.shape[1] // (2 * step) - 1
    core = place() & 1
    groups = target_all.shape[0] - 1
    spread_bits = (width // step).bit_length() - 1

    for chip in range(chips):
        rows = target_ref[chip, 2 * slots * step :, :].astype(F32).astype(jnp.int32)
        for side in range(2):
            for k in range(3):
                at = 3 * side + k
                list_all[k, 2 * chip + side : 2 * chip + side + 1] = rows[at : at + 1]
    copy = pltpu.make_async_copy(list_all, lists, list_sem)
    copy.start()

    w = w_ref[...].astype(F32)
    w_out = out_ref[...]
    back = (w * w_out).T.astype(BF16)
    spread = jnp.broadcast_to(w_out * (1.0 / width), (width, width)).T.astype(BF16)
    for ref, block in ((w_two, w_ref[...]), (out_two, spread), (back_two, back)):
        ref[...] = jnp.zeros_like(ref)
        ref[:width, :width] = block
        ref[width:, width:] = block
    b_two[:, :width] = b_ref[...]
    b_two[:, width:] = b_ref[...]
    own = right_ref.shape[0]
    right_all[:own, :] = right_ref[...]
    right_next = jnp.dot(next_ref[...], right_w_ref[...], preferred_element_type=F32)
    right_all[own:, :] = right_next.astype(BF16).astype(F32)
    rows = [target_ref[chip, : 2 * slots * step, :].astype(F32) for chip in range(chips)]
    rows = jnp.concatenate(rows, axis=0)
    for group in range(groups):
        target_all[group] = rows[group * width : (group + 1) * width].T
    target_all[groups] = jnp.zeros((width, width), F32)
    for ref in (pred_all, row_all, col_all, outer_all, bias_all, first_1, slope_1):
        ref[...] = jnp.zeros_like(ref)
    lane = lax.broadcasted_iota(jnp.int32, (width, width), 1)
    ones = jnp.ones((16, BATCH * step * pairs), BF16)

    copy.wait()
    count = jnp.int32(0)
    for share in range(shares):
        for slot in range(slots):
            offset = lists[2, share, slot]
            table[0, count] = lists[0, share, slot] & (blocks - 1)
            table[1, count] = offset
            table[2, count] = share * slots + slot
            count = count + jnp.where(offset >= 0, 1, 0)
    for spare in range(2 * BATCH):
        table[0, count + spare] = 0
        table[1, count + spare] = 0
        table[2, count + spare] = shares * slots

    def forward(turn, first_ref, slope_ref):
        pre = []
        wanted = []
        shifts = []
        floors = []
        for k in range(BATCH):
            job = turn * BATCH + k
            block, offset, slot = table[0, job], table[1, job], table[2, job]
            shift = (slot & (width // step - 1)) * step
            shifts.append((slot >> spread_bits, shift))
            at = pl.multiple_of(block * pairs, pairs)
            col_at = pl.multiple_of((block + offset) * step, step)
            right = right_all[pl.ds(col_at, step), :] + bias_ref[pl.ds(offset, 1), :]
            right = jnp.concatenate([right, right], axis=1)
            left = left_ref[pl.ds(at, pairs), :]
            pre += [left + right[j : j + 1, :] for j in range(step)]
            target = pltpu.roll(
                target_all[slot >> spread_bits], (width - shift) & (width - 1), 1
            )
            for j in range(step):
                want = jnp.broadcast_to(target[:, j : j + 1], (width, width))
                wanted.append(jnp.concatenate([want[:pairs], want[pairs:]], axis=1))
            floor = jnp.where(job < count, b_two[...], jnp.full((1, 2 * width), NEVER, F32))
            floors.append(jnp.broadcast_to(floor, (step * pairs, 2 * width)))
        first = jnp.maximum(jnp.concatenate(pre, axis=0), 0.0).astype(BF16)
        first_ref[...] = first
        act = jnp.dot(first, w_two[...], preferred_element_type=F32)
        act = act + jnp.concatenate(floors, axis=0)
        second = jnp.maximum(act, 0.0).astype(BF16)
        contact = jnp.dot(second, out_two[...], preferred_element_type=F32)
        slope = (contact - jnp.concatenate(wanted, axis=0)).astype(BF16)
        slope_ref[...] = jnp.where(second > 0, slope, jnp.zeros_like(slope))
        for k, (group, shift) in enumerate(shifts):
            found = jnp.zeros((width, width), F32)
            for j in range(step):
                here = contact[(k * step + j) * pairs : (k * step + j + 1) * pairs]
                here = jnp.concatenate([here[:, :width], here[:, width:]], axis=0)
                found = jnp.where(lane == j, here, found)
            mine = (lane >= shift) & (lane < shift + step)
            pred_all[group] = jnp.where(mine, pltpu.roll(found, shift, 1), pred_all[group])

    def backward(turn, first_ref, slope_ref):
        first = first_ref[...]
        slope = slope_ref[...]
        back = jnp.dot(slope, back_two[...], preferred_element_type=F32)
        back = jnp.where(first.astype(F32) > 0.0, back, 0.0)
        for k in range(BATCH):
            job = turn * BATCH + k
            block, offset = table[0, job], table[1, job]
            at = pl.multiple_of(block * pairs, pairs)
            rows = jnp.zeros((pairs, 2 * width), F32)
            cols = []
            for j in range(step):
                here = back[(k * step + j) * pairs : (k * step + j + 1) * pairs]
                rows = rows + here
                col = jnp.sum(here, axis=0, keepdims=True)
                cols.append(col[:, :width] + col[:, width:])
            row_all[pl.ds(at, pairs), :] += rows
            cols = jnp.concatenate(cols, axis=0)
            col_at = pl.multiple_of((block + offset) * step, step)
            col_all[pl.ds(col_at, step), :] += cols
            bias_all[pl.ds(offset, 1), :] += jnp.sum(cols, axis=0, keepdims=True)
        lhs = jnp.concatenate([first.T, ones], axis=0)
        outer_all[...] += jnp.dot(lhs, slope, preferred_element_type=F32)

    def body(pass_at, _):
        turn = 2 * pass_at
        backward(jnp.maximum(turn - 1, 0), first_1, slope_1)
        forward(turn, first_0, slope_0)
        backward(turn, first_0, slope_0)
        forward(turn + 1, first_1, slope_1)
        return 0

    passes = lax.div(count + 2 * BATCH - 1, 2 * BATCH)
    lax.fori_loop(0, passes, body, 0)
    backward(jnp.maximum(2 * passes - 1, 0), first_1, slope_1)

    flat = [(pred_all[group] * float(width)).T for group in range(groups)]
    flat = jnp.concatenate(flat, axis=0).astype(BF16)
    for chip in range(chips):
        pred_ref[chip] = flat[chip * 2 * slots * step : (chip + 1) * 2 * slots * step]
    outer = outer_all[:width, :width] + outer_all[width : 2 * width, width:]
    sum_d = outer_all[2 * width : 2 * width + 1, :width] + outer_all[2 * width : 2 * width + 1, width:]
    bias = bias_all[...]
    line = lax.broadcasted_iota(jnp.int32, bias.shape, 0)
    sum_out = jnp.sum(w * outer, axis=0, keepdims=True) + b_ref[...] * sum_d
    vectors = jnp.where(line == 5, sum_d * w_out, bias)
    vectors = jnp.where(line == 6, sum_out, vectors)
    outer = outer * w_out
    high = vectors.astype(BF16).astype(F32)
    rest = (high, vectors - high)
    col = col_all[...].astype(BF16)
    rows = []
    for block in range(blocks):
        here = row_all[block * pairs : (block + 1) * pairs, :].astype(BF16)
        rows += [here[:, :width], here[:, width:]]
    embs = [cols_ref[...], next_ref[...]]
    contract = (((0,), (0,)), ((), ()))
    grads = (
        lax.dot_general(
            jnp.concatenate(rows, axis=0), emb_ref[...], contract, preferred_element_type=F32
        ).astype(BF16),
        lax.dot_general(
            col, jnp.concatenate(embs, axis=0), contract, preferred_element_type=F32
        ).astype(BF16),
    )
    def message(share):
        side, at = share // chips, share % chips
        grad = grads[side][:, at // 2 * width : (at // 2 + 1) * width]
        more = rest[share] if share < 2 else jnp.zeros_like(high)
        small = jnp.concatenate([outer[8 * share : 8 * share + 8], more], axis=0)
        return jnp.concatenate(
            [rows[share], grad[at % 2 * pairs : (at % 2 + 1) * pairs], small.astype(BF16)], axis=0
        )

    for chip in range(chips):
        even, odd = message(2 * chip), message(2 * chip + 1)
        keep_ref[chip] = jnp.where(core == 0, even, odd)
        send_ref[chip] = jnp.where(core == 0, odd, even)
    col_ref[...] = col_all[:own]
    edge_ref[...] = col[own:]


def last_kernel(
    mine_ref, other_ref, left_w_ref, right_w_ref,
    emb_ref, left_ref, right_ref, bias_ref, w_ref, b_ref, out_ref,
    both_ref, flat_ref, col_ref,
):
    core = lax.rem(place(), 2)
    width = left_w_ref.shape[1]
    pairs = width // 2
    chips = mine_ref.shape[0]
    step = width // (2 * chips)
    lows = []
    for share in range(2 * chips):
        block = jnp.where(core == share % 2, mine_ref[share // 2], other_ref[share // 2])
        both_ref[share * pairs : (share + 1) * pairs, :width] = block[:pairs]
        block = block.astype(F32)
        for k in range(col_ref.shape[0] // width):
            to = k * width + share * step
            at = width + 16 + k * step
            col_ref[to : to + step, :] = block[at : at + step]
        flat_ref[share * pairs : (share + 1) * pairs, :] = block[pairs:width]
        small = block[width : width + 16]
        w_ref[8 * share : 8 * share + 8, :] = small[:8]
        lows.append(small[8:])
    for side, grad_ref in enumerate((left_ref, right_ref)):
        for k in range(chips // 2):
            at = (side * chips // 2 + k) * width
            grad_ref[k * width : (k + 1) * width, :] = flat_ref[at : at + width, :].T
    both_ref[:, width:] = col_ref[...].astype(BF16)
    vectors = lows[0] + lows[1]
    bias_ref[...] = vectors[:5]
    b_ref[...] = vectors[5:6]
    out_ref[...] = vectors[6:7]
    weights = jnp.concatenate([left_w_ref[...], right_w_ref[...]], axis=1)
    part = 2 * width
    for k in range(both_ref.shape[0] // part):
        emb_ref[k * part : (k + 1) * part, :] = lax.dot_general(
            both_ref[k * part : (k + 1) * part, :],
            weights,
            (((1,), (1,)), ((), ())),
            preferred_element_type=F32,
        ).astype(BF16)


def shape(*dims, dtype=F32):
    return jax.ShapeDtypeStruct(dims, dtype)


def call(kernel, outs, scratch, *args, space=VMEM, limit=32):
    return pl.pallas_call(
        kernel,
        out_shape=outs,
        in_specs=[space] * len(args),
        out_specs=(VMEM,) * len(outs),
        scratch_shapes=scratch,
        compiler_params=pltpu.CompilerParams(vmem_limit_bytes=limit * 1024 * 1024),
    )(*args)


def shifted(block, axis, distance):
    devices = range(lax.axis_size(axis))
    route = [(i - distance, i) for i in devices if i - distance in devices]
    return lax.ppermute(block, axis, route)


def swapped(block, axis, bits):
    return lax.ppermute(block, axis, [(i, i ^ bits) for i in range(lax.axis_size(axis))])


def across(block, axis, groups=None):
    return lax.all_to_all(block, axis, 0, 0, axis_index_groups=groups, tiled=True)


def per_device(embeddings, w_left, w_right, pair_bias, w_pair, b_pair, w_out, tile_list, target):
    tile = place()
    core = lax.rem(tile, 2)
    slots, width = target.shape[2:4]
    rows, features = embeddings.shape
    blocks = rows // width
    pairs = width // 2
    shares = lax.axis_size("tile")
    chips = shares // 2
    step = width // shares
    part = rows // shares
    edge = part // 2
    target = target[0, 0]
    lists = jnp.transpose(tile_list, (0, 3, 1, 2)).reshape(3, 1, slots)

    target_other = swapped(target, "tile", 1)
    lists_other = swapped(lists, "tile", 1)
    left, right, emb_cols, emb_edge = call(
        project_kernel,
        (
            shape(rows // 2, 2 * width),
            shape(part, width),
            shape(part, features, dtype=BF16),
            shape(edge, features, dtype=BF16),
        ),
        [
            pltpu.VMEM((rows, features), BF16),
            pltpu.VMEM((features, width), BF16),
            pltpu.VMEM((features, width), BF16),
            pltpu.VMEM((rows, width), F32),
            pltpu.SemaphoreType.DMA((3,)),
        ],
        embeddings, w_left, w_right, space=HBM,
    )
    emb_next = shifted(emb_edge, "bin", -1)
    target_other, emb_cols = lax.optimization_barrier((target_other, emb_cols))
    (target_send,) = call(
        split_kernel,
        (shape(chips, 2 * (slots + 1) * step, width, dtype=BF16),),
        [pltpu.VMEM((2 * slots, width, width), F32), pltpu.VMEM((2 * step, width), F32)],
        lists, lists_other, target, target_other,
    )
    groups = [list(range(k, shares, 2)) for k in range(2)]
    target_all = across(target_send, "tile", groups)

    chunk = (BATCH * step * pairs, 2 * width)
    grouped = (slots * shares * step // width + 1, width, width)
    half = shape(chips, width + 16, width, dtype=BF16)
    sums, sums_send, pred, col, col_edge = call(
        pair_kernel,
        (
            half,
            half,
            shape(chips, 2 * slots * step, width, dtype=BF16),
            shape(part, width),
            shape(edge, width, dtype=BF16),
        ),
        [
            pltpu.SMEM((3, slots * shares + 2 * BATCH), jnp.int32),
            pltpu.SMEM((3, shares, width), jnp.int32),
            pltpu.SemaphoreType.DMA,
            pltpu.VMEM((3, shares, width), jnp.int32),
            pltpu.VMEM((part + edge, width), F32),
            pltpu.VMEM(grouped, F32),
            pltpu.VMEM(grouped, F32),
            pltpu.VMEM((rows // 2, 2 * width), F32),
            pltpu.VMEM((part + edge, width), F32),
            pltpu.VMEM((2 * width + 16, 2 * width), F32),
            pltpu.VMEM((8, width), F32),
            pltpu.VMEM((2 * width, 2 * width), BF16),
            pltpu.VMEM((2 * width, 2 * width), BF16),
            pltpu.VMEM((2 * width, 2 * width), BF16),
            pltpu.VMEM((1, 2 * width), F32),
            pltpu.VMEM(chunk, BF16),
            pltpu.VMEM(chunk, BF16),
            pltpu.VMEM(chunk, BF16),
            pltpu.VMEM(chunk, BF16),
        ],
        left, right, embeddings, emb_cols, emb_next, w_right, pair_bias,
        target_all, w_pair, b_pair[None], w_out[None],
    )
    sums = (sums.astype(F32) + swapped(sums_send, "tile", 1).astype(F32)).astype(BF16)
    sums = across(jnp.concatenate([sums, pred], axis=1), "tile", groups)
    pred = sums[:, width + 16 :].reshape(chips, 2, slots * step, width)
    pred_mine, pred_send = [
        lax.dynamic_index_in_dim(pred, side, 1, keepdims=False) for side in (core, 1 - core)
    ]
    pred_other = swapped(pred_send, "tile", 1)
    share = jnp.sum(sums[:, : width + 16].astype(F32), axis=0).astype(BF16)
    weight = share[pairs:]
    here = lax.axis_index("bin")
    count = weight.shape[0]
    met = swapped(jnp.concatenate([weight, col_edge], axis=0), "bin", 1)
    weight = (weight.astype(F32) + met[:count].astype(F32)).astype(BF16)
    passed = met[count:]
    before = jnp.where(here % 2 == 1, passed.astype(F32), jnp.zeros((edge, width), F32))
    message = jnp.concatenate([weight, passed], axis=0)
    mets = [swapped(message, "bin", mask).astype(F32) for mask in BIN_MASKS]
    near, wrapped, far = [met[:count] for met in mets]
    weight = ((weight.astype(F32) + near) + (far + wrapped)).astype(BF16)
    for mask, met in zip(BIN_MASKS[:2], mets):
        before = jnp.where((here % 2 == 0) & ((here ^ mask) + 2 == here), met[count:], before)
    col = jnp.concatenate([col[:edge] + before, col[edge:]], axis=0).astype(BF16)
    share = jnp.concatenate([share[:pairs], weight, col], axis=0)
    share, pred_other = lax.optimization_barrier((share, pred_other))
    mine = across(jnp.broadcast_to(share[None], (chips, *share.shape)), "tile", groups)
    other = swapped(mine, "tile", 1)
    (predicted,) = call(
        join_kernel, (shape(slots, width, width, dtype=BF16),),
        [pltpu.VMEM((slots, width, width), F32)],
        pred_mine, pred_other,
    )
    grads = call(
        last_kernel,
        (
            shape(rows, features, dtype=BF16),
            shape(features, width),
            shape(features, width),
            shape(5, width),
            shape(width, width),
            shape(1, width),
            shape(1, width),
        ),
        [
            pltpu.VMEM((rows, 2 * width), BF16),
            pltpu.VMEM((2 * features, width), F32),
            pltpu.VMEM((rows, width), F32),
        ],
        mine, other, w_left, w_right,
    )
    return (predicted[None, None], *grads[:5], grads[5][0], grads[6][0])


def solution(mesh):
    return jax.shard_map(
        per_device,
        mesh=mesh,
        in_specs=(
            P("bin", None),
            P(),
            P(),
            P(),
            P(),
            P(),
            P(),
            P("bin", "tile", None, None),
            P("bin", "tile", None, None, None),
        ),
        out_specs=(
            P("bin", "tile", None, None, None),
            P("bin", None),
            P(),
            P(),
            P(),
            P(),
            P(),
            P(),
        ),
        check_vma=False,
    )
```

```python
import jax
import jax.numpy as jnp
from jax import lax
from jax.experimental import pallas as pl
from jax.experimental.pallas import tpu as pltpu
from jax.sharding import PartitionSpec as P

F32 = jnp.float32
BF16 = jnp.bfloat16
BATCH = 2
NEVER = -1e38
BIN_MASKS = (2, 6, 4)
VMEM = pl.BlockSpec(memory_space=pltpu.VMEM)
HBM = pl.BlockSpec(memory_space=pl.ANY)


def place():
    return lax.axis_index("tile")


def project_kernel(
    emb_hbm, left_hbm, right_hbm,
    left_ref, right_ref, cols_ref, edge_ref,
    emb_ref, left_w_ref, right_w_ref, full_ref, sems,
):
    copies = [
        pltpu.make_async_copy(source, target, sems.at[k])
        for k, (source, target) in enumerate(
            ((left_hbm, left_w_ref), (right_hbm, right_w_ref), (emb_hbm, emb_ref))
        )
    ]
    for copy in copies:
        copy.start()
    for copy in copies:
        copy.wait()
    tile = place()
    width = left_w_ref.shape[1]
    half = width // 2
    blocks = emb_ref.shape[0] // width
    step = right_ref.shape[0] // blocks
    weights = jnp.concatenate([left_w_ref[...], right_w_ref[...]], axis=1)
    for block in range(0, blocks, 2):
        both = jnp.dot(
            emb_ref[block * width : (block + 2) * width, :],
            weights,
            preferred_element_type=F32,
        ).astype(BF16).astype(F32)
        for k in range(2):
            left = both[k * width : (k + 1) * width, :width]
            at = (block + k) * half
            left_ref[at : at + half, :width] = left[:half]
            left_ref[at : at + half, width:] = left[half:]
        full_ref[block * width : (block + 2) * width, :] = both[:, width:]
    rows = []
    for block in range(blocks):
        at = pl.multiple_of(block * width + tile * step, step)
        right_ref[block * step : (block + 1) * step, :] = full_ref[pl.ds(at, step), :]
        at = pl.multiple_of(block * width + (tile >> 1) * (2 * step), 2 * step)
        near = emb_ref[pl.ds(at, 2 * step), :].astype(F32)
        rows.append(jnp.where((tile & 1) == 0, near[:step], near[step:]))
    rows = jnp.concatenate(rows, axis=0).astype(BF16)
    cols_ref[...] = rows
    edge_ref[...] = rows[: edge_ref.shape[0]]


def split_kernel(
    list_mine, list_other, target_mine, target_other, send_ref, flip_ref, listed_ref
):
    core = place() & 1
    slots, width, _ = target_mine.shape
    chips = send_ref.shape[0]
    step = width // (2 * chips)
    listed_ref[...] = jnp.zeros_like(listed_ref)
    for side in range(2):
        mine = core == side
        for k in range(3):
            listed_ref[3 * side + k : 3 * side + k + 1, :slots] = jnp.where(
                mine, list_mine[k], list_other[k]
            ).astype(F32)
        for slot in range(slots):
            block = jnp.where(mine, target_mine[slot], target_other[slot]).astype(F32)
            flip_ref[side * slots + slot] = (block * (1.0 / width)).T
    listed = listed_ref[...].astype(BF16)
    for chip in range(chips):
        for side in range(2):
            at = (2 * chip + core) * step
            at = pl.multiple_of(at, step)
            pieces = [
                flip_ref[side * slots + slot, pl.ds(at, step), :] for slot in range(slots)
            ]
            send_ref[chip, side * slots * step : (side + 1) * slots * step, :] = jnp.concatenate(
                pieces, axis=0
            ).astype(BF16)
        send_ref[chip, 2 * slots * step :, :] = listed


def join_kernel(mine_ref, other_ref, pred_ref, flip_ref):
    core = place() & 1
    slots, width, _ = pred_ref.shape
    chips = mine_ref.shape[0]
    step = width // (2 * chips)
    for chip in range(chips):
        for ref, side in ((mine_ref, core), (other_ref, 1 - core)):
            block = ref[chip].astype(F32)
            to = pl.multiple_of((2 * chip + side) * step, step)
            for slot in range(slots):
                flip_ref[slot, pl.ds(to, step), :] = block[slot * step : (slot + 1) * step]
    for slot in range(slots):
        pred_ref[slot] = flip_ref[slot].T.astype(BF16)


def pair_kernel(
    left_ref, right_ref, emb_ref, cols_ref, next_ref, right_w_ref, bias_ref, target_ref,
    w_ref, b_ref, out_ref,
    keep_ref, send_ref, pred_ref, col_ref, edge_ref,
    table, lists, list_sem, list_all, right_all, target_all, pred_all, row_all, col_all,
    outer_all, bias_all, w_two, out_two, back_two, b_two, first_0, first_1, slope_0, slope_1,
):
    width = w_ref.shape[0]
    pairs = width // 2
    blocks = left_ref.shape[0] // pairs
    chips = target_ref.shape[0]
    shares = 2 * chips
    step = width // shares
    slots = target_ref.shape[1] // (2 * step) - 1
    core = place() & 1
    groups = target_all.shape[0] - 1
    spread_bits = (width // step).bit_length() - 1

    for chip in range(chips):
        rows = target_ref[chip, 2 * slots * step :, :].astype(F32).astype(jnp.int32)
        for side in range(2):
            for k in range(3):
                at = 3 * side + k
                list_all[k, 2 * chip + side : 2 * chip + side + 1] = rows[at : at + 1]
    copy = pltpu.make_async_copy(list_all, lists, list_sem)
    copy.start()

    w = w_ref[...].astype(F32)
    w_out = out_ref[...]
    back = (w * w_out).T.astype(BF16)
    for ref, block in ((w_two, w_ref[...]), (back_two, back)):
        ref[...] = jnp.zeros_like(ref)
        ref[:width, :width] = block
        ref[width:, width:] = block
    b_two[:, :width] = b_ref[...]
    b_two[:, width:] = b_ref[...]
    out_two[:, :width] = w_out * (1.0 / width)
    out_two[:, width:] = w_out * (1.0 / width)
    own = right_ref.shape[0]
    right_all[:own, :] = right_ref[...]
    right_next = jnp.dot(next_ref[...], right_w_ref[...], preferred_element_type=F32)
    right_all[own:, :] = right_next.astype(BF16).astype(F32)
    rows = [target_ref[chip, : 2 * slots * step, :].astype(F32) for chip in range(chips)]
    rows = jnp.concatenate(rows, axis=0)
    for group in range(groups):
        target_all[group] = rows[group * width : (group + 1) * width].T
    target_all[groups] = jnp.zeros((width, width), F32)
    for ref in (pred_all, row_all, col_all, outer_all, bias_all, first_1, slope_1):
        ref[...] = jnp.zeros_like(ref)
    lane = lax.broadcasted_iota(jnp.int32, (width, width), 1)
    ones = jnp.ones((16, BATCH * step * pairs), BF16)

    copy.wait()
    count = jnp.int32(0)
    for share in range(shares):
        for slot in range(slots):
            offset = lists[2, share, slot]
            table[0, count] = lists[0, share, slot] & (blocks - 1)
            table[1, count] = offset
            table[2, count] = share * slots + slot
            count = count + jnp.where(offset >= 0, 1, 0)
    for spare in range(2 * BATCH):
        table[0, count + spare] = 0
        table[1, count + spare] = 0
        table[2, count + spare] = shares * slots

    def forward(turn, first_ref, slope_ref):
        pre = []
        wanted = []
        shifts = []
        floors = []
        for k in range(BATCH):
            job = turn * BATCH + k
            block, offset, slot = table[0, job], table[1, job], table[2, job]
            shift = (slot & (width // step - 1)) * step
            shifts.append((slot >> spread_bits, shift))
            at = pl.multiple_of(block * pairs, pairs)
            col_at = pl.multiple_of((block + offset) * step, step)
            right = right_all[pl.ds(col_at, step), :] + bias_ref[pl.ds(offset, 1), :]
            right = jnp.concatenate([right, right], axis=1)
            left = left_ref[pl.ds(at, pairs), :]
            pre += [left + right[j : j + 1, :] for j in range(step)]
            target = pltpu.roll(
                target_all[slot >> spread_bits], (width - shift) & (width - 1), 1
            )
            for j in range(step):
                want = jnp.broadcast_to(target[:, j : j + 1], (width, width))
                wanted.append(jnp.concatenate([want[:pairs], want[pairs:]], axis=1))
            floor = jnp.where(job < count, b_two[...], jnp.full((1, 2 * width), NEVER, F32))
            floors.append(jnp.broadcast_to(floor, (step * pairs, 2 * width)))
        first = jnp.maximum(jnp.concatenate(pre, axis=0), 0.0).astype(BF16)
        first_ref[...] = first
        act = jnp.dot(first, w_two[...], preferred_element_type=F32)
        act = act + jnp.concatenate(floors, axis=0)
        parts = jnp.maximum(act, 0.0) * out_two[...]
        contact = jnp.concatenate(
            [
                jnp.broadcast_to(
                    jnp.sum(parts[:, s * width : (s + 1) * width], axis=1, keepdims=True),
                    (parts.shape[0], width),
                )
                for s in range(2)
            ],
            axis=1,
        )
        slope = contact - jnp.concatenate(wanted, axis=0)
        slope_ref[...] = jnp.where(act > 0.0, slope, 0.0).astype(BF16)
        for k, (group, shift) in enumerate(shifts):
            found = jnp.zeros((width, width), F32)
            for j in range(step):
                here = contact[(k * step + j) * pairs : (k * step + j + 1) * pairs]
                here = jnp.concatenate([here[:, :width], here[:, width:]], axis=0)
                found = jnp.where(lane == j, here, found)
            mine = (lane >= shift) & (lane < shift + step)
            pred_all[group] = jnp.where(mine, pltpu.roll(found, shift, 1), pred_all[group])

    def backward(turn, first_ref, slope_ref):
        first = first_ref[...]
        slope = slope_ref[...]
        back = jnp.dot(slope, back_two[...], preferred_element_type=F32)
        back = jnp.where(first.astype(F32) > 0.0, back, 0.0)
        for k in range(BATCH):
            job = turn * BATCH + k
            block, offset = table[0, job], table[1, job]
            at = pl.multiple_of(block * pairs, pairs)
            rows = jnp.zeros((pairs, 2 * width), F32)
            cols = []
            for j in range(step):
                here = back[(k * step + j) * pairs : (k * step + j + 1) * pairs]
                rows = rows + here
                col = jnp.sum(here, axis=0, keepdims=True)
                cols.append(col[:, :width] + col[:, width:])
            row_all[pl.ds(at, pairs), :] += rows
            cols = jnp.concatenate(cols, axis=0)
            col_at = pl.multiple_of((block + offset) * step, step)
            col_all[pl.ds(col_at, step), :] += cols
            bias_all[pl.ds(offset, 1), :] += jnp.sum(cols, axis=0, keepdims=True)
        lhs = jnp.concatenate([first.T, ones], axis=0)
        outer_all[...] += jnp.dot(lhs, slope, preferred_element_type=F32)

    def body(pass_at, _):
        turn = 2 * pass_at
        backward(jnp.maximum(turn - 1, 0), first_1, slope_1)
        forward(turn, first_0, slope_0)
        backward(turn, first_0, slope_0)
        forward(turn + 1, first_1, slope_1)
        return 0

    passes = lax.div(count + 2 * BATCH - 1, 2 * BATCH)
    lax.fori_loop(0, passes, body, 0)
    backward(jnp.maximum(2 * passes - 1, 0), first_1, slope_1)

    flat = [(pred_all[group] * float(width)).T for group in range(groups)]
    flat = jnp.concatenate(flat, axis=0).astype(BF16)
    for chip in range(chips):
        pred_ref[chip] = flat[chip * 2 * slots * step : (chip + 1) * 2 * slots * step]
    outer = outer_all[:width, :width] + outer_all[width : 2 * width, width:]
    sum_d = outer_all[2 * width : 2 * width + 1, :width] + outer_all[2 * width : 2 * width + 1, width:]
    bias = bias_all[...]
    line = lax.broadcasted_iota(jnp.int32, bias.shape, 0)
    sum_out = jnp.sum(w * outer, axis=0, keepdims=True) + b_ref[...] * sum_d
    vectors = jnp.where(line == 5, sum_d * w_out, bias)
    vectors = jnp.where(line == 6, sum_out, vectors)
    outer = outer * w_out
    high = vectors.astype(BF16).astype(F32)
    rest = (high, vectors - high)
    col = col_all[...].astype(BF16)
    rows = []
    for block in range(blocks):
        here = row_all[block * pairs : (block + 1) * pairs, :].astype(BF16)
        rows += [here[:, :width], here[:, width:]]
    embs = [cols_ref[...], next_ref[...]]
    contract = (((0,), (0,)), ((), ()))
    grads = (
        lax.dot_general(
            jnp.concatenate(rows, axis=0), emb_ref[...], contract, preferred_element_type=F32
        ).astype(BF16),
        lax.dot_general(
            col, jnp.concatenate(embs, axis=0), contract, preferred_element_type=F32
        ).astype(BF16),
    )
    def message(share):
        side, at = share // chips, share % chips
        grad = grads[side][:, at // 2 * width : (at // 2 + 1) * width]
        more = rest[share] if share < 2 else jnp.zeros_like(high)
        small = jnp.concatenate([outer[8 * share : 8 * share + 8], more], axis=0)
        return jnp.concatenate(
            [rows[share], grad[at % 2 * pairs : (at % 2 + 1) * pairs], small.astype(BF16)], axis=0
        )

    for chip in range(chips):
        even, odd = message(2 * chip), message(2 * chip + 1)
        keep_ref[chip] = jnp.where(core == 0, even, odd)
        send_ref[chip] = jnp.where(core == 0, odd, even)
    col_ref[...] = col_all[:own]
    edge_ref[...] = col[own:]


def last_kernel(
    mine_ref, other_ref, left_w_ref, right_w_ref,
    emb_ref, left_ref, right_ref, bias_ref, w_ref, b_ref, out_ref,
    both_ref, flat_ref, col_ref,
):
    core = lax.rem(place(), 2)
    width = left_w_ref.shape[1]
    pairs = width // 2
    chips = mine_ref.shape[0]
    step = width // (2 * chips)
    lows = []
    for share in range(2 * chips):
        block = jnp.where(core == share % 2, mine_ref[share // 2], other_ref[share // 2])
        both_ref[share * pairs : (share + 1) * pairs, :width] = block[:pairs]
        block = block.astype(F32)
        for k in range(col_ref.shape[0] // width):
            to = k * width + share * step
            at = width + 16 + k * step
            col_ref[to : to + step, :] = block[at : at + step]
        flat_ref[share * pairs : (share + 1) * pairs, :] = block[pairs:width]
        small = block[width : width + 16]
        w_ref[8 * share : 8 * share + 8, :] = small[:8]
        lows.append(small[8:])
    for side, grad_ref in enumerate((left_ref, right_ref)):
        for k in range(chips // 2):
            at = (side * chips // 2 + k) * width
            grad_ref[k * width : (k + 1) * width, :] = flat_ref[at : at + width, :].T
    both_ref[:, width:] = col_ref[...].astype(BF16)
    vectors = lows[0] + lows[1]
    bias_ref[...] = vectors[:5]
    b_ref[...] = vectors[5:6]
    out_ref[...] = vectors[6:7]
    weights = jnp.concatenate([left_w_ref[...], right_w_ref[...]], axis=1)
    part = 2 * width
    for k in range(both_ref.shape[0] // part):
        emb_ref[k * part : (k + 1) * part, :] = lax.dot_general(
            both_ref[k * part : (k + 1) * part, :],
            weights,
            (((1,), (1,)), ((), ())),
            preferred_element_type=F32,
        ).astype(BF16)


def shape(*dims, dtype=F32):
    return jax.ShapeDtypeStruct(dims, dtype)


def call(kernel, outs, scratch, *args, space=VMEM, limit=32):
    return pl.pallas_call(
        kernel,
        out_shape=outs,
        in_specs=[space] * len(args),
        out_specs=(VMEM,) * len(outs),
        scratch_shapes=scratch,
        compiler_params=pltpu.CompilerParams(vmem_limit_bytes=limit * 1024 * 1024),
    )(*args)


def shifted(block, axis, distance):
    devices = range(lax.axis_size(axis))
    route = [(i - distance, i) for i in devices if i - distance in devices]
    return lax.ppermute(block, axis, route)


def swapped(block, axis, bits):
    return lax.ppermute(block, axis, [(i, i ^ bits) for i in range(lax.axis_size(axis))])


def across(block, axis, groups=None):
    return lax.all_to_all(block, axis, 0, 0, axis_index_groups=groups, tiled=True)


def per_device(embeddings, w_left, w_right, pair_bias, w_pair, b_pair, w_out, tile_list, target):
    tile = place()
    core = lax.rem(tile, 2)
    slots, width = target.shape[2:4]
    rows, features = embeddings.shape
    blocks = rows // width
    pairs = width // 2
    shares = lax.axis_size("tile")
    chips = shares // 2
    step = width // shares
    part = rows // shares
    edge = part // 2
    target = target[0, 0]
    lists = jnp.transpose(tile_list, (0, 3, 1, 2)).reshape(3, 1, slots)

    target_other = swapped(target, "tile", 1)
    lists_other = swapped(lists, "tile", 1)
    left, right, emb_cols, emb_edge = call(
        project_kernel,
        (
            shape(rows // 2, 2 * width),
            shape(part, width),
            shape(part, features, dtype=BF16),
            shape(edge, features, dtype=BF16),
        ),
        [
            pltpu.VMEM((rows, features), BF16),
            pltpu.VMEM((features, width), BF16),
            pltpu.VMEM((features, width), BF16),
            pltpu.VMEM((rows, width), F32),
            pltpu.SemaphoreType.DMA((3,)),
        ],
        embeddings, w_left, w_right, space=HBM, limit=56,
    )
    emb_next = shifted(emb_edge, "bin", -1)
    target_other, emb_cols = lax.optimization_barrier((target_other, emb_cols))
    (target_send,) = call(
        split_kernel,
        (shape(chips, 2 * (slots + 1) * step, width, dtype=BF16),),
        [pltpu.VMEM((2 * slots, width, width), F32), pltpu.VMEM((2 * step, width), F32)],
        lists, lists_other, target, target_other,
    )
    groups = [list(range(k, shares, 2)) for k in range(2)]
    target_send, emb_next, left, right, emb_cols = lax.optimization_barrier(
        (target_send, emb_next, left, right, emb_cols)
    )
    target_all = across(target_send, "tile", groups)

    chunk = (BATCH * step * pairs, 2 * width)
    grouped = (slots * shares * step // width + 1, width, width)
    half = shape(chips, width + 16, width, dtype=BF16)
    sums, sums_send, pred, col, col_edge = call(
        pair_kernel,
        (
            half,
            half,
            shape(chips, 2 * slots * step, width, dtype=BF16),
            shape(part, width),
            shape(edge, width, dtype=BF16),
        ),
        [
            pltpu.SMEM((3, slots * shares + 2 * BATCH), jnp.int32),
            pltpu.SMEM((3, shares, width), jnp.int32),
            pltpu.SemaphoreType.DMA,
            pltpu.VMEM((3, shares, width), jnp.int32),
            pltpu.VMEM((part + edge, width), F32),
            pltpu.VMEM(grouped, F32),
            pltpu.VMEM(grouped, F32),
            pltpu.VMEM((rows // 2, 2 * width), F32),
            pltpu.VMEM((part + edge, width), F32),
            pltpu.VMEM((2 * width + 16, 2 * width), F32),
            pltpu.VMEM((8, width), F32),
            pltpu.VMEM((2 * width, 2 * width), BF16),
            pltpu.VMEM((1, 2 * width), F32),
            pltpu.VMEM((2 * width, 2 * width), BF16),
            pltpu.VMEM((1, 2 * width), F32),
            pltpu.VMEM(chunk, BF16),
            pltpu.VMEM(chunk, BF16),
            pltpu.VMEM(chunk, BF16),
            pltpu.VMEM(chunk, BF16),
        ],
        left, right, embeddings, emb_cols, emb_next, w_right, pair_bias,
        target_all, w_pair, b_pair[None], w_out[None],
    )
    sums = (sums.astype(F32) + swapped(sums_send, "tile", 1).astype(F32)).astype(BF16)
    sums = across(jnp.concatenate([sums, pred], axis=1), "tile", groups)
    pred = sums[:, width + 16 :].reshape(chips, 2, slots * step, width)
    pred_mine, pred_send = [
        lax.dynamic_index_in_dim(pred, side, 1, keepdims=False) for side in (core, 1 - core)
    ]
    pred_other = swapped(pred_send, "tile", 1)
    share = jnp.sum(sums[:, : width + 16].astype(F32), axis=0).astype(BF16)
    weight = share[pairs:]
    here = lax.axis_index("bin")
    count = weight.shape[0]
    met = swapped(jnp.concatenate([weight, col_edge], axis=0), "bin", 1)
    weight = (weight.astype(F32) + met[:count].astype(F32)).astype(BF16)
    passed = met[count:]
    before = jnp.where(here % 2 == 1, passed.astype(F32), jnp.zeros((edge, width), F32))
    message = jnp.concatenate([weight, passed], axis=0)
    mets = [swapped(message, "bin", mask).astype(F32) for mask in BIN_MASKS]
    near, wrapped, far = [met[:count] for met in mets]
    weight = ((weight.astype(F32) + near) + (far + wrapped)).astype(BF16)
    for mask, met in zip(BIN_MASKS[:2], mets):
        before = jnp.where((here % 2 == 0) & ((here ^ mask) + 2 == here), met[count:], before)
    col = jnp.concatenate([col[:edge] + before, col[edge:]], axis=0).astype(BF16)
    share = jnp.concatenate([share[:pairs], weight, col], axis=0)
    share, pred_other = lax.optimization_barrier((share, pred_other))
    mine = across(jnp.broadcast_to(share[None], (chips, *share.shape)), "tile", groups)
    other = swapped(mine, "tile", 1)
    (predicted,) = call(
        join_kernel, (shape(slots, width, width, dtype=BF16),),
        [pltpu.VMEM((slots, width, width), F32)],
        pred_mine, pred_other,
    )
    grads = call(
        last_kernel,
        (
            shape(rows, features, dtype=BF16),
            shape(features, width),
            shape(features, width),
            shape(5, width),
            shape(width, width),
            shape(1, width),
            shape(1, width),
        ),
        [
            pltpu.VMEM((rows, 2 * width), BF16),
            pltpu.VMEM((2 * features, width), F32),
            pltpu.VMEM((rows, width), F32),
        ],
        mine, other, w_left, w_right,
    )
    return (predicted[None, None], *grads[:5], grads[5][0], grads[6][0])


def solution(mesh):
    return jax.shard_map(
        per_device,
        mesh=mesh,
        in_specs=(
            P("bin", None),
            P(),
            P(),
            P(),
            P(),
            P(),
            P(),
            P("bin", "tile", None, None),
            P("bin", "tile", None, None, None),
        ),
        out_specs=(
            P("bin", "tile", None, None, None),
            P("bin", None),
            P(),
            P(),
            P(),
            P(),
            P(),
            P(),
        ),
        check_vma=False,
    )
```

```python
import jax
import jax.numpy as jnp
from jax import lax
from jax.experimental import pallas as pl
from jax.experimental.pallas import tpu as pltpu
from jax.sharding import PartitionSpec as P

F32 = jnp.float32
BF16 = jnp.bfloat16
BATCH = 2
NEVER = -1e38
VMEM = pl.BlockSpec(memory_space=pltpu.VMEM)
HBM = pl.BlockSpec(memory_space=pl.ANY)


def place():
    return lax.axis_index("tile")


def project_kernel(
    emb_hbm, left_hbm, right_hbm,
    left_ref, right_ref,
    emb_ref, left_w_ref, right_w_ref, full_ref, sems,
):
    copies = [
        pltpu.make_async_copy(source, target, sems.at[k])
        for k, (source, target) in enumerate(
            ((left_hbm, left_w_ref), (right_hbm, right_w_ref), (emb_hbm, emb_ref))
        )
    ]
    for copy in copies:
        copy.start()
    for copy in copies:
        copy.wait()
    tile = place()
    width = left_w_ref.shape[1]
    half = width // 2
    blocks = emb_ref.shape[0] // width
    step = right_ref.shape[0] // blocks
    weights = jnp.concatenate([left_w_ref[...], right_w_ref[...]], axis=1)
    for block in range(0, blocks, 2):
        both = jnp.dot(
            emb_ref[block * width : (block + 2) * width, :],
            weights,
            preferred_element_type=F32,
        ).astype(BF16).astype(F32)
        for k in range(2):
            left = both[k * width : (k + 1) * width, :width]
            at = (block + k) * half
            left_ref[at : at + half, :width] = left[:half]
            left_ref[at : at + half, width:] = left[half:]
        full_ref[block * width : (block + 2) * width, :] = both[:, width:]
    for block in range(blocks):
        at = pl.multiple_of(block * width + tile * step, step)
        right_ref[block * step : (block + 1) * step, :] = full_ref[pl.ds(at, step), :]


def split_kernel(
    list_mine, list_other, target_mine, target_other, send_ref, flip_ref, listed_ref
):
    core = place() & 1
    slots, width, _ = target_mine.shape
    chips = send_ref.shape[0]
    step = width // (2 * chips)
    listed_ref[...] = jnp.zeros_like(listed_ref)
    for side in range(2):
        mine = core == side
        for k in range(3):
            listed_ref[3 * side + k : 3 * side + k + 1, :slots] = jnp.where(
                mine, list_mine[k], list_other[k]
            ).astype(F32)
        for slot in range(slots):
            block = jnp.where(mine, target_mine[slot], target_other[slot]).astype(F32)
            flip_ref[side * slots + slot] = (block * (1.0 / width)).T
    listed = listed_ref[...].astype(BF16)
    for chip in range(chips):
        for side in range(2):
            at = (2 * chip + core) * step
            at = pl.multiple_of(at, step)
            pieces = [
                flip_ref[side * slots + slot, pl.ds(at, step), :] for slot in range(slots)
            ]
            send_ref[chip, side * slots * step : (side + 1) * slots * step, :] = jnp.concatenate(
                pieces, axis=0
            ).astype(BF16)
        send_ref[chip, 2 * slots * step :, :] = listed


def join_kernel(mine_ref, other_ref, pred_ref, flip_ref):
    core = place() & 1
    slots, width, _ = pred_ref.shape
    chips = mine_ref.shape[0]
    step = width // (2 * chips)
    for chip in range(chips):
        for ref, side in ((mine_ref, core), (other_ref, 1 - core)):
            block = ref[chip].astype(F32)
            to = pl.multiple_of((2 * chip + side) * step, step)
            for slot in range(slots):
                flip_ref[slot, pl.ds(to, step), :] = block[slot * step : (slot + 1) * step]
    for slot in range(slots):
        pred_ref[slot] = flip_ref[slot].T.astype(BF16)


def pair_kernel(
    left_ref, right_ref, emb_ref, cols_ref, next_ref, right_w_ref, bias_ref, target_ref,
    w_ref, b_ref, out_ref,
    keep_ref, send_ref, pred_ref, col_ref, edge_ref,
    table, lists, list_sem, list_all, right_all, target_all, pred_all, row_all, col_all,
    outer_all, bias_all, w_two, out_two, back_two, b_two, first_0, first_1, slope_0, slope_1,
):
    width = w_ref.shape[0]
    pairs = width // 2
    blocks = left_ref.shape[0] // pairs
    chips = target_ref.shape[0]
    shares = 2 * chips
    step = width // shares
    slots = target_ref.shape[1] // (2 * step) - 1
    core = place() & 1
    groups = target_all.shape[0] - 1
    spread_bits = (width // step).bit_length() - 1

    for chip in range(chips):
        rows = target_ref[chip, 2 * slots * step :, :].astype(F32).astype(jnp.int32)
        for side in range(2):
            for k in range(3):
                at = 3 * side + k
                list_all[k, 2 * chip + side : 2 * chip + side + 1] = rows[at : at + 1]
    copy = pltpu.make_async_copy(list_all, lists, list_sem)
    copy.start()

    w = w_ref[...].astype(F32)
    w_out = out_ref[...]
    back = (w * w_out).T.astype(BF16)
    spread = jnp.broadcast_to(w_out * (1.0 / width), (width, width)).T.astype(BF16)
    for ref, block in ((w_two, w_ref[...]), (out_two, spread), (back_two, back)):
        ref[...] = jnp.zeros_like(ref)
        ref[:width, :width] = block
        ref[width:, width:] = block
    b_two[:, :width] = b_ref[...]
    b_two[:, width:] = b_ref[...]
    own = right_ref.shape[0]
    right_all[:own, :] = right_ref[...]
    right_next = jnp.dot(next_ref[...], right_w_ref[...], preferred_element_type=F32)
    right_all[own:, :] = right_next.astype(BF16).astype(F32)
    rows = [target_ref[chip, : 2 * slots * step, :].astype(F32) for chip in range(chips)]
    rows = jnp.concatenate(rows, axis=0)
    for group in range(groups):
        target_all[group] = rows[group * width : (group + 1) * width].T
    target_all[groups] = jnp.zeros((width, width), F32)
    for ref in (pred_all, row_all, col_all, outer_all, bias_all, first_1, slope_1):
        ref[...] = jnp.zeros_like(ref)
    lane = lax.broadcasted_iota(jnp.int32, (width, width), 1)
    ones = jnp.ones((16, BATCH * step * pairs), BF16)

    copy.wait()
    count = jnp.int32(0)
    for share in range(shares):
        for slot in range(slots):
            offset = lists[2, share, slot]
            table[0, count] = lists[0, share, slot] & (blocks - 1)
            table[1, count] = offset
            table[2, count] = share * slots + slot
            count = count + jnp.where(offset >= 0, 1, 0)
    for spare in range(2 * BATCH):
        table[0, count + spare] = 0
        table[1, count + spare] = 0
        table[2, count + spare] = shares * slots

    def forward(turn, first_ref, slope_ref):
        pre = []
        wanted = []
        shifts = []
        floors = []
        for k in range(BATCH):
            job = turn * BATCH + k
            block, offset, slot = table[0, job], table[1, job], table[2, job]
            shift = (slot & (width // step - 1)) * step
            shifts.append((slot >> spread_bits, shift))
            at = pl.multiple_of(block * pairs, pairs)
            col_at = pl.multiple_of((block + offset) * step, step)
            right = right_all[pl.ds(col_at, step), :] + bias_ref[pl.ds(offset, 1), :]
            right = jnp.concatenate([right, right], axis=1)
            left = left_ref[pl.ds(at, pairs), :]
            pre += [left + right[j : j + 1, :] for j in range(step)]
            target = pltpu.roll(
                target_all[slot >> spread_bits], (width - shift) & (width - 1), 1
            ).astype(BF16)
            for j in range(step):
                want = jnp.broadcast_to(target[:, j : j + 1], (width, width)).astype(F32)
                wanted.append(jnp.concatenate([want[:pairs], want[pairs:]], axis=1))
            floor = jnp.where(job < count, b_two[...], jnp.full((1, 2 * width), NEVER, F32))
            floors.append(jnp.broadcast_to(floor, (step * pairs, 2 * width)))
        first = jnp.maximum(jnp.concatenate(pre, axis=0), 0.0).astype(BF16)
        first_ref[...] = first
        act = jnp.dot(first, w_two[...], preferred_element_type=F32)
        act = act + jnp.concatenate(floors, axis=0)
        second = jnp.maximum(act, 0.0).astype(BF16)
        contact = jnp.dot(second, out_two[...], preferred_element_type=F32)
        slope = (contact - jnp.concatenate(wanted, axis=0)).astype(BF16)
        slope_ref[...] = jnp.where(second > 0, slope, jnp.zeros_like(slope))
        for k, (group, shift) in enumerate(shifts):
            found = jnp.zeros((width, width), F32)
            for j in range(step):
                here = contact[(k * step + j) * pairs : (k * step + j + 1) * pairs]
                here = jnp.concatenate([here[:, :width], here[:, width:]], axis=0)
                found = jnp.where(lane == j, here, found)
            mine = (lane >= shift) & (lane < shift + step)
            pred_all[group] = jnp.where(mine, pltpu.roll(found, shift, 1), pred_all[group])

    def backward(turn, first_ref, slope_ref):
        first = first_ref[...]
        slope = slope_ref[...]
        back = jnp.dot(slope, back_two[...], preferred_element_type=F32)
        back = jnp.where(first.astype(F32) > 0.0, back, 0.0)
        for k in range(BATCH):
            job = turn * BATCH + k
            block, offset = table[0, job], table[1, job]
            at = pl.multiple_of(block * pairs, pairs)
            rows = jnp.zeros((pairs, 2 * width), F32)
            cols = []
            for j in range(step):
                here = back[(k * step + j) * pairs : (k * step + j + 1) * pairs]
                rows = rows + here
                col = jnp.sum(here, axis=0, keepdims=True)
                cols.append(col[:, :width] + col[:, width:])
            row_all[pl.ds(at, pairs), :] += rows
            cols = jnp.concatenate(cols, axis=0)
            col_at = pl.multiple_of((block + offset) * step, step)
            col_all[pl.ds(col_at, step), :] += cols
            bias_all[pl.ds(offset, 1), :] += jnp.sum(cols, axis=0, keepdims=True)
        lhs = jnp.concatenate([first.T, ones], axis=0)
        outer_all[...] += jnp.dot(lhs, slope, preferred_element_type=F32)

    def body(pass_at, _):
        turn = 2 * pass_at
        backward(jnp.maximum(turn - 1, 0), first_1, slope_1)
        forward(turn, first_0, slope_0)
        backward(turn, first_0, slope_0)
        forward(turn + 1, first_1, slope_1)
        return 0

    passes = lax.div(count + 2 * BATCH - 1, 2 * BATCH)
    lax.fori_loop(0, passes, body, 0)
    backward(jnp.maximum(2 * passes - 1, 0), first_1, slope_1)

    flat = [(pred_all[group] * float(width)).T for group in range(groups)]
    flat = jnp.concatenate(flat, axis=0).astype(BF16)
    for chip in range(chips):
        pred_ref[chip] = flat[chip * 2 * slots * step : (chip + 1) * 2 * slots * step]
    outer = outer_all[:width, :width] + outer_all[width : 2 * width, width:]
    sum_d = outer_all[2 * width : 2 * width + 1, :width] + outer_all[2 * width : 2 * width + 1, width:]
    bias = bias_all[...]
    line = lax.broadcasted_iota(jnp.int32, bias.shape, 0)
    sum_out = jnp.sum(w * outer, axis=0, keepdims=True) + b_ref[...] * sum_d
    vectors = jnp.where(line == 5, sum_d * w_out, bias)
    vectors = jnp.where(line == 6, sum_out, vectors)
    outer = outer * w_out
    high = vectors.astype(BF16).astype(F32)
    rest = (high, vectors - high)
    col = col_all[...].astype(BF16)
    rows = []
    for block in range(blocks):
        here = row_all[block * pairs : (block + 1) * pairs, :].astype(BF16)
        rows += [here[:, :width], here[:, width:]]
    embs = [cols_ref[...], next_ref[...]]
    contract = (((0,), (0,)), ((), ()))
    grads = (
        lax.dot_general(
            jnp.concatenate(rows, axis=0), emb_ref[...], contract, preferred_element_type=F32
        ).astype(BF16),
        lax.dot_general(
            col, jnp.concatenate(embs, axis=0), contract, preferred_element_type=F32
        ).astype(BF16),
    )
    def message(share):
        side, at = share // chips, share % chips
        grad = grads[side][:, at // 2 * width : (at // 2 + 1) * width]
        more = rest[share] if share < 2 else jnp.zeros_like(high)
        small = jnp.concatenate([outer[8 * share : 8 * share + 8], more], axis=0)
        return jnp.concatenate(
            [rows[share], grad[at % 2 * pairs : (at % 2 + 1) * pairs], small.astype(BF16)], axis=0
        )

    for chip in range(chips):
        even, odd = message(2 * chip), message(2 * chip + 1)
        keep_ref[chip] = jnp.where(core == 0, even, odd)
        send_ref[chip] = jnp.where(core == 0, odd, even)
    col_ref[...] = col_all[:own]
    edge_ref[...] = col[own:]


def share_kernel(sum_ref, edge_ref, row_ref, message_ref, mine_ref, send_ref):
    core = place() & 1
    chips, _, width = sum_ref.shape
    pairs = width // 2
    head = width + 16
    slot_rows = mine_ref.shape[1]
    total = jnp.zeros((head, width), F32)
    for chip in range(chips):
        total = total + sum_ref[chip, :head, :].astype(F32)
        first = sum_ref[chip, head : head + slot_rows, :]
        second = sum_ref[chip, head + slot_rows :, :]
        mine_ref[chip] = jnp.where(core == 0, first, second)
        send_ref[chip] = jnp.where(core == 0, second, first)
    total = total.astype(BF16)
    row_ref[...] = total[:pairs]
    for bin_at in range(message_ref.shape[0]):
        message_ref[bin_at, : head - pairs, :] = total[pairs:]
        message_ref[bin_at, head - pairs :, :] = edge_ref[...]


def total_kernel(met_ref, row_ref, col_ref, message_ref):
    here = lax.axis_index("bin")
    bins = met_ref.shape[0]
    width = row_ref.shape[1]
    pairs = row_ref.shape[0]
    edge = col_ref.shape[0] // 2
    count = met_ref.shape[1] - edge
    total = jnp.zeros((count, width), F32)
    before = jnp.zeros((edge, width), F32)
    for bin_at in range(bins):
        total = total + met_ref[bin_at, :count, :].astype(F32)
        near = met_ref[bin_at, count:, :].astype(F32)
        before = jnp.where(here == bin_at + 1, near, before)
    total = total.astype(BF16)
    col = col_ref[...]
    top = (col[:edge] + before).astype(BF16)
    low = col[edge:].astype(BF16)
    for chip in range(message_ref.shape[0]):
        message_ref[chip, :pairs, :] = row_ref[...]
        message_ref[chip, pairs : pairs + count, :] = total
        message_ref[chip, pairs + count : pairs + count + edge, :] = top
        message_ref[chip, pairs + count + edge :, :] = low


def last_kernel(
    mine_ref, other_ref, left_w_ref, right_w_ref,
    emb_ref, left_ref, right_ref, bias_ref, w_ref, b_ref, out_ref,
    both_ref, flat_ref, col_ref,
):
    core = lax.rem(place(), 2)
    width = left_w_ref.shape[1]
    pairs = width // 2
    chips = mine_ref.shape[0]
    step = width // (2 * chips)
    lows = []
    for share in range(2 * chips):
        block = jnp.where(core == share % 2, mine_ref[share // 2], other_ref[share // 2])
        both_ref[share * pairs : (share + 1) * pairs, :width] = block[:pairs]
        block = block.astype(F32)
        for k in range(col_ref.shape[0] // width):
            to = k * width + share * step
            at = width + 16 + k * step
            col_ref[to : to + step, :] = block[at : at + step]
        flat_ref[share * pairs : (share + 1) * pairs, :] = block[pairs:width]
        small = block[width : width + 16]
        w_ref[8 * share : 8 * share + 8, :] = small[:8]
        lows.append(small[8:])
    for side, grad_ref in enumerate((left_ref, right_ref)):
        for k in range(chips // 2):
            at = (side * chips // 2 + k) * width
            grad_ref[k * width : (k + 1) * width, :] = flat_ref[at : at + width, :].T
    both_ref[:, width:] = col_ref[...].astype(BF16)
    vectors = lows[0] + lows[1]
    bias_ref[...] = vectors[:5]
    b_ref[...] = vectors[5:6]
    out_ref[...] = vectors[6:7]
    weights = jnp.concatenate([left_w_ref[...], right_w_ref[...]], axis=1)
    part = 2 * width
    for k in range(both_ref.shape[0] // part):
        emb_ref[k * part : (k + 1) * part, :] = lax.dot_general(
            both_ref[k * part : (k + 1) * part, :],
            weights,
            (((1,), (1,)), ((), ())),
            preferred_element_type=F32,
        ).astype(BF16)


def shape(*dims, dtype=F32):
    return jax.ShapeDtypeStruct(dims, dtype)


def call(kernel, outs, scratch, *args, space=VMEM, limit=32):
    return pl.pallas_call(
        kernel,
        out_shape=outs,
        in_specs=[space] * len(args),
        out_specs=(VMEM,) * len(outs),
        scratch_shapes=scratch,
        compiler_params=pltpu.CompilerParams(vmem_limit_bytes=limit * 1024 * 1024),
    )(*args)


def shifted(block, axis, distance):
    devices = range(lax.axis_size(axis))
    route = [(i - distance, i) for i in devices if i - distance in devices]
    return lax.ppermute(block, axis, route)


def swapped(block, axis, bits):
    return lax.ppermute(block, axis, [(i, i ^ bits) for i in range(lax.axis_size(axis))])


def across(block, axis, groups=None):
    return lax.all_to_all(block, axis, 0, 0, axis_index_groups=groups, tiled=True)


def per_device(embeddings, w_left, w_right, pair_bias, w_pair, b_pair, w_out, tile_list, target):
    tile = place()
    core = lax.rem(tile, 2)
    slots, width = target.shape[2:4]
    rows, features = embeddings.shape
    blocks = rows // width
    pairs = width // 2
    shares = lax.axis_size("tile")
    chips = shares // 2
    step = width // shares
    part = rows // shares
    edge = part // 2
    target = target[0, 0]
    lists = jnp.transpose(tile_list, (0, 3, 1, 2)).reshape(3, 1, slots)

    emb_cols = lax.dynamic_slice_in_dim(
        embeddings.reshape(blocks, shares, step, features), tile, 1, 1
    ).reshape(part, features)
    emb_next = shifted(emb_cols[:edge], "bin", -1)
    target_other = swapped(target, "tile", 1)
    lists_other = swapped(lists, "tile", 1)
    left, right = call(
        project_kernel,
        (shape(rows // 2, 2 * width), shape(part, width)),
        [
            pltpu.VMEM((rows, features), BF16),
            pltpu.VMEM((features, width), BF16),
            pltpu.VMEM((features, width), BF16),
            pltpu.VMEM((rows, width), F32),
            pltpu.SemaphoreType.DMA((3,)),
        ],
        embeddings, w_left, w_right, space=HBM, limit=56,
    )
    target_other, emb_next, left = lax.optimization_barrier((target_other, emb_next, left))
    (target_send,) = call(
        split_kernel,
        (shape(chips, 2 * (slots + 1) * step, width, dtype=BF16),),
        [pltpu.VMEM((2 * slots, width, width), F32), pltpu.VMEM((2 * step, width), F32)],
        lists, lists_other, target, target_other,
    )
    groups = [list(range(k, shares, 2)) for k in range(2)]
    target_all = across(target_send, "tile", groups)

    chunk = (BATCH * step * pairs, 2 * width)
    grouped = (slots * shares * step // width + 1, width, width)
    half = shape(chips, width + 16, width, dtype=BF16)
    sums, sums_send, pred, col, col_edge = call(
        pair_kernel,
        (
            half,
            half,
            shape(chips, 2 * slots * step, width, dtype=BF16),
            shape(part, width),
            shape(edge, width, dtype=BF16),
        ),
        [
            pltpu.SMEM((3, slots * shares + 2 * BATCH), jnp.int32),
            pltpu.SMEM((3, shares, width), jnp.int32),
            pltpu.SemaphoreType.DMA,
            pltpu.VMEM((3, shares, width), jnp.int32),
            pltpu.VMEM((part + edge, width), F32),
            pltpu.VMEM(grouped, F32),
            pltpu.VMEM(grouped, F32),
            pltpu.VMEM((rows // 2, 2 * width), F32),
            pltpu.VMEM((part + edge, width), F32),
            pltpu.VMEM((2 * width + 16, 2 * width), F32),
            pltpu.VMEM((8, width), F32),
            pltpu.VMEM((2 * width, 2 * width), BF16),
            pltpu.VMEM((2 * width, 2 * width), BF16),
            pltpu.VMEM((2 * width, 2 * width), BF16),
            pltpu.VMEM((1, 2 * width), F32),
            pltpu.VMEM(chunk, BF16),
            pltpu.VMEM(chunk, BF16),
            pltpu.VMEM(chunk, BF16),
            pltpu.VMEM(chunk, BF16),
        ],
        left, right, embeddings, emb_cols, emb_next, w_right, pair_bias,
        target_all, w_pair, b_pair[None], w_out[None],
    )
    sums = (sums.astype(F32) + swapped(sums_send, "tile", 1).astype(F32)).astype(BF16)
    sums = across(jnp.concatenate([sums, pred], axis=1), "tile", groups)
    bins = lax.axis_size("bin")
    row, weight, pred_mine, pred_send = call(
        share_kernel,
        (
            shape(pairs, width, dtype=BF16),
            shape(bins, pairs + 16 + edge, width, dtype=BF16),
            shape(chips, slots * step, width, dtype=BF16),
            shape(chips, slots * step, width, dtype=BF16),
        ),
        [], sums, col_edge,
    )
    weight = across(weight, "bin")
    (mine,) = call(
        total_kernel,
        (shape(chips, width + 16 + part, width, dtype=BF16),),
        [], weight, row, col,
    )
    mine = across(mine, "tile", groups)
    mine, pred_send = lax.optimization_barrier((mine, pred_send))
    pred_other = swapped(pred_send, "tile", 1)
    other = swapped(mine, "tile", 1)
    (predicted,) = call(
        join_kernel, (shape(slots, width, width, dtype=BF16),),
        [pltpu.VMEM((slots, width, width), F32)],
        pred_mine, pred_other,
    )
    grads = call(
        last_kernel,
        (
            shape(rows, features, dtype=BF16),
            shape(features, width),
            shape(features, width),
            shape(5, width),
            shape(width, width),
            shape(1, width),
            shape(1, width),
        ),
        [
            pltpu.VMEM((rows, 2 * width), BF16),
            pltpu.VMEM((2 * features, width), F32),
            pltpu.VMEM((rows, width), F32),
        ],
        mine, other, w_left, w_right,
    )
    return (predicted[None, None], *grads[:5], grads[5][0], grads[6][0])


def solution(mesh):
    return jax.shard_map(
        per_device,
        mesh=mesh,
        in_specs=(
            P("bin", None),
            P(),
            P(),
            P(),
            P(),
            P(),
            P(),
            P("bin", "tile", None, None),
            P("bin", "tile", None, None, None),
        ),
        out_specs=(
            P("bin", "tile", None, None, None),
            P("bin", None),
            P(),
            P(),
            P(),
            P(),
            P(),
            P(),
        ),
        check_vma=False,
    )
```

```python
import jax
import jax.numpy as jnp
from jax import lax
from jax.experimental import pallas as pl
from jax.experimental.pallas import tpu as pltpu
from jax.sharding import PartitionSpec as P

F32 = jnp.float32
BF16 = jnp.bfloat16
BATCH = 2
NEVER = -1e38
VMEM = pl.BlockSpec(memory_space=pltpu.VMEM)


def place():
    return lax.axis_index("tile")


def split_kernel(
    list_mine, list_other, target_mine, target_other, send_ref, flip_ref, listed_ref
):
    core = place() & 1
    slots, width, _ = target_mine.shape
    chips = send_ref.shape[0]
    step = width // (2 * chips)
    listed_ref[...] = jnp.zeros_like(listed_ref)
    for side in range(2):
        mine = core == side
        for k in range(3):
            listed_ref[3 * side + k : 3 * side + k + 1, :slots] = jnp.where(
                mine, list_mine[k], list_other[k]
            ).astype(F32)
        for slot in range(slots):
            block = jnp.where(mine, target_mine[slot], target_other[slot]).astype(F32)
            flip_ref[side * slots + slot] = (block * (1.0 / width)).T
    listed = listed_ref[...].astype(BF16)
    for chip in range(chips):
        for side in range(2):
            at = (2 * chip + core) * step
            at = pl.multiple_of(at, step)
            pieces = [
                flip_ref[side * slots + slot, pl.ds(at, step), :] for slot in range(slots)
            ]
            send_ref[chip, side * slots * step : (side + 1) * slots * step, :] = jnp.concatenate(
                pieces, axis=0
            ).astype(BF16)
        send_ref[chip, 2 * slots * step :, :] = listed


def join_kernel(mine_ref, other_ref, pred_ref, flip_ref):
    core = place() & 1
    slots, width, _ = pred_ref.shape
    chips = mine_ref.shape[0]
    step = width // (2 * chips)
    for chip in range(chips):
        for ref, side in ((mine_ref, core), (other_ref, 1 - core)):
            block = ref[chip].astype(F32)
            to = pl.multiple_of((2 * chip + side) * step, step)
            for slot in range(slots):
                flip_ref[slot, pl.ds(to, step), :] = block[slot * step : (slot + 1) * step]
    for slot in range(slots):
        pred_ref[slot] = flip_ref[slot].T.astype(BF16)


def pair_kernel(
    emb_ref, cols_ref, next_ref, left_w_ref, right_w_ref, const_ref, target_ref, w_ref,
    keep_ref, send_ref, pred_ref, col_ref, edge_ref,
    table, lists, list_sem, list_all, left_ref, full_ref, right_all, target_all, pred_all, row_all, col_all,
    outer_all, bias_all, w_two, out_two, back_two, b_two, scale_two, first_0, first_1, slope_0, slope_1,
):
    tile = place()
    width = w_ref.shape[0]
    pairs = width // 2
    blocks = emb_ref.shape[0] // width
    chips = target_ref.shape[0]
    shares = 2 * chips
    step = width // shares
    slots = target_ref.shape[1] // (2 * step) - 1
    core = tile & 1
    groups = target_all.shape[0] - 1
    spread_bits = (width // step).bit_length() - 1

    for chip in range(chips):
        rows = target_ref[chip, 2 * slots * step :, :].astype(F32).astype(jnp.int32)
        for side in range(2):
            for k in range(3):
                at = 3 * side + k
                list_all[k, 2 * chip + side : 2 * chip + side + 1] = rows[at : at + 1]
    copy = pltpu.make_async_copy(list_all, lists, list_sem)
    copy.start()

    w = w_ref[...].astype(F32)
    w_out = const_ref[6:7, :]
    b_pair = const_ref[5:6, :]
    back = (w * w_out).T.astype(BF16)
    spread = jnp.broadcast_to(w_out * (1.0 / width), (width, width)).T.astype(BF16)
    for ref, block in ((w_two, w_ref[...]), (out_two, spread), (back_two, back)):
        ref[...] = jnp.zeros_like(ref)
        ref[:width, :width] = block
        ref[width:, width:] = block
    w_low = (w_out * (1.0 / width)).astype(BF16).astype(F32)
    scale = jnp.where(w_low == 0.0, 1.0, w_out * (1.0 / width) / jnp.where(w_low == 0.0, 1.0, w_low))
    scale_two[:, :width] = scale
    scale_two[:, width:] = scale
    b_two[:, :width] = b_pair
    b_two[:, width:] = b_pair
    weights = jnp.concatenate([left_w_ref[...], right_w_ref[...]], axis=1)
    for block in range(0, blocks, 2):
        both = jnp.dot(
            emb_ref[block * width : (block + 2) * width, :],
            weights,
            preferred_element_type=F32,
        ).astype(BF16).astype(F32)
        for k in range(2):
            left = both[k * width : (k + 1) * width, :width]
            at = (block + k) * pairs
            left_ref[at : at + pairs, :width] = left[:pairs]
            left_ref[at : at + pairs, width:] = left[pairs:]
        full_ref[block * width : (block + 2) * width, :] = both[:, width:]
    own = blocks * step
    for block in range(blocks):
        at = pl.multiple_of(block * width + tile * step, step)
        right_all[block * step : (block + 1) * step, :] = full_ref[pl.ds(at, step), :]
    right_next = jnp.dot(next_ref[...], right_w_ref[...], preferred_element_type=F32)
    right_all[own:, :] = right_next.astype(BF16).astype(F32)
    rows = [target_ref[chip, : 2 * slots * step, :].astype(F32) for chip in range(chips)]
    rows = jnp.concatenate(rows, axis=0)
    for group in range(groups):
        target_all[group] = rows[group * width : (group + 1) * width].T
    target_all[groups] = jnp.zeros((width, width), F32)
    for ref in (pred_all, row_all, col_all, outer_all, bias_all, first_1, slope_1):
        ref[...] = jnp.zeros_like(ref)
    lane = lax.broadcasted_iota(jnp.int32, (width, width), 1)
    ones = jnp.ones((16, BATCH * step * pairs), BF16)

    copy.wait()
    count = jnp.int32(0)
    for share in range(shares):
        for slot in range(slots):
            offset = lists[2, share, slot]
            table[0, count] = lists[0, share, slot] & (blocks - 1)
            table[1, count] = offset
            table[2, count] = share * slots + slot
            count = count + jnp.where(offset >= 0, 1, 0)
    for spare in range(2 * BATCH):
        table[0, count + spare] = 0
        table[1, count + spare] = 0
        table[2, count + spare] = shares * slots

    def forward(turn, first_ref, slope_ref):
        pre = []
        wanted = []
        shifts = []
        floors = []
        for k in range(BATCH):
            job = turn * BATCH + k
            block, offset, slot = table[0, job], table[1, job], table[2, job]
            shift = (slot & (width // step - 1)) * step
            shifts.append((slot >> spread_bits, shift))
            at = pl.multiple_of(block * pairs, pairs)
            col_at = pl.multiple_of((block + offset) * step, step)
            right = right_all[pl.ds(col_at, step), :] + const_ref[pl.ds(offset, 1), :]
            right = jnp.concatenate([right, right], axis=1)
            left = left_ref[pl.ds(at, pairs), :]
            pre += [left + right[j : j + 1, :] for j in range(step)]
            target = pltpu.roll(
                target_all[slot >> spread_bits], (width - shift) & (width - 1), 1
            ).astype(BF16)
            for j in range(step):
                want = jnp.broadcast_to(target[:, j : j + 1], (width, width)).astype(F32)
                wanted.append(jnp.concatenate([want[:pairs], want[pairs:]], axis=1))
            floor = jnp.where(job < count, b_two[...], jnp.full((1, 2 * width), NEVER, F32))
            floors.append(jnp.broadcast_to(floor, (step * pairs, 2 * width)))
        first = jnp.maximum(jnp.concatenate(pre, axis=0), 0.0).astype(BF16)
        first_ref[...] = first
        act = jnp.dot(first, w_two[...], preferred_element_type=F32)
        act = act + jnp.concatenate(floors, axis=0)
        second = (jnp.maximum(act, 0.0) * scale_two[...]).astype(BF16)
        contact = jnp.dot(second, out_two[...], preferred_element_type=F32)
        slope = (contact - jnp.concatenate(wanted, axis=0)).astype(BF16)
        slope_ref[...] = jnp.where(second > 0, slope, jnp.zeros_like(slope))
        for k, (group, shift) in enumerate(shifts):
            found = jnp.zeros((width, width), F32)
            for j in range(step):
                here = contact[(k * step + j) * pairs : (k * step + j + 1) * pairs]
                here = jnp.concatenate([here[:, :width], here[:, width:]], axis=0)
                found = jnp.where(lane == j, here, found)
            mine = (lane >= shift) & (lane < shift + step)
            pred_all[group] = jnp.where(mine, pltpu.roll(found, shift, 1), pred_all[group])

    def backward(turn, first_ref, slope_ref):
        first = first_ref[...]
        slope = slope_ref[...]
        back = jnp.dot(slope, back_two[...], preferred_element_type=F32)
        back = jnp.where(first.astype(F32) > 0.0, back, 0.0)
        for k in range(BATCH):
            job = turn * BATCH + k
            block, offset = table[0, job], table[1, job]
            at = pl.multiple_of(block * pairs, pairs)
            rows = jnp.zeros((pairs, 2 * width), F32)
            cols = []
            for j in range(step):
                here = back[(k * step + j) * pairs : (k * step + j + 1) * pairs]
                rows = rows + here
                col = jnp.sum(here, axis=0, keepdims=True)
                cols.append(col[:, :width] + col[:, width:])
            row_all[pl.ds(at, pairs), :] += rows
            cols = jnp.concatenate(cols, axis=0)
            col_at = pl.multiple_of((block + offset) * step, step)
            col_all[pl.ds(col_at, step), :] += cols
            bias_all[pl.ds(offset, 1), :] += jnp.sum(cols, axis=0, keepdims=True)
        lhs = jnp.concatenate([first.T, ones], axis=0)
        outer_all[...] += jnp.dot(lhs, slope, preferred_element_type=F32)

    def body(pass_at, _):
        turn = 2 * pass_at
        backward(jnp.maximum(turn - 1, 0), first_1, slope_1)
        forward(turn, first_0, slope_0)
        backward(turn, first_0, slope_0)
        forward(turn + 1, first_1, slope_1)
        return 0

    passes = lax.div(count + 2 * BATCH - 1, 2 * BATCH)
    lax.fori_loop(0, passes, body, 0)
    backward(jnp.maximum(2 * passes - 1, 0), first_1, slope_1)

    flat = [(pred_all[group] * float(width)).T for group in range(groups)]
    flat = jnp.concatenate(flat, axis=0).astype(BF16)
    for chip in range(chips):
        pred_ref[chip] = flat[chip * 2 * slots * step : (chip + 1) * 2 * slots * step]
    outer = outer_all[:width, :width] + outer_all[width : 2 * width, width:]
    sum_d = outer_all[2 * width : 2 * width + 1, :width] + outer_all[2 * width : 2 * width + 1, width:]
    bias = bias_all[...]
    line = lax.broadcasted_iota(jnp.int32, bias.shape, 0)
    sum_out = jnp.sum(w * outer, axis=0, keepdims=True) + b_pair * sum_d
    vectors = jnp.where(line == 5, sum_d * w_out, bias)
    vectors = jnp.where(line == 6, sum_out, vectors)
    outer = outer * w_out
    high = vectors.astype(BF16).astype(F32)
    rest = (high, vectors - high)
    col = col_all[...].astype(BF16)
    rows = []
    for block in range(blocks):
        here = row_all[block * pairs : (block + 1) * pairs, :].astype(BF16)
        rows += [here[:, :width], here[:, width:]]
    embs = [cols_ref[...], next_ref[...]]
    contract = (((0,), (0,)), ((), ()))
    grads = (
        lax.dot_general(
            jnp.concatenate(rows, axis=0), emb_ref[...], contract, preferred_element_type=F32
        ).astype(BF16),
        lax.dot_general(
            col, jnp.concatenate(embs, axis=0), contract, preferred_element_type=F32
        ).astype(BF16),
    )
    def message(share):
        side, at = share // chips, share % chips
        grad = grads[side][:, at // 2 * width : (at // 2 + 1) * width]
        more = rest[share] if share < 2 else jnp.zeros_like(high)
        small = jnp.concatenate([outer[8 * share : 8 * share + 8], more], axis=0)
        return jnp.concatenate(
            [rows[share], grad[at % 2 * pairs : (at % 2 + 1) * pairs], small.astype(BF16)], axis=0
        )

    for chip in range(chips):
        even, odd = message(2 * chip), message(2 * chip + 1)
        keep_ref[chip] = jnp.where(core == 0, even, odd)
        send_ref[chip] = jnp.where(core == 0, odd, even)
    col_ref[...] = col_all[:own]
    edge_ref[...] = col[own:]


def share_kernel(sum_ref, edge_ref, row_ref, message_ref, mine_ref, send_ref):
    core = place() & 1
    chips, _, width = sum_ref.shape
    pairs = width // 2
    head = width + 16
    slot_rows = mine_ref.shape[1]
    total = jnp.zeros((head, width), F32)
    for chip in range(chips):
        total = total + sum_ref[chip, :head, :].astype(F32)
        first = sum_ref[chip, head : head + slot_rows, :]
        second = sum_ref[chip, head + slot_rows :, :]
        mine_ref[chip] = jnp.where(core == 0, first, second)
        send_ref[chip] = jnp.where(core == 0, second, first)
    total = total.astype(BF16)
    row_ref[...] = total[:pairs]
    for bin_at in range(message_ref.shape[0]):
        message_ref[bin_at, : head - pairs, :] = total[pairs:]
        message_ref[bin_at, head - pairs :, :] = edge_ref[...]


def total_kernel(met_ref, row_ref, col_ref, message_ref):
    here = lax.axis_index("bin")
    bins = met_ref.shape[0]
    width = row_ref.shape[1]
    pairs = row_ref.shape[0]
    edge = col_ref.shape[0] // 2
    count = met_ref.shape[1] - edge
    total = jnp.zeros((count, width), F32)
    before = jnp.zeros((edge, width), F32)
    for bin_at in range(bins):
        total = total + met_ref[bin_at, :count, :].astype(F32)
        near = met_ref[bin_at, count:, :].astype(F32)
        before = jnp.where(here == bin_at + 1, near, before)
    total = total.astype(BF16)
    col = col_ref[...]
    top = (col[:edge] + before).astype(BF16)
    low = col[edge:].astype(BF16)
    for chip in range(message_ref.shape[0]):
        message_ref[chip, :pairs, :] = row_ref[...]
        message_ref[chip, pairs : pairs + count, :] = total
        message_ref[chip, pairs + count : pairs + count + edge, :] = top
        message_ref[chip, pairs + count + edge :, :] = low


def last_kernel(
    mine_ref, other_ref, left_w_ref, right_w_ref,
    emb_ref, left_ref, right_ref, bias_ref, w_ref, b_ref, out_ref,
    both_ref, flat_ref, col_ref,
):
    core = lax.rem(place(), 2)
    width = left_w_ref.shape[1]
    pairs = width // 2
    chips = mine_ref.shape[0]
    step = width // (2 * chips)
    lows = []
    for share in range(2 * chips):
        block = jnp.where(core == share % 2, mine_ref[share // 2], other_ref[share // 2])
        both_ref[share * pairs : (share + 1) * pairs, :width] = block[:pairs]
        block = block.astype(F32)
        for k in range(col_ref.shape[0] // width):
            to = k * width + share * step
            at = width + 16 + k * step
            col_ref[to : to + step, :] = block[at : at + step]
        flat_ref[share * pairs : (share + 1) * pairs, :] = block[pairs:width]
        small = block[width : width + 16]
        w_ref[8 * share : 8 * share + 8, :] = small[:8]
        lows.append(small[8:])
    for side, grad_ref in enumerate((left_ref, right_ref)):
        for k in range(chips // 2):
            at = (side * chips // 2 + k) * width
            grad_ref[k * width : (k + 1) * width, :] = flat_ref[at : at + width, :].T
    both_ref[:, width:] = col_ref[...].astype(BF16)
    vectors = lows[0] + lows[1]
    bias_ref[...] = vectors[:5]
    b_ref[...] = vectors[5:6]
    out_ref[...] = vectors[6:7]
    weights = jnp.concatenate([left_w_ref[...], right_w_ref[...]], axis=1)
    part = 2 * width
    for k in range(both_ref.shape[0] // part):
        emb_ref[k * part : (k + 1) * part, :] = lax.dot_general(
            both_ref[k * part : (k + 1) * part, :],
            weights,
            (((1,), (1,)), ((), ())),
            preferred_element_type=F32,
        ).astype(BF16)


def shape(*dims, dtype=F32):
    return jax.ShapeDtypeStruct(dims, dtype)


def call(kernel, outs, scratch, *args):
    return pl.pallas_call(
        kernel,
        out_shape=outs,
        in_specs=[VMEM] * len(args),
        out_specs=(VMEM,) * len(outs),
        scratch_shapes=scratch,
        compiler_params=pltpu.CompilerParams(vmem_limit_bytes=32 * 1024 * 1024),
    )(*args)


def swapped(block, axis, bits):
    return lax.ppermute(block, axis, [(i, i ^ bits) for i in range(lax.axis_size(axis))])


def across(block, axis, groups=None):
    return lax.all_to_all(block, axis, 0, 0, axis_index_groups=groups, tiled=True)


def per_device(embeddings, w_left, w_right, pair_bias, w_pair, b_pair, w_out, tile_list, target):
    tile = place()
    core = lax.rem(tile, 2)
    slots, width = target.shape[2:4]
    rows, features = embeddings.shape
    blocks = rows // width
    pairs = width // 2
    shares = lax.axis_size("tile")
    chips = shares // 2
    step = width // shares
    part = rows // shares
    edge = part // 2
    target = target[0, 0]
    lists = jnp.transpose(tile_list, (0, 3, 1, 2)).reshape(3, 1, slots)

    emb_cols = lax.dynamic_slice_in_dim(
        embeddings.reshape(blocks, shares, step, features), tile, 1, 1
    ).reshape(part, features)
    target_other = swapped(target, "tile", 1)
    lists_other = swapped(lists, "tile", 1)
    bins = lax.axis_size("bin")
    emb_next = lax.ppermute(emb_cols[:edge], "bin", [(k + 1, k) for k in range(bins - 1)])
    consts = jnp.concatenate(
        [pair_bias, b_pair[None], w_out[None], jnp.zeros((1, width), F32)], axis=0
    )
    (target_send,) = call(
        split_kernel,
        (shape(chips, 2 * (slots + 1) * step, width, dtype=BF16),),
        [pltpu.VMEM((2 * slots, width, width), F32), pltpu.VMEM((2 * step, width), F32)],
        lists, lists_other, target, target_other,
    )
    groups = [list(range(k, shares, 2)) for k in range(2)]
    target_all = across(target_send, "tile", groups)

    chunk = (BATCH * step * pairs, 2 * width)
    grouped = (slots * shares * step // width + 1, width, width)
    half = shape(chips, width + 16, width, dtype=BF16)
    sums, sums_send, pred, col, col_edge = call(
        pair_kernel,
        (
            half,
            half,
            shape(chips, 2 * slots * step, width, dtype=BF16),
            shape(part, width),
            shape(edge, width, dtype=BF16),
        ),
        [
            pltpu.SMEM((3, slots * shares + 2 * BATCH), jnp.int32),
            pltpu.SMEM((3, shares, width), jnp.int32),
            pltpu.SemaphoreType.DMA,
            pltpu.VMEM((3, shares, width), jnp.int32),
            pltpu.VMEM((rows // 2, 2 * width), F32),
            pltpu.VMEM((rows, width), F32),
            pltpu.VMEM((part + edge, width), F32),
            pltpu.VMEM(grouped, F32),
            pltpu.VMEM(grouped, F32),
            pltpu.VMEM((rows // 2, 2 * width), F32),
            pltpu.VMEM((part + edge, width), F32),
            pltpu.VMEM((2 * width + 16, 2 * width), F32),
            pltpu.VMEM((8, width), F32),
            pltpu.VMEM((2 * width, 2 * width), BF16),
            pltpu.VMEM((2 * width, 2 * width), BF16),
            pltpu.VMEM((2 * width, 2 * width), BF16),
            pltpu.VMEM((1, 2 * width), F32),
            pltpu.VMEM((1, 2 * width), F32),
            pltpu.VMEM(chunk, BF16),
            pltpu.VMEM(chunk, BF16),
            pltpu.VMEM(chunk, BF16),
            pltpu.VMEM(chunk, BF16),
        ],
        embeddings, emb_cols, emb_next, w_left, w_right, consts, target_all, w_pair,
    )
    sums = (sums.astype(F32) + swapped(sums_send, "tile", 1).astype(F32)).astype(BF16)
    sums = across(jnp.concatenate([sums, pred], axis=1), "tile", groups)
    row, weight, pred_mine, pred_send = call(
        share_kernel,
        (
            shape(pairs, width, dtype=BF16),
            shape(bins, pairs + 16 + edge, width, dtype=BF16),
            shape(chips, slots * step, width, dtype=BF16),
            shape(chips, slots * step, width, dtype=BF16),
        ),
        [], sums, col_edge,
    )
    weight = across(weight, "bin")
    (mine,) = call(
        total_kernel,
        (shape(chips, width + 16 + part, width, dtype=BF16),),
        [], weight, row, col,
    )
    mine = across(mine, "tile", groups)
    mine, pred_send = lax.optimization_barrier((mine, pred_send))
    pred_other = swapped(pred_send, "tile", 1)
    other = swapped(mine, "tile", 1)
    (predicted,) = call(
        join_kernel, (shape(slots, width, width, dtype=BF16),),
        [pltpu.VMEM((slots, width, width), F32)],
        pred_mine, pred_other,
    )
    grads = call(
        last_kernel,
        (
            shape(rows, features, dtype=BF16),
            shape(features, width),
            shape(features, width),
            shape(5, width),
            shape(width, width),
            shape(1, width),
            shape(1, width),
        ),
        [
            pltpu.VMEM((rows, 2 * width), BF16),
            pltpu.VMEM((2 * features, width), F32),
            pltpu.VMEM((rows, width), F32),
        ],
        mine, other, w_left, w_right,
    )
    return (predicted[None, None], *grads[:5], grads[5][0], grads[6][0])


def solution(mesh):
    return jax.shard_map(
        per_device,
        mesh=mesh,
        in_specs=(
            P("bin", None),
            P(),
            P(),
            P(),
            P(),
            P(),
            P(),
            P("bin", "tile", None, None),
            P("bin", "tile", None, None, None),
        ),
        out_specs=(
            P("bin", "tile", None, None, None),
            P("bin", None),
            P(),
            P(),
            P(),
            P(),
            P(),
            P(),
        ),
        check_vma=False,
    )
```

```python
import jax
import jax.numpy as jnp
from jax import lax
from jax.experimental import pallas as pl
from jax.experimental.pallas import tpu as pltpu
from jax.sharding import PartitionSpec as P

F32 = jnp.float32
BF16 = jnp.bfloat16
BATCH = 2
NEVER = -1e38
TINY = 1e-30
VMEM = pl.BlockSpec(memory_space=pltpu.VMEM)
HBM = pl.BlockSpec(memory_space=pl.ANY)


def place():
    return lax.axis_index("tile")


def split_kernel(
    list_mine, list_other, target_mine, target_other, send_ref, flip_ref, listed_ref
):
    core = place() & 1
    slots, width, _ = target_mine.shape
    chips = send_ref.shape[0]
    step = width // (2 * chips)
    listed_ref[...] = jnp.zeros_like(listed_ref)
    for side in range(2):
        mine = core == side
        for k in range(3):
            listed_ref[3 * side + k : 3 * side + k + 1, :slots] = jnp.where(
                mine, list_mine[k], list_other[k]
            ).astype(F32)
        for slot in range(slots):
            block = jnp.where(mine, target_mine[slot], target_other[slot]).astype(F32)
            flip_ref[side * slots + slot] = (block * (1.0 / width)).T
    listed = listed_ref[...].astype(BF16)
    for chip in range(chips):
        for side in range(2):
            at = (2 * chip + core) * step
            at = pl.multiple_of(at, step)
            pieces = [
                flip_ref[side * slots + slot, pl.ds(at, step), :] for slot in range(slots)
            ]
            send_ref[chip, side * slots * step : (side + 1) * slots * step, :] = jnp.concatenate(
                pieces, axis=0
            ).astype(BF16)
        send_ref[chip, 2 * slots * step :, :] = listed


def pair_kernel(
    emb_ref, cols_ref, next_ref, left_w_ref, right_w_ref, const_ref, target_ref, w_ref,
    keep_ref, send_ref, pred_ref, col_ref, edge_ref,
    table, lists, list_sem, list_all, left_ref, full_ref, right_all, target_all, pred_all, row_all, col_all,
    outer_all, bias_all, w_two, out_two, back_two, b_two, scale_two, first_0, first_1, slope_0, slope_1,
):
    tile = place()
    width = w_ref.shape[0]
    pairs = width // 2
    blocks = emb_ref.shape[0] // width
    chips = target_ref.shape[0]
    shares = 2 * chips
    step = width // shares
    slots = target_ref.shape[1] // (2 * step) - 1
    core = tile & 1
    groups = target_all.shape[0] - 1
    spread_bits = (width // step).bit_length() - 1

    for chip in range(chips):
        rows = target_ref[chip, 2 * slots * step :, :].astype(F32).astype(jnp.int32)
        for side in range(2):
            for k in range(3):
                at = 3 * side + k
                list_all[k, 2 * chip + side : 2 * chip + side + 1] = rows[at : at + 1]
    copy = pltpu.make_async_copy(list_all, lists, list_sem)
    copy.start()

    w = w_ref[...].astype(F32)
    w_out = const_ref[6:7, :]
    b_pair = const_ref[5:6, :]
    size = jnp.abs(w_out)
    power = jnp.exp2(jnp.floor(jnp.log2(jnp.maximum(size, TINY))))
    power = jnp.where(size < TINY, 0.0, power).astype(BF16).astype(F32)
    power = jnp.where(w_out < 0.0, -power, power)
    ratio = jnp.where(size < TINY, 1.0, w_out / jnp.where(size < TINY, 1.0, power))
    back = (w * power).T.astype(BF16)
    spread = jnp.broadcast_to(power * (1.0 / width), (width, width)).T.astype(BF16)
    for ref, block in ((w_two, w_ref[...]), (out_two, spread), (back_two, back)):
        ref[...] = jnp.zeros_like(ref)
        ref[:width, :width] = block
        ref[width:, width:] = block
    scale_two[:, :width] = ratio
    scale_two[:, width:] = ratio
    b_two[:, :width] = b_pair
    b_two[:, width:] = b_pair
    weights = jnp.concatenate([left_w_ref[...], right_w_ref[...]], axis=1)
    for block in range(0, blocks, 2):
        both = jnp.dot(
            emb_ref[block * width : (block + 2) * width, :],
            weights,
            preferred_element_type=F32,
        ).astype(BF16).astype(F32)
        for k in range(2):
            left = both[k * width : (k + 1) * width, :width]
            at = (block + k) * pairs
            left_ref[at : at + pairs, :width] = left[:pairs]
            left_ref[at : at + pairs, width:] = left[pairs:]
        full_ref[block * width : (block + 2) * width, :] = both[:, width:]
    own = blocks * step
    for block in range(blocks):
        at = pl.multiple_of(block * width + tile * step, step)
        right_all[block * step : (block + 1) * step, :] = full_ref[pl.ds(at, step), :]
    right_next = jnp.dot(next_ref[...], right_w_ref[...], preferred_element_type=F32)
    right_all[own:, :] = right_next.astype(BF16).astype(F32)
    rows = [target_ref[chip, : 2 * slots * step, :].astype(F32) for chip in range(chips)]
    rows = jnp.concatenate(rows, axis=0)
    for group in range(groups):
        target_all[group] = rows[group * width : (group + 1) * width].T
    target_all[groups] = jnp.zeros((width, width), F32)
    for ref in (pred_all, row_all, col_all, outer_all, bias_all, first_1, slope_1):
        ref[...] = jnp.zeros_like(ref)
    lane = lax.broadcasted_iota(jnp.int32, (width, width), 1)
    ones = jnp.ones((16, BATCH * step * pairs), BF16)

    copy.wait()
    count = jnp.int32(0)
    for share in range(shares):
        for slot in range(slots):
            offset = lists[2, share, slot]
            table[0, count] = lists[0, share, slot] & (blocks - 1)
            table[1, count] = offset
            table[2, count] = share * slots + slot
            count = count + jnp.where(offset >= 0, 1, 0)
    for spare in range(2 * BATCH):
        table[0, count + spare] = 0
        table[1, count + spare] = 0
        table[2, count + spare] = shares * slots

    def forward(turn, first_ref, slope_ref):
        pre = []
        wanted = []
        shifts = []
        floors = []
        for k in range(BATCH):
            job = turn * BATCH + k
            block, offset, slot = table[0, job], table[1, job], table[2, job]
            shift = (slot & (width // step - 1)) * step
            shifts.append((slot >> spread_bits, shift))
            at = pl.multiple_of(block * pairs, pairs)
            col_at = pl.multiple_of((block + offset) * step, step)
            right = right_all[pl.ds(col_at, step), :] + const_ref[pl.ds(offset, 1), :]
            right = jnp.concatenate([right, right], axis=1)
            left = left_ref[pl.ds(at, pairs), :]
            pre += [left + right[j : j + 1, :] for j in range(step)]
            target = pltpu.roll(
                target_all[slot >> spread_bits], (width - shift) & (width - 1), 1
            ).astype(BF16)
            for j in range(step):
                want = jnp.broadcast_to(target[:, j : j + 1], (width, width)).astype(F32)
                wanted.append(jnp.concatenate([want[:pairs], want[pairs:]], axis=1))
            floor = jnp.where(job < count, b_two[...], jnp.full((1, 2 * width), NEVER, F32))
            floors.append(jnp.broadcast_to(floor, (step * pairs, 2 * width)))
        first = jnp.maximum(jnp.concatenate(pre, axis=0), 0.0).astype(BF16)
        first_ref[...] = first
        act = jnp.dot(first, w_two[...], preferred_element_type=F32)
        act = act + jnp.concatenate(floors, axis=0)
        second = (jnp.maximum(act, 0.0) * scale_two[...]).astype(BF16)
        contact = jnp.dot(second, out_two[...], preferred_element_type=F32)
        slope = (contact - jnp.concatenate(wanted, axis=0)) * scale_two[...]
        slope = slope.astype(BF16)
        slope_ref[...] = jnp.where(second > 0, slope, jnp.zeros_like(slope))
        for k, (group, shift) in enumerate(shifts):
            found = jnp.zeros((width, width), F32)
            for j in range(step):
                here = contact[(k * step + j) * pairs : (k * step + j + 1) * pairs]
                here = jnp.concatenate([here[:, :width], here[:, width:]], axis=0)
                found = jnp.where(lane == j, here, found)
            mine = (lane >= shift) & (lane < shift + step)
            pred_all[group] = jnp.where(mine, pltpu.roll(found, shift, 1), pred_all[group])

    def backward(turn, first_ref, slope_ref):
        first = first_ref[...]
        slope = slope_ref[...]
        back = jnp.dot(slope, back_two[...], preferred_element_type=F32)
        back = jnp.where(first.astype(F32) > 0.0, back, 0.0)
        for k in range(BATCH):
            job = turn * BATCH + k
            block, offset = table[0, job], table[1, job]
            at = pl.multiple_of(block * pairs, pairs)
            rows = jnp.zeros((pairs, 2 * width), F32)
            cols = []
            for j in range(step):
                here = back[(k * step + j) * pairs : (k * step + j + 1) * pairs]
                rows = rows + here
                col = jnp.sum(here, axis=0, keepdims=True)
                cols.append(col[:, :width] + col[:, width:])
            row_all[pl.ds(at, pairs), :] += rows
            cols = jnp.concatenate(cols, axis=0)
            col_at = pl.multiple_of((block + offset) * step, step)
            col_all[pl.ds(col_at, step), :] += cols
            bias_all[pl.ds(offset, 1), :] += jnp.sum(cols, axis=0, keepdims=True)
        lhs = jnp.concatenate([first.T, ones], axis=0)
        outer_all[...] += jnp.dot(lhs, slope, preferred_element_type=F32)

    def body(pass_at, _):
        turn = 2 * pass_at
        backward(jnp.maximum(turn - 1, 0), first_1, slope_1)
        forward(turn, first_0, slope_0)
        backward(turn, first_0, slope_0)
        forward(turn + 1, first_1, slope_1)
        return 0

    passes = lax.div(count + 2 * BATCH - 1, 2 * BATCH)
    lax.fori_loop(0, passes, body, 0)
    backward(jnp.maximum(2 * passes - 1, 0), first_1, slope_1)

    flat = [(pred_all[group] * float(width)).T for group in range(groups)]
    flat = jnp.concatenate(flat, axis=0).astype(BF16)
    for chip in range(chips):
        pred_ref[chip] = flat[chip * 2 * slots * step : (chip + 1) * 2 * slots * step]
    outer = outer_all[:width, :width] + outer_all[width : 2 * width, width:]
    sum_d = outer_all[2 * width : 2 * width + 1, :width] + outer_all[2 * width : 2 * width + 1, width:]
    bias = bias_all[...]
    line = lax.broadcasted_iota(jnp.int32, bias.shape, 0)
    sum_out = (jnp.sum(w * outer, axis=0, keepdims=True) + b_pair * sum_d) / ratio
    vectors = jnp.where(line == 5, sum_d * power, bias)
    vectors = jnp.where(line == 6, sum_out, vectors)
    outer = outer * power
    high = vectors.astype(BF16).astype(F32)
    rest = (high, vectors - high)
    col = col_all[...].astype(BF16)
    rows = []
    for block in range(blocks):
        here = row_all[block * pairs : (block + 1) * pairs, :].astype(BF16)
        rows += [here[:, :width], here[:, width:]]
    embs = [cols_ref[...], next_ref[...]]
    contract = (((0,), (0,)), ((), ()))
    grads = (
        lax.dot_general(
            jnp.concatenate(rows, axis=0), emb_ref[...], contract, preferred_element_type=F32
        ).astype(BF16),
        lax.dot_general(
            col, jnp.concatenate(embs, axis=0), contract, preferred_element_type=F32
        ).astype(BF16),
    )
    def message(share):
        side, at = share // chips, share % chips
        grad = grads[side][:, at // 2 * width : (at // 2 + 1) * width]
        more = rest[share] if share < 2 else jnp.zeros_like(high)
        small = jnp.concatenate([outer[8 * share : 8 * share + 8], more], axis=0)
        return jnp.concatenate(
            [rows[share], grad[at % 2 * pairs : (at % 2 + 1) * pairs], small.astype(BF16)], axis=0
        )

    for chip in range(chips):
        even, odd = message(2 * chip), message(2 * chip + 1)
        keep_ref[chip] = jnp.where(core == 0, even, odd)
        send_ref[chip] = jnp.where(core == 0, odd, even)
    col_ref[...] = col_all[:own]
    edge_ref[...] = col[own:]


def share_kernel(sum_ref, edge_ref, row_ref, message_ref, mine_ref, send_ref):
    core = place() & 1
    chips, _, width = sum_ref.shape
    pairs = width // 2
    head = width + 16
    slot_rows = mine_ref.shape[1]
    total = jnp.zeros((head, width), F32)
    for chip in range(chips):
        total = total + sum_ref[chip, :head, :].astype(F32)
        first = sum_ref[chip, head : head + slot_rows, :]
        second = sum_ref[chip, head + slot_rows :, :]
        mine_ref[chip] = jnp.where(core == 0, first, second)
        send_ref[chip] = jnp.where(core == 0, second, first)
    total = total.astype(BF16)
    row_ref[...] = total[:pairs]
    for bin_at in range(message_ref.shape[0]):
        message_ref[bin_at, : head - pairs, :] = total[pairs:]
        message_ref[bin_at, head - pairs :, :] = edge_ref[...]


def total_kernel(met_ref, row_ref, col_ref, message_ref):
    here = lax.axis_index("bin")
    bins = met_ref.shape[0]
    width = row_ref.shape[1]
    pairs = row_ref.shape[0]
    edge = col_ref.shape[0] // 2
    count = met_ref.shape[1] - edge
    total = jnp.zeros((count, width), F32)
    before = jnp.zeros((edge, width), F32)
    for bin_at in range(bins):
        total = total + met_ref[bin_at, :count, :].astype(F32)
        near = met_ref[bin_at, count:, :].astype(F32)
        before = jnp.where(here == bin_at + 1, near, before)
    total = total.astype(BF16)
    col = col_ref[...]
    top = (col[:edge] + before).astype(BF16)
    low = col[edge:].astype(BF16)
    for chip in range(message_ref.shape[0]):
        message_ref[chip, :pairs, :] = row_ref[...]
        message_ref[chip, pairs : pairs + count, :] = total
        message_ref[chip, pairs + count : pairs + count + edge, :] = top
        message_ref[chip, pairs + count + edge :, :] = low


def last_kernel(
    mine_ref, other_ref, pred_mine, pred_other, left_w_ref, right_w_ref,
    pred_hbm, emb_hbm, left_hbm, right_hbm, bias_hbm, w_hbm, b_hbm, out_hbm,
    pred_ref, emb_ref, left_ref, right_ref, bias_ref, w_ref, b_ref, out_ref,
    both_ref, flat_ref, col_ref, flip_ref, sems,
):
    core = place() & 1
    width = left_w_ref.shape[1]
    pairs = width // 2
    chips = mine_ref.shape[0]
    slots = pred_ref.shape[0]
    step = width // (2 * chips)
    copies = []

    def leave(source, target):
        copies.append(pltpu.make_async_copy(source, target, sems.at[len(copies)]))
        copies[-1].start()

    lows = []
    for share in range(2 * chips):
        block = jnp.where(core == share % 2, mine_ref[share // 2], other_ref[share // 2])
        both_ref[share * pairs : (share + 1) * pairs, :width] = block[:pairs]
        block = block.astype(F32)
        for k in range(col_ref.shape[0] // width):
            to = k * width + share * step
            at = width + 16 + k * step
            col_ref[to : to + step, :] = block[at : at + step]
        flat_ref[share * pairs : (share + 1) * pairs, :] = block[pairs:width]
        small = block[width : width + 16]
        w_ref[8 * share : 8 * share + 8, :] = small[:8]
        lows.append(small[8:])
    both_ref[:, width:] = col_ref[...].astype(BF16)
    weights = jnp.concatenate([left_w_ref[...], right_w_ref[...]], axis=1)
    part = 2 * width
    for k in range(both_ref.shape[0] // part):
        rows = pl.ds(k * part, part)
        emb_ref[rows, :] = lax.dot_general(
            both_ref[rows, :], weights, (((1,), (1,)), ((), ())), preferred_element_type=F32
        ).astype(BF16)
        leave(emb_ref.at[rows, :], emb_hbm.at[rows, :])
    for side, (grad_ref, grad_hbm) in enumerate(((left_ref, left_hbm), (right_ref, right_hbm))):
        for k in range(chips // 2):
            at = (side * chips // 2 + k) * width
            grad_ref[k * width : (k + 1) * width, :] = flat_ref[at : at + width, :].T
        leave(grad_ref, grad_hbm)
    vectors = lows[0] + lows[1]
    bias_ref[...] = vectors[:5]
    b_ref[...] = vectors[5:6]
    out_ref[...] = vectors[6:7]
    for source, target in ((w_ref, w_hbm), (bias_ref, bias_hbm), (b_ref, b_hbm), (out_ref, out_hbm)):
        leave(source, target)
    for chip in range(chips):
        for ref, side in ((pred_mine, core), (pred_other, 1 - core)):
            block = ref[chip].astype(F32)
            to = pl.multiple_of((2 * chip + side) * step, step)
            for slot in range(slots):
                flip_ref[slot, pl.ds(to, step), :] = block[slot * step : (slot + 1) * step]
    for slot in range(slots):
        pred_ref[slot] = flip_ref[slot].T.astype(BF16)
    leave(pred_ref, pred_hbm)
    for copy in copies:
        copy.wait()


def shape(*dims, dtype=F32):
    return jax.ShapeDtypeStruct(dims, dtype)


def call(kernel, outs, scratch, *args, space=None, out_space=VMEM, limit=32):
    return pl.pallas_call(
        kernel,
        out_shape=outs,
        in_specs=space or [VMEM] * len(args),
        out_specs=(out_space,) * len(outs),
        scratch_shapes=scratch,
        compiler_params=pltpu.CompilerParams(vmem_limit_bytes=limit * 1024 * 1024),
    )(*args)


def swapped(block, axis, bits):
    return lax.ppermute(block, axis, [(i, i ^ bits) for i in range(lax.axis_size(axis))])


def across(block, axis, groups=None):
    return lax.all_to_all(block, axis, 0, 0, axis_index_groups=groups, tiled=True)


def per_device(embeddings, w_left, w_right, pair_bias, w_pair, b_pair, w_out, tile_list, target):
    tile = place()
    core = lax.rem(tile, 2)
    slots, width = target.shape[2:4]
    rows, features = embeddings.shape
    blocks = rows // width
    pairs = width // 2
    shares = lax.axis_size("tile")
    chips = shares // 2
    step = width // shares
    part = rows // shares
    edge = part // 2
    target = target[0, 0]
    lists = jnp.transpose(tile_list, (0, 3, 1, 2)).reshape(3, 1, slots)

    emb_cols = lax.dynamic_slice_in_dim(
        embeddings.reshape(blocks, shares, step, features), tile, 1, 1
    ).reshape(part, features)
    target_other = swapped(target, "tile", 1)
    lists_other = swapped(lists, "tile", 1)
    bins = lax.axis_size("bin")
    emb_next = lax.ppermute(emb_cols[:edge], "bin", [(k + 1, k) for k in range(bins - 1)])
    consts = jnp.concatenate(
        [pair_bias, b_pair[None], w_out[None], jnp.zeros((1, width), F32)], axis=0
    )
    (target_send,) = call(
        split_kernel,
        (shape(chips, 2 * (slots + 1) * step, width, dtype=BF16),),
        [pltpu.VMEM((2 * slots, width, width), F32), pltpu.VMEM((2 * step, width), F32)],
        lists, lists_other, target, target_other,
    )
    groups = [list(range(k, shares, 2)) for k in range(2)]
    target_all = across(target_send, "tile", groups)

    chunk = (BATCH * step * pairs, 2 * width)
    grouped = (slots * shares * step // width + 1, width, width)
    half = shape(chips, width + 16, width, dtype=BF16)
    sums, sums_send, pred, col, col_edge = call(
        pair_kernel,
        (
            half,
            half,
            shape(chips, 2 * slots * step, width, dtype=BF16),
            shape(part, width),
            shape(edge, width, dtype=BF16),
        ),
        [
            pltpu.SMEM((3, slots * shares + 2 * BATCH), jnp.int32),
            pltpu.SMEM((3, shares, width), jnp.int32),
            pltpu.SemaphoreType.DMA,
            pltpu.VMEM((3, shares, width), jnp.int32),
            pltpu.VMEM((rows // 2, 2 * width), F32),
            pltpu.VMEM((rows, width), F32),
            pltpu.VMEM((part + edge, width), F32),
            pltpu.VMEM(grouped, F32),
            pltpu.VMEM(grouped, F32),
            pltpu.VMEM((rows // 2, 2 * width), F32),
            pltpu.VMEM((part + edge, width), F32),
            pltpu.VMEM((2 * width + 16, 2 * width), F32),
            pltpu.VMEM((8, width), F32),
            pltpu.VMEM((2 * width, 2 * width), BF16),
            pltpu.VMEM((2 * width, 2 * width), BF16),
            pltpu.VMEM((2 * width, 2 * width), BF16),
            pltpu.VMEM((1, 2 * width), F32),
            pltpu.VMEM((1, 2 * width), F32),
            pltpu.VMEM(chunk, BF16),
            pltpu.VMEM(chunk, BF16),
            pltpu.VMEM(chunk, BF16),
            pltpu.VMEM(chunk, BF16),
        ],
        embeddings, emb_cols, emb_next, w_left, w_right, consts, target_all, w_pair,
    )
    sums = (sums.astype(F32) + swapped(sums_send, "tile", 1).astype(F32)).astype(BF16)
    sums = across(jnp.concatenate([sums, pred], axis=1), "tile", groups)
    row, weight, pred_mine, pred_send = call(
        share_kernel,
        (
            shape(pairs, width, dtype=BF16),
            shape(bins, pairs + 16 + edge, width, dtype=BF16),
            shape(chips, slots * step, width, dtype=BF16),
            shape(chips, slots * step, width, dtype=BF16),
        ),
        [], sums, col_edge,
    )
    weight = across(weight, "bin")
    (mine,) = call(
        total_kernel,
        (shape(chips, width + 16 + part, width, dtype=BF16),),
        [], weight, row, col,
    )
    mine = across(mine, "tile", groups)
    mine, pred_send = lax.optimization_barrier((mine, pred_send))
    pred_other = swapped(pred_send, "tile", 1)
    other = swapped(mine, "tile", 1)
    outs = (
        shape(slots, width, width, dtype=BF16),
        shape(rows, features, dtype=BF16),
        shape(features, width),
        shape(features, width),
        shape(5, width),
        shape(width, width),
        shape(1, width),
        shape(1, width),
    )
    outs = call(
        last_kernel,
        outs,
        [pltpu.VMEM(out.shape, out.dtype) for out in outs]
        + [
            pltpu.VMEM((rows, 2 * width), BF16),
            pltpu.VMEM((2 * features, width), F32),
            pltpu.VMEM((rows, width), F32),
            pltpu.VMEM((slots, width, width), F32),
            pltpu.SemaphoreType.DMA((rows // (2 * width) + 7,)),
        ],
        mine, other, pred_mine, pred_other, w_left, w_right, out_space=HBM,
    )
    return (outs[0][None, None], *outs[1:6], outs[6][0], outs[7][0])


def solution(mesh):
    return jax.shard_map(
        per_device,
        mesh=mesh,
        in_specs=(
            P("bin", None),
            P(),
            P(),
            P(),
            P(),
            P(),
            P(),
            P("bin", "tile", None, None),
            P("bin", "tile", None, None, None),
        ),
        out_specs=(
            P("bin", "tile", None, None, None),
            P("bin", None),
            P(),
            P(),
            P(),
            P(),
            P(),
            P(),
        ),
        check_vma=False,
    )
```

```python
import jax
import jax.numpy as jnp
from jax import lax
from jax.experimental import pallas as pl
from jax.experimental.pallas import tpu as pltpu
from jax.sharding import PartitionSpec as P

F32 = jnp.float32
BF16 = jnp.bfloat16
BATCH = 2
NEVER = -1e38
TINY = 1e-30
VMEM = pl.BlockSpec(memory_space=pltpu.VMEM)
HBM = pl.BlockSpec(memory_space=pl.ANY)


def place():
    return lax.axis_index("tile")


def split_kernel(
    list_mine, list_other, target_mine, target_other, send_ref, flip_ref, listed_ref
):
    core = place() & 1
    slots, width, _ = target_mine.shape
    chips = send_ref.shape[0]
    step = width // (2 * chips)
    listed_ref[...] = jnp.zeros_like(listed_ref)
    for side in range(2):
        mine = core == side
        for k in range(3):
            listed_ref[3 * side + k : 3 * side + k + 1, :slots] = jnp.where(
                mine, list_mine[k], list_other[k]
            ).astype(F32)
        for slot in range(slots):
            block = jnp.where(mine, target_mine[slot], target_other[slot]).astype(F32)
            flip_ref[side * slots + slot] = (block * (1.0 / width)).T
    listed = listed_ref[...].astype(BF16)
    for chip in range(chips):
        for side in range(2):
            at = (2 * chip + core) * step
            at = pl.multiple_of(at, step)
            pieces = [
                flip_ref[side * slots + slot, pl.ds(at, step), :] for slot in range(slots)
            ]
            send_ref[chip, side * slots * step : (side + 1) * slots * step, :] = jnp.concatenate(
                pieces, axis=0
            ).astype(BF16)
        send_ref[chip, 2 * slots * step :, :] = listed


def pair_kernel(
    emb_ref, cols_ref, next_ref, left_w_ref, right_w_ref, const_ref, target_ref, w_ref,
    keep_ref, send_ref, pred_ref, col_ref, edge_ref,
    table, lists, list_sem, list_all, left_ref, full_ref, right_all, target_all, pred_all, row_all, col_all,
    outer_all, bias_all, w_two, out_two, back_two, b_two, scale_two, first_0, first_1, slope_0, slope_1,
):
    tile = place()
    width = w_ref.shape[0]
    pairs = width // 2
    blocks = emb_ref.shape[0] // width
    chips = target_ref.shape[0]
    shares = 2 * chips
    step = width // shares
    slots = target_ref.shape[1] // (2 * step) - 1
    core = tile & 1
    groups = target_all.shape[0] - 1
    spread_bits = (width // step).bit_length() - 1

    for chip in range(chips):
        rows = target_ref[chip, 2 * slots * step :, :].astype(F32).astype(jnp.int32)
        for side in range(2):
            for k in range(3):
                at = 3 * side + k
                list_all[k, 2 * chip + side : 2 * chip + side + 1] = rows[at : at + 1]
    copy = pltpu.make_async_copy(list_all, lists, list_sem)
    copy.start()

    w = w_ref[...].astype(F32)
    w_out = const_ref[6:7, :]
    b_pair = const_ref[5:6, :]
    size = jnp.abs(w_out)
    power = jnp.exp2(jnp.floor(jnp.log2(jnp.maximum(size, TINY))))
    power = jnp.where(size < TINY, 0.0, power).astype(BF16).astype(F32)
    power = jnp.where(w_out < 0.0, -power, power)
    ratio = jnp.where(size < TINY, 1.0, w_out / jnp.where(size < TINY, 1.0, power))
    back = (w * w_out).T.astype(BF16)
    spread = jnp.broadcast_to(power * (1.0 / width), (width, width)).T.astype(BF16)
    for ref, block in ((w_two, w_ref[...]), (out_two, spread), (back_two, back)):
        ref[...] = jnp.zeros_like(ref)
        ref[:width, :width] = block
        ref[width:, width:] = block
    scale_two[:, :width] = ratio
    scale_two[:, width:] = ratio
    b_two[:, :width] = b_pair
    b_two[:, width:] = b_pair
    weights = jnp.concatenate([left_w_ref[...], right_w_ref[...]], axis=1)
    for block in range(0, blocks, 2):
        both = jnp.dot(
            emb_ref[block * width : (block + 2) * width, :],
            weights,
            preferred_element_type=F32,
        ).astype(BF16).astype(F32)
        for k in range(2):
            left = both[k * width : (k + 1) * width, :width]
            at = (block + k) * pairs
            left_ref[at : at + pairs, :width] = left[:pairs]
            left_ref[at : at + pairs, width:] = left[pairs:]
        full_ref[block * width : (block + 2) * width, :] = both[:, width:]
    own = blocks * step
    for block in range(blocks):
        at = pl.multiple_of(block * width + tile * step, step)
        right_all[block * step : (block + 1) * step, :] = full_ref[pl.ds(at, step), :]
    right_next = jnp.dot(next_ref[...], right_w_ref[...], preferred_element_type=F32)
    right_all[own:, :] = right_next.astype(BF16).astype(F32)
    rows = [target_ref[chip, : 2 * slots * step, :].astype(F32) for chip in range(chips)]
    rows = jnp.concatenate(rows, axis=0)
    for group in range(groups):
        target_all[group] = rows[group * width : (group + 1) * width].T
    target_all[groups] = jnp.zeros((width, width), F32)
    for ref in (pred_all, row_all, col_all, outer_all, bias_all, first_1, slope_1):
        ref[...] = jnp.zeros_like(ref)
    lane = lax.broadcasted_iota(jnp.int32, (width, width), 1)
    ones = jnp.ones((16, BATCH * step * pairs), BF16)

    copy.wait()
    count = jnp.int32(0)
    for share in range(shares):
        for slot in range(slots):
            offset = lists[2, share, slot]
            table[0, count] = lists[0, share, slot] & (blocks - 1)
            table[1, count] = offset
            table[2, count] = share * slots + slot
            count = count + jnp.where(offset >= 0, 1, 0)
    for spare in range(2 * BATCH):
        table[0, count + spare] = 0
        table[1, count + spare] = 0
        table[2, count + spare] = shares * slots

    def forward(turn, first_ref, slope_ref):
        pre = []
        wanted = []
        shifts = []
        floors = []
        for k in range(BATCH):
            job = turn * BATCH + k
            block, offset, slot = table[0, job], table[1, job], table[2, job]
            shift = (slot & (width // step - 1)) * step
            shifts.append((slot >> spread_bits, shift))
            at = pl.multiple_of(block * pairs, pairs)
            col_at = pl.multiple_of((block + offset) * step, step)
            right = right_all[pl.ds(col_at, step), :] + const_ref[pl.ds(offset, 1), :]
            right = jnp.concatenate([right, right], axis=1)
            left = left_ref[pl.ds(at, pairs), :]
            pre += [left + right[j : j + 1, :] for j in range(step)]
            target = pltpu.roll(
                target_all[slot >> spread_bits], (width - shift) & (width - 1), 1
            )
            for j in range(step):
                want = jnp.broadcast_to(target[:, j : j + 1], (width, width))
                wanted.append(jnp.concatenate([want[:pairs], want[pairs:]], axis=1))
            floor = jnp.where(job < count, b_two[...], jnp.full((1, 2 * width), NEVER, F32))
            floors.append(jnp.broadcast_to(floor, (step * pairs, 2 * width)))
        first = jnp.maximum(jnp.concatenate(pre, axis=0).astype(BF16), 0.0)
        first_ref[...] = first
        act = jnp.dot(first, w_two[...], preferred_element_type=F32)
        act = act + jnp.concatenate(floors, axis=0)
        second = jnp.maximum((act * scale_two[...]).astype(BF16), 0.0)
        contact = jnp.dot(second, out_two[...], preferred_element_type=F32)
        slope = (contact - jnp.concatenate(wanted, axis=0)).astype(BF16)
        slope_ref[...] = jnp.where(second > 0, slope, jnp.zeros_like(slope))
        for k, (group, shift) in enumerate(shifts):
            found = jnp.zeros((width, width), F32)
            for j in range(step):
                here = contact[(k * step + j) * pairs : (k * step + j + 1) * pairs]
                here = jnp.concatenate([here[:, :width], here[:, width:]], axis=0)
                found = jnp.where(lane == j, here, found)
            mine = (lane >= shift) & (lane < shift + step)
            pred_all[group] = jnp.where(mine, pltpu.roll(found, shift, 1), pred_all[group])

    def backward(turn, first_ref, slope_ref):
        first = first_ref[...]
        slope = slope_ref[...]
        back = jnp.dot(slope, back_two[...], preferred_element_type=F32)
        back = jnp.where(first.astype(F32) > 0.0, back, 0.0)
        for k in range(BATCH):
            job = turn * BATCH + k
            block, offset = table[0, job], table[1, job]
            at = pl.multiple_of(block * pairs, pairs)
            rows = jnp.zeros((pairs, 2 * width), F32)
            cols = []
            for j in range(step):
                here = back[(k * step + j) * pairs : (k * step + j + 1) * pairs]
                rows = rows + here
                cols.append(sum(here[g : g + 8] for g in range(0, pairs, 8)))
            row_all[pl.ds(at, pairs), :] += rows
            col_at = pl.multiple_of((block + offset) * (8 * step), 8 * step)
            col_all[pl.ds(col_at, 8 * step), :] += jnp.concatenate(cols, axis=0)
            bias_all[pl.ds(pl.multiple_of(offset * 8, 8), 8), :] += sum(cols)
        lhs = jnp.concatenate([first.T, ones], axis=0)
        outer_all[...] += jnp.dot(lhs, slope, preferred_element_type=F32)

    def body(pass_at, _):
        turn = 2 * pass_at
        backward(jnp.maximum(turn - 1, 0), first_1, slope_1)
        forward(turn, first_0, slope_0)
        backward(turn, first_0, slope_0)
        forward(turn + 1, first_1, slope_1)
        return 0

    passes = lax.div(count + 2 * BATCH - 1, 2 * BATCH)
    lax.fori_loop(0, passes, body, 0)
    backward(jnp.maximum(2 * passes - 1, 0), first_1, slope_1)

    flat = [(pred_all[group] * float(width)).T for group in range(groups)]
    flat = jnp.concatenate(flat, axis=0).astype(BF16)
    for chip in range(chips):
        pred_ref[chip] = flat[chip * 2 * slots * step : (chip + 1) * 2 * slots * step]
    def folded(ref, count):
        sums = [
            jnp.sum(ref[8 * k : 8 * k + 8, :], axis=0, keepdims=True) for k in range(count)
        ]
        sums = jnp.concatenate(sums, axis=0)
        return sums[:, :width] + sums[:, width:]

    col = folded(col_all, col_all.shape[0] // 8)
    bias = folded(bias_all, 8)
    outer = outer_all[:width, :width] + outer_all[width : 2 * width, width:]
    sum_d = outer_all[2 * width : 2 * width + 1, :width] + outer_all[2 * width : 2 * width + 1, width:]
    line = lax.broadcasted_iota(jnp.int32, bias.shape, 0)
    sum_out = jnp.sum(w * outer, axis=0, keepdims=True) + b_pair * sum_d
    vectors = jnp.where(line == 5, sum_d * w_out, bias)
    vectors = jnp.where(line == 6, sum_out, vectors)
    outer = outer * w_out
    high = vectors.astype(BF16).astype(F32)
    rest = (high, vectors - high)
    col_low = col.astype(BF16)
    rows = []
    for block in range(blocks):
        here = row_all[block * pairs : (block + 1) * pairs, :].astype(BF16)
        rows += [here[:, :width], here[:, width:]]
    embs = [cols_ref[...], next_ref[...]]
    contract = (((0,), (0,)), ((), ()))
    grads = (
        lax.dot_general(
            jnp.concatenate(rows, axis=0), emb_ref[...], contract, preferred_element_type=F32
        ).astype(BF16),
        lax.dot_general(
            col_low, jnp.concatenate(embs, axis=0), contract, preferred_element_type=F32
        ).astype(BF16),
    )
    def message(share):
        side, at = share // chips, share % chips
        grad = grads[side][:, at // 2 * width : (at // 2 + 1) * width]
        more = rest[share] if share < 2 else jnp.zeros_like(high)
        small = jnp.concatenate([outer[8 * share : 8 * share + 8], more], axis=0)
        return jnp.concatenate(
            [rows[share], grad[at % 2 * pairs : (at % 2 + 1) * pairs], small.astype(BF16)], axis=0
        )

    for chip in range(chips):
        even, odd = message(2 * chip), message(2 * chip + 1)
        keep_ref[chip] = jnp.where(core == 0, even, odd)
        send_ref[chip] = jnp.where(core == 0, odd, even)
    col_ref[...] = col[:own]
    edge_ref[...] = col_low[own:]


def share_kernel(sum_ref, edge_ref, row_ref, message_ref, mine_ref, send_ref):
    core = place() & 1
    chips, _, width = sum_ref.shape
    pairs = width // 2
    head = width + 16
    slot_rows = mine_ref.shape[1]
    total = jnp.zeros((head, width), F32)
    for chip in range(chips):
        total = total + sum_ref[chip, :head, :].astype(F32)
        first = sum_ref[chip, head : head + slot_rows, :]
        second = sum_ref[chip, head + slot_rows :, :]
        mine_ref[chip] = jnp.where(core == 0, first, second)
        send_ref[chip] = jnp.where(core == 0, second, first)
    total = total.astype(BF16)
    row_ref[...] = total[:pairs]
    for bin_at in range(message_ref.shape[0]):
        message_ref[bin_at, : head - pairs, :] = total[pairs:]
        message_ref[bin_at, head - pairs :, :] = edge_ref[...]


def total_kernel(met_ref, row_ref, col_ref, message_ref):
    here = lax.axis_index("bin")
    bins = met_ref.shape[0]
    width = row_ref.shape[1]
    pairs = row_ref.shape[0]
    edge = col_ref.shape[0] // 2
    count = met_ref.shape[1] - edge
    total = jnp.zeros((count, width), F32)
    before = jnp.zeros((edge, width), F32)
    for bin_at in range(bins):
        total = total + met_ref[bin_at, :count, :].astype(F32)
        near = met_ref[bin_at, count:, :].astype(F32)
        before = jnp.where(here == bin_at + 1, near, before)
    total = total.astype(BF16)
    col = col_ref[...]
    top = (col[:edge] + before).astype(BF16)
    low = col[edge:].astype(BF16)
    for chip in range(message_ref.shape[0]):
        message_ref[chip, :pairs, :] = row_ref[...]
        message_ref[chip, pairs : pairs + count, :] = total
        message_ref[chip, pairs + count : pairs + count + edge, :] = top
        message_ref[chip, pairs + count + edge :, :] = low


def last_kernel(
    mine_ref, other_ref, pred_mine, pred_other, left_w_ref, right_w_ref,
    pred_hbm, emb_hbm, left_hbm, right_hbm, bias_hbm, w_hbm, b_hbm, out_hbm,
    pred_ref, emb_ref, left_ref, right_ref, bias_ref, w_ref, b_ref, out_ref,
    both_ref, flat_ref, col_ref, flip_ref, sems,
):
    core = place() & 1
    width = left_w_ref.shape[1]
    pairs = width // 2
    chips = mine_ref.shape[0]
    slots = pred_ref.shape[0]
    step = width // (2 * chips)
    copies = []

    def leave(source, target):
        copies.append(pltpu.make_async_copy(source, target, sems.at[len(copies)]))
        copies[-1].start()

    lows = []
    for share in range(2 * chips):
        block = jnp.where(core == share % 2, mine_ref[share // 2], other_ref[share // 2])
        both_ref[share * pairs : (share + 1) * pairs, :width] = block[:pairs]
        block = block.astype(F32)
        for k in range(col_ref.shape[0] // width):
            to = k * width + share * step
            at = width + 16 + k * step
            col_ref[to : to + step, :] = block[at : at + step]
        flat_ref[share * pairs : (share + 1) * pairs, :] = block[pairs:width]
        small = block[width : width + 16]
        w_ref[8 * share : 8 * share + 8, :] = small[:8]
        lows.append(small[8:])
    both_ref[:, width:] = col_ref[...].astype(BF16)
    weights = jnp.concatenate([left_w_ref[...], right_w_ref[...]], axis=1)
    part = 2 * width
    for k in range(both_ref.shape[0] // part):
        rows = pl.ds(k * part, part)
        emb_ref[rows, :] = lax.dot_general(
            both_ref[rows, :], weights, (((1,), (1,)), ((), ())), preferred_element_type=F32
        ).astype(BF16)
        leave(emb_ref.at[rows, :], emb_hbm.at[rows, :])
    for side, (grad_ref, grad_hbm) in enumerate(((left_ref, left_hbm), (right_ref, right_hbm))):
        for k in range(chips // 2):
            at = (side * chips // 2 + k) * width
            grad_ref[k * width : (k + 1) * width, :] = flat_ref[at : at + width, :].T
        leave(grad_ref, grad_hbm)
    vectors = lows[0] + lows[1]
    bias_ref[...] = vectors[:5]
    b_ref[...] = vectors[5:6]
    out_ref[...] = vectors[6:7]
    for source, target in ((w_ref, w_hbm), (bias_ref, bias_hbm), (b_ref, b_hbm), (out_ref, out_hbm)):
        leave(source, target)
    for chip in range(chips):
        for ref, side in ((pred_mine, core), (pred_other, 1 - core)):
            block = ref[chip].astype(F32)
            to = pl.multiple_of((2 * chip + side) * step, step)
            for slot in range(slots):
                flip_ref[slot, pl.ds(to, step), :] = block[slot * step : (slot + 1) * step]
    for slot in range(slots):
        pred_ref[slot] = flip_ref[slot].T.astype(BF16)
    leave(pred_ref, pred_hbm)
    for copy in copies:
        copy.wait()


def shape(*dims, dtype=F32):
    return jax.ShapeDtypeStruct(dims, dtype)


def call(kernel, outs, scratch, *args, space=None, out_space=VMEM, limit=32):
    return pl.pallas_call(
        kernel,
        out_shape=outs,
        in_specs=space or [VMEM] * len(args),
        out_specs=(out_space,) * len(outs),
        scratch_shapes=scratch,
        compiler_params=pltpu.CompilerParams(vmem_limit_bytes=limit * 1024 * 1024),
    )(*args)


def swapped(block, axis, bits):
    return lax.ppermute(block, axis, [(i, i ^ bits) for i in range(lax.axis_size(axis))])


def across(block, axis, groups=None):
    return lax.all_to_all(block, axis, 0, 0, axis_index_groups=groups, tiled=True)


def per_device(embeddings, w_left, w_right, pair_bias, w_pair, b_pair, w_out, tile_list, target):
    tile = place()
    core = lax.rem(tile, 2)
    slots, width = target.shape[2:4]
    rows, features = embeddings.shape
    blocks = rows // width
    pairs = width // 2
    shares = lax.axis_size("tile")
    chips = shares // 2
    step = width // shares
    part = rows // shares
    edge = part // 2
    target = target[0, 0]
    lists = jnp.transpose(tile_list, (0, 3, 1, 2)).reshape(3, 1, slots)

    emb_cols = lax.dynamic_slice_in_dim(
        embeddings.reshape(blocks, shares, step, features), tile, 1, 1
    ).reshape(part, features)
    target_other = swapped(target, "tile", 1)
    lists_other = swapped(lists, "tile", 1)
    bins = lax.axis_size("bin")
    emb_next = lax.ppermute(emb_cols[:edge], "bin", [(k + 1, k) for k in range(bins - 1)])
    consts = jnp.concatenate(
        [pair_bias, b_pair[None], w_out[None], jnp.zeros((1, width), F32)], axis=0
    )
    (target_send,) = call(
        split_kernel,
        (shape(chips, 2 * (slots + 1) * step, width, dtype=BF16),),
        [pltpu.VMEM((2 * slots, width, width), F32), pltpu.VMEM((2 * step, width), F32)],
        lists, lists_other, target, target_other,
    )
    groups = [list(range(k, shares, 2)) for k in range(2)]
    target_all = across(target_send, "tile", groups)

    chunk = (BATCH * step * pairs, 2 * width)
    grouped = (slots * shares * step // width + 1, width, width)
    half = shape(chips, width + 16, width, dtype=BF16)
    sums, sums_send, pred, col, col_edge = call(
        pair_kernel,
        (
            half,
            half,
            shape(chips, 2 * slots * step, width, dtype=BF16),
            shape(part, width),
            shape(edge, width, dtype=BF16),
        ),
        [
            pltpu.SMEM((3, slots * shares + 2 * BATCH), jnp.int32),
            pltpu.SMEM((3, shares, width), jnp.int32),
            pltpu.SemaphoreType.DMA,
            pltpu.VMEM((3, shares, width), jnp.int32),
            pltpu.VMEM((rows // 2, 2 * width), F32),
            pltpu.VMEM((rows, width), F32),
            pltpu.VMEM((part + edge, width), F32),
            pltpu.VMEM(grouped, F32),
            pltpu.VMEM(grouped, F32),
            pltpu.VMEM((rows // 2, 2 * width), F32),
            pltpu.VMEM((8 * (part + edge), 2 * width), F32),
            pltpu.VMEM((2 * width + 16, 2 * width), F32),
            pltpu.VMEM((64, 2 * width), F32),
            pltpu.VMEM((2 * width, 2 * width), BF16),
            pltpu.VMEM((2 * width, 2 * width), BF16),
            pltpu.VMEM((2 * width, 2 * width), BF16),
            pltpu.VMEM((1, 2 * width), F32),
            pltpu.VMEM((1, 2 * width), F32),
            pltpu.VMEM(chunk, BF16),
            pltpu.VMEM(chunk, BF16),
            pltpu.VMEM(chunk, BF16),
            pltpu.VMEM(chunk, BF16),
        ],
        embeddings, emb_cols, emb_next, w_left, w_right, consts, target_all, w_pair,
    )
    sums = (sums.astype(F32) + swapped(sums_send, "tile", 1).astype(F32)).astype(BF16)
    sums = across(jnp.concatenate([sums, pred], axis=1), "tile", groups)
    row, weight, pred_mine, pred_send = call(
        share_kernel,
        (
            shape(pairs, width, dtype=BF16),
            shape(bins, pairs + 16 + edge, width, dtype=BF16),
            shape(chips, slots * step, width, dtype=BF16),
            shape(chips, slots * step, width, dtype=BF16),
        ),
        [], sums, col_edge,
    )
    weight = across(weight, "bin")
    (mine,) = call(
        total_kernel,
        (shape(chips, width + 16 + part, width, dtype=BF16),),
        [], weight, row, col,
    )
    mine = across(mine, "tile", groups)
    mine, pred_send = lax.optimization_barrier((mine, pred_send))
    pred_other = swapped(pred_send, "tile", 1)
    other = swapped(mine, "tile", 1)
    outs = (
        shape(slots, width, width, dtype=BF16),
        shape(rows, features, dtype=BF16),
        shape(features, width),
        shape(features, width),
        shape(5, width),
        shape(width, width),
        shape(1, width),
        shape(1, width),
    )
    outs = call(
        last_kernel,
        outs,
        [pltpu.VMEM(out.shape, out.dtype) for out in outs]
        + [
            pltpu.VMEM((rows, 2 * width), BF16),
            pltpu.VMEM((2 * features, width), F32),
            pltpu.VMEM((rows, width), F32),
            pltpu.VMEM((slots, width, width), F32),
            pltpu.SemaphoreType.DMA((rows // (2 * width) + 7,)),
        ],
        mine, other, pred_mine, pred_other, w_left, w_right, out_space=HBM,
    )
    return (outs[0][None, None], *outs[1:6], outs[6][0], outs[7][0])


def solution(mesh):
    return jax.shard_map(
        per_device,
        mesh=mesh,
        in_specs=(
            P("bin", None),
            P(),
            P(),
            P(),
            P(),
            P(),
            P(),
            P("bin", "tile", None, None),
            P("bin", "tile", None, None, None),
        ),
        out_specs=(
            P("bin", "tile", None, None, None),
            P("bin", None),
            P(),
            P(),
            P(),
            P(),
            P(),
            P(),
        ),
        check_vma=False,
    )
```

```python
import jax
import jax.numpy as jnp
from jax import lax
from jax.experimental import pallas as pl
from jax.experimental.pallas import tpu as pltpu
from jax.sharding import PartitionSpec as P

F32 = jnp.float32
BF16 = jnp.bfloat16
BATCH = 2
NEVER = -1e38
TINY = 1e-30
VMEM = pl.BlockSpec(memory_space=pltpu.VMEM)
HBM = pl.BlockSpec(memory_space=pl.ANY)


def place():
    return lax.axis_index("tile")


def split_kernel(
    list_mine, list_other, target_mine, target_other, send_ref, flip_ref, listed_ref
):
    core = place() & 1
    slots, width, _ = target_mine.shape
    chips = send_ref.shape[0]
    step = width // (2 * chips)
    listed_ref[...] = jnp.zeros_like(listed_ref)
    for side in range(2):
        mine = core == side
        for k in range(3):
            listed_ref[3 * side + k : 3 * side + k + 1, :slots] = jnp.where(
                mine, list_mine[k], list_other[k]
            ).astype(F32)
        for slot in range(slots):
            block = jnp.where(mine, target_mine[slot], target_other[slot]).astype(F32)
            flip_ref[side * slots + slot] = (block * (1.0 / width)).T
    listed = listed_ref[...].astype(BF16)
    for chip in range(chips):
        for side in range(2):
            at = (2 * chip + core) * step
            at = pl.multiple_of(at, step)
            pieces = [
                flip_ref[side * slots + slot, pl.ds(at, step), :] for slot in range(slots)
            ]
            send_ref[chip, side * slots * step : (side + 1) * slots * step, :] = jnp.concatenate(
                pieces, axis=0
            ).astype(BF16)
        send_ref[chip, 2 * slots * step :, :] = listed


def ready_kernel(
    emb_ref, next_ref, left_w_ref, right_w_ref, const_ref, w_ref,
    left_ref, right_ref, w_two, out_two, back_two, lines_ref, full_ref,
):
    tile = place()
    width = w_ref.shape[0]
    pairs = width // 2
    blocks = emb_ref.shape[0] // width
    edge = next_ref.shape[0]
    own = right_ref.shape[0] - edge
    step = own // blocks
    w = w_ref[...].astype(F32)
    w_out = const_ref[6:7, :]
    b_pair = const_ref[5:6, :]
    size = jnp.abs(w_out)
    power = jnp.exp2(jnp.floor(jnp.log2(jnp.maximum(size, TINY))))
    power = jnp.where(size < TINY, 0.0, power).astype(BF16).astype(F32)
    power = jnp.where(w_out < 0.0, -power, power)
    ratio = jnp.where(size < TINY, 1.0, w_out / jnp.where(size < TINY, 1.0, power))
    back = (w * w_out).T.astype(BF16)
    spread = jnp.broadcast_to(power * (1.0 / width), (width, width)).T.astype(BF16)
    for ref, block in ((w_two, w_ref[...]), (out_two, spread), (back_two, back)):
        ref[...] = jnp.zeros_like(ref)
        ref[:width, :width] = block
        ref[width:, width:] = block
    lines = jnp.concatenate([ratio, b_pair, jnp.zeros((6, width), F32)], axis=0)
    lines_ref[:, :width] = lines
    lines_ref[:, width:] = lines
    weights = jnp.concatenate([left_w_ref[...], right_w_ref[...]], axis=1)
    for block in range(0, blocks, 2):
        both = jnp.dot(
            emb_ref[block * width : (block + 2) * width, :],
            weights,
            preferred_element_type=F32,
        ).astype(BF16).astype(F32)
        for k in range(2):
            left = both[k * width : (k + 1) * width, :width]
            at = (block + k) * pairs
            left_ref[at : at + pairs, :width] = left[:pairs]
            left_ref[at : at + pairs, width:] = left[pairs:]
        full_ref[block * width : (block + 2) * width, :] = both[:, width:]
    for block in range(blocks):
        at = pl.multiple_of(block * width + tile * step, step)
        right_ref[block * step : (block + 1) * step, :] = full_ref[pl.ds(at, step), :]
    right_next = jnp.dot(next_ref[...], right_w_ref[...], preferred_element_type=F32)
    right_ref[own:, :] = right_next.astype(BF16).astype(F32)


def pair_kernel(
    emb_ref, cols_ref, next_ref, const_ref, target_ref, w_ref,
    left_ref, right_all, w_two, out_two, back_two, lines_ref,
    keep_ref, send_ref, pred_ref, col_ref, edge_ref,
    table, lists, list_sem, list_all, target_all, pred_all, row_all, col_all,
    outer_all, bias_all, first_0, first_1, slope_0, slope_1,
):
    tile = place()
    width = w_ref.shape[0]
    pairs = width // 2
    blocks = emb_ref.shape[0] // width
    chips = target_ref.shape[0]
    shares = 2 * chips
    step = width // shares
    slots = target_ref.shape[1] // (2 * step) - 1
    core = tile & 1
    groups = target_all.shape[0] - 1
    spread_bits = (width // step).bit_length() - 1

    for chip in range(chips):
        rows = target_ref[chip, 2 * slots * step :, :].astype(F32).astype(jnp.int32)
        for side in range(2):
            for k in range(3):
                at = 3 * side + k
                list_all[k, 2 * chip + side : 2 * chip + side + 1] = rows[at : at + 1]
    copy = pltpu.make_async_copy(list_all, lists, list_sem)
    copy.start()

    w = w_ref[...].astype(F32)
    w_out = const_ref[6:7, :]
    b_pair = const_ref[5:6, :]
    own = blocks * step
    rows = [target_ref[chip, : 2 * slots * step, :].astype(F32) for chip in range(chips)]
    rows = jnp.concatenate(rows, axis=0)
    for group in range(groups):
        target_all[group] = rows[group * width : (group + 1) * width].T
    target_all[groups] = jnp.zeros((width, width), F32)
    for ref in (pred_all, row_all, col_all, outer_all, bias_all, first_1, slope_1):
        ref[...] = jnp.zeros_like(ref)
    lane = lax.broadcasted_iota(jnp.int32, (width, width), 1)
    ones = jnp.ones((16, BATCH * step * pairs), BF16)

    copy.wait()
    count = jnp.int32(0)
    for share in range(shares):
        for slot in range(slots):
            offset = lists[2, share, slot]
            table[0, count] = lists[0, share, slot] & (blocks - 1)
            table[1, count] = offset
            table[2, count] = share * slots + slot
            count = count + jnp.where(offset >= 0, 1, 0)
    for spare in range(2 * BATCH):
        table[0, count + spare] = 0
        table[1, count + spare] = 0
        table[2, count + spare] = shares * slots

    def forward(turn, first_ref, slope_ref):
        pre = []
        wanted = []
        shifts = []
        floors = []
        for k in range(BATCH):
            job = turn * BATCH + k
            block, offset, slot = table[0, job], table[1, job], table[2, job]
            shift = (slot & (width // step - 1)) * step
            shifts.append((slot >> spread_bits, shift))
            at = pl.multiple_of(block * pairs, pairs)
            col_at = pl.multiple_of((block + offset) * step, step)
            right = right_all[pl.ds(col_at, step), :] + const_ref[pl.ds(offset, 1), :]
            right = jnp.concatenate([right, right], axis=1)
            left = left_ref[pl.ds(at, pairs), :]
            pre += [left + right[j : j + 1, :] for j in range(step)]
            target = pltpu.roll(
                target_all[slot >> spread_bits], (width - shift) & (width - 1), 1
            )
            for j in range(step):
                want = jnp.broadcast_to(target[:, j : j + 1], (width, width))
                wanted.append(jnp.concatenate([want[:pairs], want[pairs:]], axis=1))
            floor = jnp.where(job < count, lines_ref[1:2, :], jnp.full((1, 2 * width), NEVER, F32))
            floors.append(jnp.broadcast_to(floor, (step * pairs, 2 * width)))
        first = jnp.maximum(jnp.concatenate(pre, axis=0).astype(BF16), 0.0)
        first_ref[...] = first
        act = jnp.dot(first, w_two[...], preferred_element_type=F32)
        act = act + jnp.concatenate(floors, axis=0)
        second = jnp.maximum((act * lines_ref[0:1, :]).astype(BF16), 0.0)
        contact = jnp.dot(second, out_two[...], preferred_element_type=F32)
        slope = (contact - jnp.concatenate(wanted, axis=0)).astype(BF16)
        slope_ref[...] = jnp.where(second > 0, slope, jnp.zeros_like(slope))
        for k, (group, shift) in enumerate(shifts):
            found = jnp.zeros((width, width), F32)
            for j in range(step):
                here = contact[(k * step + j) * pairs : (k * step + j + 1) * pairs]
                here = jnp.concatenate([here[:, :width], here[:, width:]], axis=0)
                found = jnp.where(lane == j, here, found)
            mine = (lane >= shift) & (lane < shift + step)
            pred_all[group] = jnp.where(mine, pltpu.roll(found, shift, 1), pred_all[group])

    def backward(turn, first_ref, slope_ref):
        first = first_ref[...]
        slope = slope_ref[...]
        back = jnp.dot(slope, back_two[...], preferred_element_type=F32)
        back = jnp.where(first.astype(F32) > 0.0, back, 0.0)
        for k in range(BATCH):
            job = turn * BATCH + k
            block, offset = table[0, job], table[1, job]
            at = pl.multiple_of(block * pairs, pairs)
            rows = jnp.zeros((pairs, 2 * width), F32)
            cols = []
            for j in range(step):
                here = back[(k * step + j) * pairs : (k * step + j + 1) * pairs]
                rows = rows + here
                cols.append(sum(here[g : g + 8] for g in range(0, pairs, 8)))
            row_all[pl.ds(at, pairs), :] += rows
            col_at = pl.multiple_of((block + offset) * (8 * step), 8 * step)
            col_all[pl.ds(col_at, 8 * step), :] += jnp.concatenate(cols, axis=0)
            bias_all[pl.ds(pl.multiple_of(offset * 8, 8), 8), :] += sum(cols)
        lhs = jnp.concatenate([first.T, ones], axis=0)
        outer_all[...] += jnp.dot(lhs, slope, preferred_element_type=F32)

    def body(pass_at, _):
        turn = 2 * pass_at
        backward(jnp.maximum(turn - 1, 0), first_1, slope_1)
        forward(turn, first_0, slope_0)
        backward(turn, first_0, slope_0)
        forward(turn + 1, first_1, slope_1)
        return 0

    passes = lax.div(count + 2 * BATCH - 1, 2 * BATCH)
    lax.fori_loop(0, passes, body, 0)
    backward(jnp.maximum(2 * passes - 1, 0), first_1, slope_1)

    flat = [(pred_all[group] * float(width)).T for group in range(groups)]
    flat = jnp.concatenate(flat, axis=0).astype(BF16)
    for chip in range(chips):
        pred_ref[chip] = flat[chip * 2 * slots * step : (chip + 1) * 2 * slots * step]
    def folded(ref, count):
        sums = [
            jnp.sum(ref[8 * k : 8 * k + 8, :], axis=0, keepdims=True) for k in range(count)
        ]
        sums = jnp.concatenate(sums, axis=0)
        return sums[:, :width] + sums[:, width:]

    col = folded(col_all, col_all.shape[0] // 8)
    bias = folded(bias_all, 8)
    outer = outer_all[:width, :width] + outer_all[width : 2 * width, width:]
    sum_d = outer_all[2 * width : 2 * width + 1, :width] + outer_all[2 * width : 2 * width + 1, width:]
    line = lax.broadcasted_iota(jnp.int32, bias.shape, 0)
    sum_out = jnp.sum(w * outer, axis=0, keepdims=True) + b_pair * sum_d
    vectors = jnp.where(line == 5, sum_d * w_out, bias)
    vectors = jnp.where(line == 6, sum_out, vectors)
    outer = outer * w_out
    high = vectors.astype(BF16).astype(F32)
    rest = (high, vectors - high)
    col_low = col.astype(BF16)
    rows = []
    for block in range(blocks):
        here = row_all[block * pairs : (block + 1) * pairs, :].astype(BF16)
        rows += [here[:, :width], here[:, width:]]
    embs = [cols_ref[...], next_ref[...]]
    contract = (((0,), (0,)), ((), ()))
    grads = (
        lax.dot_general(
            jnp.concatenate(rows, axis=0), emb_ref[...], contract, preferred_element_type=F32
        ).astype(BF16),
        lax.dot_general(
            col_low, jnp.concatenate(embs, axis=0), contract, preferred_element_type=F32
        ).astype(BF16),
    )
    def message(share):
        side, at = share // chips, share % chips
        grad = grads[side][:, at // 2 * width : (at // 2 + 1) * width]
        more = rest[share] if share < 2 else jnp.zeros_like(high)
        small = jnp.concatenate([outer[8 * share : 8 * share + 8], more], axis=0)
        return jnp.concatenate(
            [rows[share], grad[at % 2 * pairs : (at % 2 + 1) * pairs], small.astype(BF16)], axis=0
        )

    for chip in range(chips):
        even, odd = message(2 * chip), message(2 * chip + 1)
        keep_ref[chip] = jnp.where(core == 0, even, odd)
        send_ref[chip] = jnp.where(core == 0, odd, even)
    col_ref[...] = col[:own]
    edge_ref[...] = col_low[own:]


def share_kernel(sum_ref, edge_ref, row_ref, message_ref, mine_ref, send_ref):
    core = place() & 1
    chips, _, width = sum_ref.shape
    pairs = width // 2
    head = width + 16
    slot_rows = mine_ref.shape[1]
    total = jnp.zeros((head, width), F32)
    for chip in range(chips):
        total = total + sum_ref[chip, :head, :].astype(F32)
        first = sum_ref[chip, head : head + slot_rows, :]
        second = sum_ref[chip, head + slot_rows :, :]
        mine_ref[chip] = jnp.where(core == 0, first, second)
        send_ref[chip] = jnp.where(core == 0, second, first)
    total = total.astype(BF16)
    row_ref[...] = total[:pairs]
    for bin_at in range(message_ref.shape[0]):
        message_ref[bin_at, : head - pairs, :] = total[pairs:]
        message_ref[bin_at, head - pairs :, :] = edge_ref[...]


def total_kernel(met_ref, row_ref, col_ref, message_ref):
    here = lax.axis_index("bin")
    bins = met_ref.shape[0]
    width = row_ref.shape[1]
    pairs = row_ref.shape[0]
    edge = col_ref.shape[0] // 2
    count = met_ref.shape[1] - edge
    total = jnp.zeros((count, width), F32)
    before = jnp.zeros((edge, width), F32)
    for bin_at in range(bins):
        total = total + met_ref[bin_at, :count, :].astype(F32)
        near = met_ref[bin_at, count:, :].astype(F32)
        before = jnp.where(here == bin_at + 1, near, before)
    total = total.astype(BF16)
    col = col_ref[...]
    top = (col[:edge] + before).astype(BF16)
    low = col[edge:].astype(BF16)
    for chip in range(message_ref.shape[0]):
        message_ref[chip, :pairs, :] = row_ref[...]
        message_ref[chip, pairs : pairs + count, :] = total
        message_ref[chip, pairs + count : pairs + count + edge, :] = top
        message_ref[chip, pairs + count + edge :, :] = low


def last_kernel(
    mine_ref, other_ref, pred_mine, pred_other, left_w_ref, right_w_ref,
    pred_hbm, emb_hbm, left_hbm, right_hbm, bias_hbm, w_hbm, b_hbm, out_hbm,
    pred_ref, emb_ref, left_ref, right_ref, bias_ref, w_ref, b_ref, out_ref,
    both_ref, flat_ref, col_ref, flip_ref, sems,
):
    core = place() & 1
    width = left_w_ref.shape[1]
    pairs = width // 2
    chips = mine_ref.shape[0]
    slots = pred_ref.shape[0]
    step = width // (2 * chips)
    copies = []

    def leave(source, target):
        copies.append(pltpu.make_async_copy(source, target, sems.at[len(copies)]))
        copies[-1].start()

    lows = []
    for share in range(2 * chips):
        block = jnp.where(core == share % 2, mine_ref[share // 2], other_ref[share // 2])
        both_ref[share * pairs : (share + 1) * pairs, :width] = block[:pairs]
        block = block.astype(F32)
        for k in range(col_ref.shape[0] // width):
            to = k * width + share * step
            at = width + 16 + k * step
            col_ref[to : to + step, :] = block[at : at + step]
        flat_ref[share * pairs : (share + 1) * pairs, :] = block[pairs:width]
        small = block[width : width + 16]
        w_ref[8 * share : 8 * share + 8, :] = small[:8]
        lows.append(small[8:])
    both_ref[:, width:] = col_ref[...].astype(BF16)
    weights = jnp.concatenate([left_w_ref[...], right_w_ref[...]], axis=1)
    part = 2 * width
    for k in range(both_ref.shape[0] // part):
        rows = pl.ds(k * part, part)
        emb_ref[rows, :] = lax.dot_general(
            both_ref[rows, :], weights, (((1,), (1,)), ((), ())), preferred_element_type=F32
        ).astype(BF16)
        leave(emb_ref.at[rows, :], emb_hbm.at[rows, :])
    for side, (grad_ref, grad_hbm) in enumerate(((left_ref, left_hbm), (right_ref, right_hbm))):
        for k in range(chips // 2):
            at = (side * chips // 2 + k) * width
            grad_ref[k * width : (k + 1) * width, :] = flat_ref[at : at + width, :].T
        leave(grad_ref, grad_hbm)
    vectors = lows[0] + lows[1]
    bias_ref[...] = vectors[:5]
    b_ref[...] = vectors[5:6]
    out_ref[...] = vectors[6:7]
    for source, target in ((w_ref, w_hbm), (bias_ref, bias_hbm), (b_ref, b_hbm), (out_ref, out_hbm)):
        leave(source, target)
    for chip in range(chips):
        for ref, side in ((pred_mine, core), (pred_other, 1 - core)):
            block = ref[chip].astype(F32)
            to = pl.multiple_of((2 * chip + side) * step, step)
            for slot in range(slots):
                flip_ref[slot, pl.ds(to, step), :] = block[slot * step : (slot + 1) * step]
    for slot in range(slots):
        pred_ref[slot] = flip_ref[slot].T.astype(BF16)
    leave(pred_ref, pred_hbm)
    for copy in copies:
        copy.wait()


def shape(*dims, dtype=F32):
    return jax.ShapeDtypeStruct(dims, dtype)


def call(kernel, outs, scratch, *args, space=None, out_space=VMEM, limit=32):
    return pl.pallas_call(
        kernel,
        out_shape=outs,
        in_specs=space or [VMEM] * len(args),
        out_specs=(out_space,) * len(outs),
        scratch_shapes=scratch,
        compiler_params=pltpu.CompilerParams(vmem_limit_bytes=limit * 1024 * 1024),
    )(*args)


def swapped(block, axis, bits):
    return lax.ppermute(block, axis, [(i, i ^ bits) for i in range(lax.axis_size(axis))])


def across(block, axis, groups=None):
    return lax.all_to_all(block, axis, 0, 0, axis_index_groups=groups, tiled=True)


def per_device(embeddings, w_left, w_right, pair_bias, w_pair, b_pair, w_out, tile_list, target):
    tile = place()
    core = lax.rem(tile, 2)
    slots, width = target.shape[2:4]
    rows, features = embeddings.shape
    blocks = rows // width
    pairs = width // 2
    shares = lax.axis_size("tile")
    chips = shares // 2
    step = width // shares
    part = rows // shares
    edge = part // 2
    target = target[0, 0]
    lists = jnp.transpose(tile_list, (0, 3, 1, 2)).reshape(3, 1, slots)

    emb_cols = lax.dynamic_slice_in_dim(
        embeddings.reshape(blocks, shares, step, features), tile, 1, 1
    ).reshape(part, features)
    target_other = swapped(target, "tile", 1)
    lists_other = swapped(lists, "tile", 1)
    bins = lax.axis_size("bin")
    emb_next = lax.ppermute(emb_cols[:edge], "bin", [(k + 1, k) for k in range(bins - 1)])
    consts = jnp.concatenate(
        [pair_bias, b_pair[None], w_out[None], jnp.zeros((1, width), F32)], axis=0
    )
    (target_send,) = call(
        split_kernel,
        (shape(chips, 2 * (slots + 1) * step, width, dtype=BF16),),
        [pltpu.VMEM((2 * slots, width, width), F32), pltpu.VMEM((2 * step, width), F32)],
        lists, lists_other, target, target_other,
    )
    groups = [list(range(k, shares, 2)) for k in range(2)]
    target_send, consts = lax.optimization_barrier((target_send, consts))
    target_all = across(target_send, "tile", groups)

    chunk = (BATCH * step * pairs, 2 * width)
    grouped = (slots * shares * step // width + 1, width, width)
    double = shape(2 * width, 2 * width, dtype=BF16)
    ready = call(
        ready_kernel,
        (
            shape(rows // 2, 2 * width),
            shape(part + edge, width),
            double,
            double,
            double,
            shape(8, 2 * width),
        ),
        [pltpu.VMEM((rows, width), F32)],
        embeddings, emb_next, w_left, w_right, consts, w_pair,
    )
    half = shape(chips, width + 16, width, dtype=BF16)
    sums, sums_send, pred, col, col_edge = call(
        pair_kernel,
        (
            half,
            half,
            shape(chips, 2 * slots * step, width, dtype=BF16),
            shape(part, width),
            shape(edge, width, dtype=BF16),
        ),
        [
            pltpu.SMEM((3, slots * shares + 2 * BATCH), jnp.int32),
            pltpu.SMEM((3, shares, width), jnp.int32),
            pltpu.SemaphoreType.DMA,
            pltpu.VMEM((3, shares, width), jnp.int32),
            pltpu.VMEM(grouped, F32),
            pltpu.VMEM(grouped, F32),
            pltpu.VMEM((rows // 2, 2 * width), F32),
            pltpu.VMEM((8 * (part + edge), 2 * width), F32),
            pltpu.VMEM((2 * width + 16, 2 * width), F32),
            pltpu.VMEM((64, 2 * width), F32),
            pltpu.VMEM(chunk, BF16),
            pltpu.VMEM(chunk, BF16),
            pltpu.VMEM(chunk, BF16),
            pltpu.VMEM(chunk, BF16),
        ],
        embeddings, emb_cols, emb_next, consts, target_all, w_pair, *ready,
    )
    sums = (sums.astype(F32) + swapped(sums_send, "tile", 1).astype(F32)).astype(BF16)
    sums = across(jnp.concatenate([sums, pred], axis=1), "tile", groups)
    row, weight, pred_mine, pred_send = call(
        share_kernel,
        (
            shape(pairs, width, dtype=BF16),
            shape(bins, pairs + 16 + edge, width, dtype=BF16),
            shape(chips, slots * step, width, dtype=BF16),
            shape(chips, slots * step, width, dtype=BF16),
        ),
        [], sums, col_edge,
    )
    weight = across(weight, "bin")
    (mine,) = call(
        total_kernel,
        (shape(chips, width + 16 + part, width, dtype=BF16),),
        [], weight, row, col,
    )
    mine = across(mine, "tile", groups)
    mine, pred_send = lax.optimization_barrier((mine, pred_send))
    pred_other = swapped(pred_send, "tile", 1)
    other = swapped(mine, "tile", 1)
    outs = (
        shape(slots, width, width, dtype=BF16),
        shape(rows, features, dtype=BF16),
        shape(features, width),
        shape(features, width),
        shape(5, width),
        shape(width, width),
        shape(1, width),
        shape(1, width),
    )
    outs = call(
        last_kernel,
        outs,
        [pltpu.VMEM(out.shape, out.dtype) for out in outs]
        + [
            pltpu.VMEM((rows, 2 * width), BF16),
            pltpu.VMEM((2 * features, width), F32),
            pltpu.VMEM((rows, width), F32),
            pltpu.VMEM((slots, width, width), F32),
            pltpu.SemaphoreType.DMA((rows // (2 * width) + 7,)),
        ],
        mine, other, pred_mine, pred_other, w_left, w_right, out_space=HBM,
    )
    return (outs[0][None, None], *outs[1:6], outs[6][0], outs[7][0])


def solution(mesh):
    return jax.shard_map(
        per_device,
        mesh=mesh,
        in_specs=(
            P("bin", None),
            P(),
            P(),
            P(),
            P(),
            P(),
            P(),
            P("bin", "tile", None, None),
            P("bin", "tile", None, None, None),
        ),
        out_specs=(
            P("bin", "tile", None, None, None),
            P("bin", None),
            P(),
            P(),
            P(),
            P(),
            P(),
            P(),
        ),
        check_vma=False,
    )
```

```python
import jax
import jax.numpy as jnp
from jax import lax
from jax.experimental import pallas as pl
from jax.experimental.pallas import tpu as pltpu
from jax.sharding import PartitionSpec as P

F32 = jnp.float32
BF16 = jnp.bfloat16
BATCH = 2
NEVER = -1e38
TINY = 1e-30
VMEM = pl.BlockSpec(memory_space=pltpu.VMEM)
HBM = pl.BlockSpec(memory_space=pl.ANY)


def place():
    return lax.axis_index("tile")


def split_kernel(
    list_mine, list_other, target_mine, target_other, send_ref, flip_ref, listed_ref
):
    core = place() & 1
    slots, width, _ = target_mine.shape
    chips = send_ref.shape[0]
    step = width // (2 * chips)
    listed_ref[...] = jnp.zeros_like(listed_ref)
    for side in range(2):
        mine = core == side
        for k in range(3):
            listed_ref[3 * side + k : 3 * side + k + 1, :slots] = jnp.where(
                mine, list_mine[k], list_other[k]
            ).astype(F32)
        for slot in range(slots):
            block = jnp.where(mine, target_mine[slot], target_other[slot]).astype(F32)
            flip_ref[side * slots + slot] = (block * (1.0 / width)).T
    listed = listed_ref[...].astype(BF16)
    for chip in range(chips):
        for side in range(2):
            at = (2 * chip + core) * step
            at = pl.multiple_of(at, step)
            pieces = [
                flip_ref[side * slots + slot, pl.ds(at, step), :] for slot in range(slots)
            ]
            send_ref[chip, side * slots * step : (side + 1) * slots * step, :] = jnp.concatenate(
                pieces, axis=0
            ).astype(BF16)
        send_ref[chip, 2 * slots * step :, :] = listed


def ready_kernel(
    emb_ref, left_w_ref, right_w_ref, const_ref, w_ref,
    left_ref, right_ref, w_two, out_two, back_two, lines_ref, full_ref,
):
    tile = place()
    width = w_ref.shape[0]
    pairs = width // 2
    blocks = emb_ref.shape[0] // width
    step = right_ref.shape[0] // blocks
    w = w_ref[...].astype(F32)
    w_out = const_ref[6:7, :]
    b_pair = const_ref[5:6, :]
    size = jnp.abs(w_out)
    power = jnp.exp2(jnp.floor(jnp.log2(jnp.maximum(size, TINY))))
    power = jnp.where(size < TINY, 0.0, power).astype(BF16).astype(F32)
    power = jnp.where(w_out < 0.0, -power, power)
    ratio = jnp.where(size < TINY, 1.0, w_out / jnp.where(size < TINY, 1.0, power))
    back = (w * w_out).T.astype(BF16)
    spread = jnp.broadcast_to(power * (1.0 / width), (width, width)).T.astype(BF16)
    for ref, block in ((w_two, w_ref[...]), (out_two, spread), (back_two, back)):
        ref[...] = jnp.zeros_like(ref)
        ref[:width, :width] = block
        ref[width:, width:] = block
    lines = jnp.concatenate([ratio, b_pair, jnp.zeros((6, width), F32)], axis=0)
    lines_ref[:, :width] = lines
    lines_ref[:, width:] = lines
    weights = jnp.concatenate([left_w_ref[...], right_w_ref[...]], axis=1)
    for block in range(0, blocks, 2):
        both = jnp.dot(
            emb_ref[block * width : (block + 2) * width, :],
            weights,
            preferred_element_type=F32,
        ).astype(BF16).astype(F32)
        for k in range(2):
            left = both[k * width : (k + 1) * width, :width]
            at = (block + k) * pairs
            left_ref[at : at + pairs, :width] = left[:pairs]
            left_ref[at : at + pairs, width:] = left[pairs:]
        full_ref[block * width : (block + 2) * width, :] = both[:, width:]
    for block in range(blocks):
        at = pl.multiple_of(block * width + tile * step, step)
        right_ref[block * step : (block + 1) * step, :] = full_ref[pl.ds(at, step), :]


def pair_kernel(
    emb_ref, cols_ref, next_ref, right_w_ref, const_ref, target_ref, w_ref,
    left_ref, right_ref, w_two, out_two, back_two, lines_ref,
    keep_ref, send_ref, pred_ref, col_ref, edge_ref,
    table, lists, list_sem, list_all, target_all, pred_all, row_all, col_all,
    outer_all, bias_all, right_all, first_0, first_1, slope_0, slope_1,
):
    tile = place()
    width = w_ref.shape[0]
    pairs = width // 2
    blocks = emb_ref.shape[0] // width
    chips = target_ref.shape[0]
    shares = 2 * chips
    step = width // shares
    slots = target_ref.shape[1] // (2 * step) - 1
    core = tile & 1
    groups = target_all.shape[0] - 1
    spread_bits = (width // step).bit_length() - 1

    for chip in range(chips):
        rows = target_ref[chip, 2 * slots * step :, :].astype(F32).astype(jnp.int32)
        for side in range(2):
            for k in range(3):
                at = 3 * side + k
                list_all[k, 2 * chip + side : 2 * chip + side + 1] = rows[at : at + 1]
    copy = pltpu.make_async_copy(list_all, lists, list_sem)
    copy.start()

    w = w_ref[...].astype(F32)
    w_out = const_ref[6:7, :]
    b_pair = const_ref[5:6, :]
    own = blocks * step
    right_all[:own, :] = right_ref[...]
    right_next = jnp.dot(next_ref[...], right_w_ref[...], preferred_element_type=F32)
    right_all[own:, :] = right_next.astype(BF16).astype(F32)
    rows = [target_ref[chip, : 2 * slots * step, :].astype(F32) for chip in range(chips)]
    rows = jnp.concatenate(rows, axis=0)
    for group in range(groups):
        target_all[group] = rows[group * width : (group + 1) * width].T
    target_all[groups] = jnp.zeros((width, width), F32)
    for ref in (pred_all, row_all, col_all, outer_all, bias_all, first_1, slope_1):
        ref[...] = jnp.zeros_like(ref)
    lane = lax.broadcasted_iota(jnp.int32, (width, width), 1)
    ones = jnp.ones((16, BATCH * step * pairs), BF16)

    copy.wait()
    count = jnp.int32(0)
    for share in range(shares):
        for slot in range(slots):
            offset = lists[2, share, slot]
            table[0, count] = lists[0, share, slot] & (blocks - 1)
            table[1, count] = offset
            table[2, count] = share * slots + slot
            count = count + jnp.where(offset >= 0, 1, 0)
    for spare in range(2 * BATCH):
        table[0, count + spare] = 0
        table[1, count + spare] = 0
        table[2, count + spare] = shares * slots

    def forward(turn, first_ref, slope_ref):
        pre = []
        wanted = []
        shifts = []
        floors = []
        for k in range(BATCH):
            job = turn * BATCH + k
            block, offset, slot = table[0, job], table[1, job], table[2, job]
            shift = (slot & (width // step - 1)) * step
            shifts.append((slot >> spread_bits, shift))
            at = pl.multiple_of(block * pairs, pairs)
            col_at = pl.multiple_of((block + offset) * step, step)
            right = right_all[pl.ds(col_at, step), :] + const_ref[pl.ds(offset, 1), :]
            right = jnp.concatenate([right, right], axis=1)
            left = left_ref[pl.ds(at, pairs), :]
            pre += [left + right[j : j + 1, :] for j in range(step)]
            target = pltpu.roll(
                target_all[slot >> spread_bits], (width - shift) & (width - 1), 1
            )
            for j in range(step):
                want = jnp.broadcast_to(target[:, j : j + 1], (width, width))
                wanted.append(jnp.concatenate([want[:pairs], want[pairs:]], axis=1))
            floor = jnp.where(job < count, lines_ref[1:2, :], jnp.full((1, 2 * width), NEVER, F32))
            floors.append(jnp.broadcast_to(floor, (step * pairs, 2 * width)))
        first = jnp.maximum(jnp.concatenate(pre, axis=0).astype(BF16), 0.0)
        first_ref[...] = first
        act = jnp.dot(first, w_two[...], preferred_element_type=F32)
        act = act + jnp.concatenate(floors, axis=0)
        second = jnp.maximum((act * lines_ref[0:1, :]).astype(BF16), 0.0)
        contact = jnp.dot(second, out_two[...], preferred_element_type=F32)
        slope = (contact - jnp.concatenate(wanted, axis=0)).astype(BF16)
        slope_ref[...] = jnp.where(second > 0, slope, jnp.zeros_like(slope))
        for k, (group, shift) in enumerate(shifts):
            found = jnp.zeros((width, width), F32)
            for j in range(step):
                here = contact[(k * step + j) * pairs : (k * step + j + 1) * pairs]
                here = jnp.concatenate([here[:, :width], here[:, width:]], axis=0)
                found = jnp.where(lane == j, here, found)
            mine = (lane >= shift) & (lane < shift + step)
            pred_all[group] = jnp.where(mine, pltpu.roll(found, shift, 1), pred_all[group])

    def backward(turn, first_ref, slope_ref):
        first = first_ref[...]
        slope = slope_ref[...]
        back = jnp.dot(slope, back_two[...], preferred_element_type=F32)
        back = jnp.where(first.astype(F32) > 0.0, back, 0.0)
        for k in range(BATCH):
            job = turn * BATCH + k
            block, offset = table[0, job], table[1, job]
            at = pl.multiple_of(block * pairs, pairs)
            rows = jnp.zeros((pairs, 2 * width), F32)
            cols = []
            for j in range(step):
                here = back[(k * step + j) * pairs : (k * step + j + 1) * pairs]
                rows = rows + here
                cols.append(sum(here[g : g + 8] for g in range(0, pairs, 8)))
            row_all[pl.ds(at, pairs), :] += rows
            col_at = pl.multiple_of((block + offset) * (8 * step), 8 * step)
            col_all[pl.ds(col_at, 8 * step), :] += jnp.concatenate(cols, axis=0)
            bias_all[pl.ds(pl.multiple_of(offset * 8, 8), 8), :] += sum(cols)
        lhs = jnp.concatenate([first.T, ones], axis=0)
        outer_all[...] += jnp.dot(lhs, slope, preferred_element_type=F32)

    def body(pass_at, _):
        turn = 2 * pass_at
        backward(jnp.maximum(turn - 1, 0), first_1, slope_1)
        forward(turn, first_0, slope_0)
        backward(turn, first_0, slope_0)
        forward(turn + 1, first_1, slope_1)
        return 0

    passes = lax.div(count + 2 * BATCH - 1, 2 * BATCH)
    lax.fori_loop(0, passes, body, 0)
    backward(jnp.maximum(2 * passes - 1, 0), first_1, slope_1)

    flat = [(pred_all[group] * float(width)).T for group in range(groups)]
    flat = jnp.concatenate(flat, axis=0).astype(BF16)
    for chip in range(chips):
        pred_ref[chip] = flat[chip * 2 * slots * step : (chip + 1) * 2 * slots * step]
    def folded(ref, count):
        sums = [
            jnp.sum(ref[8 * k : 8 * k + 8, :], axis=0, keepdims=True) for k in range(count)
        ]
        sums = jnp.concatenate(sums, axis=0)
        return sums[:, :width] + sums[:, width:]

    col = folded(col_all, col_all.shape[0] // 8)
    bias = folded(bias_all, 8)
    outer = outer_all[:width, :width] + outer_all[width : 2 * width, width:]
    sum_d = outer_all[2 * width : 2 * width + 1, :width] + outer_all[2 * width : 2 * width + 1, width:]
    line = lax.broadcasted_iota(jnp.int32, bias.shape, 0)
    sum_out = jnp.sum(w * outer, axis=0, keepdims=True) + b_pair * sum_d
    vectors = jnp.where(line == 5, sum_d * w_out, bias)
    vectors = jnp.where(line == 6, sum_out, vectors)
    outer = outer * w_out
    high = vectors.astype(BF16).astype(F32)
    rest = (high, vectors - high)
    col_low = col.astype(BF16)
    rows = []
    for block in range(blocks):
        here = row_all[block * pairs : (block + 1) * pairs, :].astype(BF16)
        rows += [here[:, :width], here[:, width:]]
    embs = [cols_ref[...], next_ref[...]]
    contract = (((0,), (0,)), ((), ()))
    grads = (
        lax.dot_general(
            jnp.concatenate(rows, axis=0), emb_ref[...], contract, preferred_element_type=F32
        ).astype(BF16),
        lax.dot_general(
            col_low, jnp.concatenate(embs, axis=0), contract, preferred_element_type=F32
        ).astype(BF16),
    )
    def message(share):
        side, at = share // chips, share % chips
        grad = grads[side][:, at // 2 * width : (at // 2 + 1) * width]
        more = rest[share] if share < 2 else jnp.zeros_like(high)
        small = jnp.concatenate([outer[8 * share : 8 * share + 8], more], axis=0)
        return jnp.concatenate(
            [rows[share], grad[at % 2 * pairs : (at % 2 + 1) * pairs], small.astype(BF16)], axis=0
        )

    for chip in range(chips):
        even, odd = message(2 * chip), message(2 * chip + 1)
        keep_ref[chip] = jnp.where(core == 0, even, odd)
        send_ref[chip] = jnp.where(core == 0, odd, even)
    col_ref[...] = col[:own]
    edge_ref[...] = col_low[own:]


def share_kernel(sum_ref, edge_ref, row_ref, message_ref, mine_ref, send_ref):
    core = place() & 1
    chips, _, width = sum_ref.shape
    pairs = width // 2
    head = width + 16
    slot_rows = mine_ref.shape[1]
    total = jnp.zeros((head, width), F32)
    for chip in range(chips):
        total = total + sum_ref[chip, :head, :].astype(F32)
        first = sum_ref[chip, head : head + slot_rows, :]
        second = sum_ref[chip, head + slot_rows :, :]
        mine_ref[chip] = jnp.where(core == 0, first, second)
        send_ref[chip] = jnp.where(core == 0, second, first)
    total = total.astype(BF16)
    row_ref[...] = total[:pairs]
    for bin_at in range(message_ref.shape[0]):
        message_ref[bin_at, : head - pairs, :] = total[pairs:]
        message_ref[bin_at, head - pairs :, :] = edge_ref[...]


def total_kernel(met_ref, row_ref, col_ref, message_ref):
    here = lax.axis_index("bin")
    bins = met_ref.shape[0]
    width = row_ref.shape[1]
    pairs = row_ref.shape[0]
    edge = col_ref.shape[0] // 2
    count = met_ref.shape[1] - edge
    total = jnp.zeros((count, width), F32)
    before = jnp.zeros((edge, width), F32)
    for bin_at in range(bins):
        total = total + met_ref[bin_at, :count, :].astype(F32)
        near = met_ref[bin_at, count:, :].astype(F32)
        before = jnp.where(here == bin_at + 1, near, before)
    total = total.astype(BF16)
    col = col_ref[...]
    top = (col[:edge] + before).astype(BF16)
    low = col[edge:].astype(BF16)
    for chip in range(message_ref.shape[0]):
        message_ref[chip, :pairs, :] = row_ref[...]
        message_ref[chip, pairs : pairs + count, :] = total
        message_ref[chip, pairs + count : pairs + count + edge, :] = top
        message_ref[chip, pairs + count + edge :, :] = low


def last_kernel(
    mine_ref, other_ref, pred_mine, pred_other, left_w_ref, right_w_ref,
    pred_hbm, emb_hbm, left_hbm, right_hbm, bias_hbm, w_hbm, b_hbm, out_hbm,
    pred_ref, emb_ref, left_ref, right_ref, bias_ref, w_ref, b_ref, out_ref,
    both_ref, flat_ref, col_ref, flip_ref, sems,
):
    core = place() & 1
    width = left_w_ref.shape[1]
    pairs = width // 2
    chips = mine_ref.shape[0]
    slots = pred_ref.shape[0]
    step = width // (2 * chips)
    copies = []

    def leave(source, target):
        copies.append(pltpu.make_async_copy(source, target, sems.at[len(copies)]))
        copies[-1].start()

    lows = []
    for share in range(2 * chips):
        block = jnp.where(core == share % 2, mine_ref[share // 2], other_ref[share // 2])
        both_ref[share * pairs : (share + 1) * pairs, :width] = block[:pairs]
        block = block.astype(F32)
        for k in range(col_ref.shape[0] // width):
            to = k * width + share * step
            at = width + 16 + k * step
            col_ref[to : to + step, :] = block[at : at + step]
        flat_ref[share * pairs : (share + 1) * pairs, :] = block[pairs:width]
        small = block[width : width + 16]
        w_ref[8 * share : 8 * share + 8, :] = small[:8]
        lows.append(small[8:])
    both_ref[:, width:] = col_ref[...].astype(BF16)
    weights = jnp.concatenate([left_w_ref[...], right_w_ref[...]], axis=1)
    part = 2 * width
    for k in range(both_ref.shape[0] // part):
        rows = pl.ds(k * part, part)
        emb_ref[rows, :] = lax.dot_general(
            both_ref[rows, :], weights, (((1,), (1,)), ((), ())), preferred_element_type=F32
        ).astype(BF16)
        leave(emb_ref.at[rows, :], emb_hbm.at[rows, :])
    for side, (grad_ref, grad_hbm) in enumerate(((left_ref, left_hbm), (right_ref, right_hbm))):
        for k in range(chips // 2):
            at = (side * chips // 2 + k) * width
            grad_ref[k * width : (k + 1) * width, :] = flat_ref[at : at + width, :].T
        leave(grad_ref, grad_hbm)
    vectors = lows[0] + lows[1]
    bias_ref[...] = vectors[:5]
    b_ref[...] = vectors[5:6]
    out_ref[...] = vectors[6:7]
    for source, target in ((w_ref, w_hbm), (bias_ref, bias_hbm), (b_ref, b_hbm), (out_ref, out_hbm)):
        leave(source, target)
    for chip in range(chips):
        for ref, side in ((pred_mine, core), (pred_other, 1 - core)):
            block = ref[chip].astype(F32)
            to = pl.multiple_of((2 * chip + side) * step, step)
            for slot in range(slots):
                flip_ref[slot, pl.ds(to, step), :] = block[slot * step : (slot + 1) * step]
    for slot in range(slots):
        pred_ref[slot] = flip_ref[slot].T.astype(BF16)
    leave(pred_ref, pred_hbm)
    for copy in copies:
        copy.wait()


def shape(*dims, dtype=F32):
    return jax.ShapeDtypeStruct(dims, dtype)


def call(kernel, outs, scratch, *args, space=None, out_space=VMEM, limit=32):
    return pl.pallas_call(
        kernel,
        out_shape=outs,
        in_specs=space or [VMEM] * len(args),
        out_specs=(out_space,) * len(outs),
        scratch_shapes=scratch,
        compiler_params=pltpu.CompilerParams(vmem_limit_bytes=limit * 1024 * 1024),
    )(*args)


def swapped(block, axis, bits):
    return lax.ppermute(block, axis, [(i, i ^ bits) for i in range(lax.axis_size(axis))])


def across(block, axis, groups=None):
    return lax.all_to_all(block, axis, 0, 0, axis_index_groups=groups, tiled=True)


def per_device(embeddings, w_left, w_right, pair_bias, w_pair, b_pair, w_out, tile_list, target):
    tile = place()
    core = lax.rem(tile, 2)
    slots, width = target.shape[2:4]
    rows, features = embeddings.shape
    blocks = rows // width
    pairs = width // 2
    shares = lax.axis_size("tile")
    chips = shares // 2
    step = width // shares
    part = rows // shares
    edge = part // 2
    target = target[0, 0]
    lists = jnp.transpose(tile_list, (0, 3, 1, 2)).reshape(3, 1, slots)

    emb_cols = lax.dynamic_slice_in_dim(
        embeddings.reshape(blocks, shares, step, features), tile, 1, 1
    ).reshape(part, features)
    target_other = swapped(target, "tile", 1)
    lists_other = swapped(lists, "tile", 1)
    bins = lax.axis_size("bin")
    emb_next = lax.ppermute(emb_cols[:edge], "bin", [(k + 1, k) for k in range(bins - 1)])
    consts = jnp.concatenate(
        [pair_bias, b_pair[None], w_out[None], jnp.zeros((1, width), F32)], axis=0
    )
    (target_send,) = call(
        split_kernel,
        (shape(chips, 2 * (slots + 1) * step, width, dtype=BF16),),
        [pltpu.VMEM((2 * slots, width, width), F32), pltpu.VMEM((2 * step, width), F32)],
        lists, lists_other, target, target_other,
    )
    groups = [list(range(k, shares, 2)) for k in range(2)]
    target_send, consts = lax.optimization_barrier((target_send, consts))
    target_all = across(target_send, "tile", groups)

    chunk = (BATCH * step * pairs, 2 * width)
    grouped = (slots * shares * step // width + 1, width, width)
    double = shape(2 * width, 2 * width, dtype=BF16)
    ready = call(
        ready_kernel,
        (
            shape(rows // 2, 2 * width),
            shape(part, width),
            double,
            double,
            double,
            shape(8, 2 * width),
        ),
        [pltpu.VMEM((rows, width), F32)],
        embeddings, w_left, w_right, consts, w_pair,
    )
    half = shape(chips, width + 16, width, dtype=BF16)
    sums, sums_send, pred, col, col_edge = call(
        pair_kernel,
        (
            half,
            half,
            shape(chips, 2 * slots * step, width, dtype=BF16),
            shape(part, width),
            shape(edge, width, dtype=BF16),
        ),
        [
            pltpu.SMEM((3, slots * shares + 2 * BATCH), jnp.int32),
            pltpu.SMEM((3, shares, width), jnp.int32),
            pltpu.SemaphoreType.DMA,
            pltpu.VMEM((3, shares, width), jnp.int32),
            pltpu.VMEM(grouped, F32),
            pltpu.VMEM(grouped, F32),
            pltpu.VMEM((rows // 2, 2 * width), F32),
            pltpu.VMEM((8 * (part + edge), 2 * width), F32),
            pltpu.VMEM((2 * width + 16, 2 * width), F32),
            pltpu.VMEM((64, 2 * width), F32),
            pltpu.VMEM((part + edge, width), F32),
            pltpu.VMEM(chunk, BF16),
            pltpu.VMEM(chunk, BF16),
            pltpu.VMEM(chunk, BF16),
            pltpu.VMEM(chunk, BF16),
        ],
        embeddings, emb_cols, emb_next, w_right, consts, target_all, w_pair, *ready,
    )
    sums = (sums.astype(F32) + swapped(sums_send, "tile", 1).astype(F32)).astype(BF16)
    sums = across(jnp.concatenate([sums, pred], axis=1), "tile", groups)
    row, weight, pred_mine, pred_send = call(
        share_kernel,
        (
            shape(pairs, width, dtype=BF16),
            shape(bins, pairs + 16 + edge, width, dtype=BF16),
            shape(chips, slots * step, width, dtype=BF16),
            shape(chips, slots * step, width, dtype=BF16),
        ),
        [], sums, col_edge,
    )
    weight = across(weight, "bin")
    (mine,) = call(
        total_kernel,
        (shape(chips, width + 16 + part, width, dtype=BF16),),
        [], weight, row, col,
    )
    mine = across(mine, "tile", groups)
    mine, pred_send = lax.optimization_barrier((mine, pred_send))
    pred_other = swapped(pred_send, "tile", 1)
    other = swapped(mine, "tile", 1)
    outs = (
        shape(slots, width, width, dtype=BF16),
        shape(rows, features, dtype=BF16),
        shape(features, width),
        shape(features, width),
        shape(5, width),
        shape(width, width),
        shape(1, width),
        shape(1, width),
    )
    outs = call(
        last_kernel,
        outs,
        [pltpu.VMEM(out.shape, out.dtype) for out in outs]
        + [
            pltpu.VMEM((rows, 2 * width), BF16),
            pltpu.VMEM((2 * features, width), F32),
            pltpu.VMEM((rows, width), F32),
            pltpu.VMEM((slots, width, width), F32),
            pltpu.SemaphoreType.DMA((rows // (2 * width) + 7,)),
        ],
        mine, other, pred_mine, pred_other, w_left, w_right, out_space=HBM,
    )
    return (outs[0][None, None], *outs[1:6], outs[6][0], outs[7][0])


def solution(mesh):
    return jax.shard_map(
        per_device,
        mesh=mesh,
        in_specs=(
            P("bin", None),
            P(),
            P(),
            P(),
            P(),
            P(),
            P(),
            P("bin", "tile", None, None),
            P("bin", "tile", None, None, None),
        ),
        out_specs=(
            P("bin", "tile", None, None, None),
            P("bin", None),
            P(),
            P(),
            P(),
            P(),
            P(),
            P(),
        ),
        check_vma=False,
    )
```

```python
import jax
import jax.numpy as jnp
from jax import lax
from jax.experimental import pallas as pl
from jax.experimental.pallas import tpu as pltpu
from jax.sharding import PartitionSpec as P

F32 = jnp.float32
BF16 = jnp.bfloat16
BATCH = 2
NEVER = -1e38
TINY = 1e-30
VMEM = pl.BlockSpec(memory_space=pltpu.VMEM)
HBM = pl.BlockSpec(memory_space=pl.ANY)


def place():
    return lax.axis_index("tile")


def split_kernel(
    list_mine, list_other, target_mine, target_other, send_ref, flip_ref, listed_ref
):
    core = place() & 1
    slots, width, _ = target_mine.shape
    chips = send_ref.shape[0]
    step = width // (2 * chips)
    listed_ref[...] = jnp.zeros_like(listed_ref)
    for side in range(2):
        mine = core == side
        for k in range(3):
            listed_ref[3 * side + k : 3 * side + k + 1, :slots] = jnp.where(
                mine, list_mine[k], list_other[k]
            ).astype(F32)
        for slot in range(slots):
            block = jnp.where(mine, target_mine[slot], target_other[slot]).astype(F32)
            flip_ref[side * slots + slot] = (block * (1.0 / width)).T
    listed = listed_ref[...].astype(BF16)
    for chip in range(chips):
        for side in range(2):
            at = (2 * chip + core) * step
            at = pl.multiple_of(at, step)
            pieces = [
                flip_ref[side * slots + slot, pl.ds(at, step), :] for slot in range(slots)
            ]
            send_ref[chip, side * slots * step : (side + 1) * slots * step, :] = jnp.concatenate(
                pieces, axis=0
            ).astype(BF16)
        send_ref[chip, 2 * slots * step :, :] = listed


def ready_kernel(
    emb_ref, left_w_ref, right_w_ref, const_ref, w_ref,
    left_ref, right_ref, w_two, out_two, back_two, lines_ref, full_ref,
):
    tile = place()
    width = w_ref.shape[0]
    pairs = width // 2
    blocks = emb_ref.shape[0] // width
    step = right_ref.shape[0] // blocks
    w = w_ref[...].astype(F32)
    w_out = const_ref[6:7, :]
    b_pair = const_ref[5:6, :]
    size = jnp.abs(w_out)
    power = jnp.exp2(jnp.floor(jnp.log2(jnp.maximum(size, TINY))))
    power = jnp.where(size < TINY, 0.0, power).astype(BF16).astype(F32)
    power = jnp.where(w_out < 0.0, -power, power)
    ratio = jnp.where(size < TINY, 1.0, w_out / jnp.where(size < TINY, 1.0, power))
    back = (w * w_out).T.astype(BF16)
    spread = jnp.broadcast_to(power * (1.0 / width), (width, width)).T.astype(BF16)
    for ref, block in ((w_two, w_ref[...]), (out_two, spread), (back_two, back)):
        ref[...] = jnp.zeros_like(ref)
        ref[:width, :width] = block
        ref[width:, width:] = block
    lines = jnp.concatenate([ratio, b_pair, jnp.zeros((6, width), F32)], axis=0)
    lines_ref[:, :width] = lines
    lines_ref[:, width:] = lines
    weights = jnp.concatenate([left_w_ref[...], right_w_ref[...]], axis=1)
    for block in range(0, blocks, 2):
        both = jnp.dot(
            emb_ref[block * width : (block + 2) * width, :],
            weights,
            preferred_element_type=F32,
        ).astype(BF16).astype(F32)
        for k in range(2):
            left = both[k * width : (k + 1) * width, :width]
            at = (block + k) * pairs
            left_ref[at : at + pairs, :width] = left[:pairs]
            left_ref[at : at + pairs, width:] = left[pairs:]
        full_ref[block * width : (block + 2) * width, :] = both[:, width:]
    for block in range(blocks):
        at = pl.multiple_of(block * width + tile * step, step)
        right_ref[block * step : (block + 1) * step, :] = full_ref[pl.ds(at, step), :]


def pair_kernel(
    emb_ref, cols_ref, next_ref, right_w_ref, const_ref, target_ref, w_ref,
    left_ref, right_ref, w_two, out_two, back_two, lines_ref,
    keep_ref, send_ref, pred_ref, col_ref, edge_ref,
    table, lists, list_sem, list_all, target_all, pred_all, row_all, col_all,
    outer_all, bias_all, right_all, first_0, first_1, slope_0, slope_1,
):
    tile = place()
    width = w_ref.shape[0]
    pairs = width // 2
    blocks = emb_ref.shape[0] // width
    chips = target_ref.shape[0]
    shares = 2 * chips
    step = width // shares
    slots = target_ref.shape[1] // (2 * step) - 1
    core = tile & 1
    groups = target_all.shape[0] - 1
    spread_bits = (width // step).bit_length() - 1

    for chip in range(chips):
        rows = target_ref[chip, 2 * slots * step :, :].astype(F32).astype(jnp.int32)
        for side in range(2):
            for k in range(3):
                at = 3 * side + k
                list_all[k, 2 * chip + side : 2 * chip + side + 1] = rows[at : at + 1]
    copy = pltpu.make_async_copy(list_all, lists, list_sem)
    copy.start()

    w = w_ref[...].astype(F32)
    w_out = const_ref[6:7, :]
    b_pair = const_ref[5:6, :]
    own = blocks * step
    right_all[:own, :] = right_ref[...]
    right_next = jnp.dot(next_ref[...], right_w_ref[...], preferred_element_type=F32)
    right_all[own:, :] = right_next.astype(BF16).astype(F32)
    rows = [target_ref[chip, : 2 * slots * step, :].astype(F32) for chip in range(chips)]
    rows = jnp.concatenate(rows, axis=0)
    for group in range(groups):
        target_all[group] = rows[group * width : (group + 1) * width].T
    target_all[groups] = jnp.zeros((width, width), F32)
    for ref in (pred_all, row_all, col_all, outer_all, bias_all, first_1, slope_1):
        ref[...] = jnp.zeros_like(ref)
    lane = lax.broadcasted_iota(jnp.int32, (width, width), 1)
    ones = jnp.ones((16, BATCH * step * pairs), BF16)

    copy.wait()
    count = jnp.int32(0)
    for share in range(shares):
        for slot in range(slots):
            offset = lists[2, share, slot]
            table[0, count] = lists[0, share, slot] & (blocks - 1)
            table[1, count] = offset
            table[2, count] = share * slots + slot
            count = count + jnp.where(offset >= 0, 1, 0)
    for spare in range(2 * BATCH):
        table[0, count + spare] = 0
        table[1, count + spare] = 0
        table[2, count + spare] = shares * slots

    def forward(turn, first_ref, slope_ref):
        pre = []
        wanted = []
        shifts = []
        floors = []
        for k in range(BATCH):
            job = turn * BATCH + k
            block, offset, slot = table[0, job], table[1, job], table[2, job]
            shift = (slot & (width // step - 1)) * step
            shifts.append((slot >> spread_bits, shift))
            at = pl.multiple_of(block * pairs, pairs)
            col_at = pl.multiple_of((block + offset) * step, step)
            right = right_all[pl.ds(col_at, step), :] + const_ref[pl.ds(offset, 1), :]
            right = jnp.concatenate([right, right], axis=1)
            left = left_ref[pl.ds(at, pairs), :]
            pre += [left + right[j : j + 1, :] for j in range(step)]
            target = pltpu.roll(
                target_all[slot >> spread_bits], (width - shift) & (width - 1), 1
            )
            for j in range(step):
                want = jnp.broadcast_to(target[:, j : j + 1], (width, width))
                wanted.append(jnp.concatenate([want[:pairs], want[pairs:]], axis=1))
            floor = jnp.where(job < count, lines_ref[1:2, :], jnp.full((1, 2 * width), NEVER, F32))
            floors.append(jnp.broadcast_to(floor, (step * pairs, 2 * width)))
        first = jnp.maximum(jnp.concatenate(pre, axis=0).astype(BF16), 0.0)
        first_ref[...] = first
        act = jnp.dot(first, w_two[...], preferred_element_type=F32)
        act = act + jnp.concatenate(floors, axis=0)
        second = jnp.maximum((act * lines_ref[0:1, :]).astype(BF16), 0.0)
        contact = jnp.dot(second, out_two[...], preferred_element_type=F32)
        slope = (contact - jnp.concatenate(wanted, axis=0)).astype(BF16)
        slope_ref[...] = jnp.where(second > 0, slope, jnp.zeros_like(slope))
        for k, (group, shift) in enumerate(shifts):
            found = jnp.zeros((width, width), F32)
            for j in range(step):
                here = contact[(k * step + j) * pairs : (k * step + j + 1) * pairs]
                here = jnp.concatenate([here[:, :width], here[:, width:]], axis=0)
                found = jnp.where(lane == j, here, found)
            mine = (lane >= shift) & (lane < shift + step)
            pred_all[group] = jnp.where(mine, pltpu.roll(found, shift, 1), pred_all[group])

    def backward(turn, first_ref, slope_ref):
        first = first_ref[...]
        slope = slope_ref[...]
        back = jnp.dot(slope, back_two[...], preferred_element_type=F32)
        back = jnp.where(first.astype(F32) > 0.0, back, 0.0)
        for k in range(BATCH):
            job = turn * BATCH + k
            block, offset = table[0, job], table[1, job]
            at = pl.multiple_of(block * pairs, pairs)
            rows = jnp.zeros((pairs, 2 * width), F32)
            cols = []
            for j in range(step):
                here = back[(k * step + j) * pairs : (k * step + j + 1) * pairs]
                rows = rows + here
                cols.append(sum(here[g : g + 8] for g in range(0, pairs, 8)))
            row_all[pl.ds(at, pairs), :] += rows
            col_at = pl.multiple_of((block + offset) * (8 * step), 8 * step)
            col_all[pl.ds(col_at, 8 * step), :] += jnp.concatenate(cols, axis=0)
            bias_all[pl.ds(pl.multiple_of(offset * 8, 8), 8), :] += sum(cols)
        lhs = jnp.concatenate([first.T, ones], axis=0)
        outer_all[...] += jnp.dot(lhs, slope, preferred_element_type=F32)

    def body(pass_at, _):
        turn = 2 * pass_at
        backward(jnp.maximum(turn - 1, 0), first_1, slope_1)
        forward(turn, first_0, slope_0)
        backward(turn, first_0, slope_0)
        forward(turn + 1, first_1, slope_1)
        return 0

    passes = lax.div(count + 2 * BATCH - 1, 2 * BATCH)
    lax.fori_loop(0, passes, body, 0)
    backward(jnp.maximum(2 * passes - 1, 0), first_1, slope_1)

    flat = [(pred_all[group] * float(width)).T for group in range(groups)]
    flat = jnp.concatenate(flat, axis=0).astype(BF16)
    for chip in range(chips):
        pred_ref[chip] = flat[chip * 2 * slots * step : (chip + 1) * 2 * slots * step]
    def folded(ref, count):
        sums = [
            jnp.sum(ref[8 * k : 8 * k + 8, :], axis=0, keepdims=True) for k in range(count)
        ]
        sums = jnp.concatenate(sums, axis=0)
        return sums[:, :width] + sums[:, width:]

    col = folded(col_all, col_all.shape[0] // 8)
    bias = folded(bias_all, 8)
    outer = outer_all[:width, :width] + outer_all[width : 2 * width, width:]
    sum_d = outer_all[2 * width : 2 * width + 1, :width] + outer_all[2 * width : 2 * width + 1, width:]
    line = lax.broadcasted_iota(jnp.int32, bias.shape, 0)
    sum_out = jnp.sum(w * outer, axis=0, keepdims=True) + b_pair * sum_d
    vectors = jnp.where(line == 5, sum_d * w_out, bias)
    vectors = jnp.where(line == 6, sum_out, vectors)
    outer = outer * w_out
    high = vectors.astype(BF16).astype(F32)
    rest = (high, vectors - high)
    col_low = col.astype(BF16)
    rows = []
    for block in range(blocks):
        here = row_all[block * pairs : (block + 1) * pairs, :].astype(BF16)
        rows += [here[:, :width], here[:, width:]]
    embs = [cols_ref[...], next_ref[...]]
    contract = (((0,), (0,)), ((), ()))
    grads = (
        lax.dot_general(
            jnp.concatenate(rows, axis=0), emb_ref[...], contract, preferred_element_type=F32
        ).astype(BF16),
        lax.dot_general(
            col_low, jnp.concatenate(embs, axis=0), contract, preferred_element_type=F32
        ).astype(BF16),
    )
    def message(share):
        side, at = share // chips, share % chips
        grad = grads[side][:, at // 2 * width : (at // 2 + 1) * width]
        more = rest[share] if share < 2 else jnp.zeros_like(high)
        small = jnp.concatenate([outer[8 * share : 8 * share + 8], more], axis=0)
        return jnp.concatenate(
            [rows[share], grad[at % 2 * pairs : (at % 2 + 1) * pairs], small.astype(BF16)], axis=0
        )

    for chip in range(chips):
        even, odd = message(2 * chip), message(2 * chip + 1)
        keep_ref[chip] = jnp.where(core == 0, even, odd)
        send_ref[chip] = jnp.where(core == 0, odd, even)
    col_ref[...] = col[:own]
    edge_ref[...] = col_low[own:]


def share_kernel(sum_ref, edge_ref, row_ref, message_ref, mine_ref, send_ref):
    core = place() & 1
    chips, _, width = sum_ref.shape
    pairs = width // 2
    head = width + 16
    slot_rows = mine_ref.shape[1]
    total = jnp.zeros((head, width), F32)
    for chip in range(chips):
        total = total + sum_ref[chip, :head, :].astype(F32)
        first = sum_ref[chip, head : head + slot_rows, :]
        second = sum_ref[chip, head + slot_rows :, :]
        mine_ref[chip] = jnp.where(core == 0, first, second)
        send_ref[chip] = jnp.where(core == 0, second, first)
    total = total.astype(BF16)
    row_ref[...] = total[:pairs]
    for bin_at in range(message_ref.shape[0]):
        message_ref[bin_at, : head - pairs, :] = total[pairs:]
        message_ref[bin_at, head - pairs :, :] = edge_ref[...]


def total_kernel(met_ref, row_ref, col_ref, message_ref):
    here = lax.axis_index("bin")
    bins = met_ref.shape[0]
    width = row_ref.shape[1]
    pairs = row_ref.shape[0]
    edge = col_ref.shape[0] // 2
    count = met_ref.shape[1] - edge
    total = jnp.zeros((count, width), F32)
    before = jnp.zeros((edge, width), F32)
    for bin_at in range(bins):
        total = total + met_ref[bin_at, :count, :].astype(F32)
        near = met_ref[bin_at, count:, :].astype(F32)
        before = jnp.where(here == bin_at + 1, near, before)
    total = total.astype(BF16)
    col = col_ref[...]
    top = (col[:edge] + before).astype(BF16)
    low = col[edge:].astype(BF16)
    for chip in range(message_ref.shape[0]):
        message_ref[chip, :pairs, :] = row_ref[...]
        message_ref[chip, pairs : pairs + count, :] = total
        message_ref[chip, pairs + count : pairs + count + edge, :] = top
        message_ref[chip, pairs + count + edge :, :] = low


def last_kernel(
    mine_ref, other_ref, pred_mine, pred_other, left_w_ref, right_w_ref,
    pred_hbm, emb_hbm, left_hbm, right_hbm, bias_hbm, w_hbm, b_hbm, out_hbm,
    pred_ref, emb_ref, left_ref, right_ref, bias_ref, w_ref, b_ref, out_ref,
    both_ref, flat_ref, col_ref, flip_ref, sems,
):
    core = place() & 1
    width = left_w_ref.shape[1]
    pairs = width // 2
    chips = mine_ref.shape[0]
    slots = pred_ref.shape[0]
    step = width // (2 * chips)
    copies = []

    def leave(source, target):
        copies.append(pltpu.make_async_copy(source, target, sems.at[len(copies)]))
        copies[-1].start()

    lows = []
    for share in range(2 * chips):
        block = jnp.where(core == share % 2, mine_ref[share // 2], other_ref[share // 2])
        both_ref[share * pairs : (share + 1) * pairs, :width] = block[:pairs]
        block = block.astype(F32)
        for k in range(col_ref.shape[0] // width):
            to = k * width + share * step
            at = width + 16 + k * step
            col_ref[to : to + step, :] = block[at : at + step]
        flat_ref[share * pairs : (share + 1) * pairs, :] = block[pairs:width]
        small = block[width : width + 16]
        w_ref[8 * share : 8 * share + 8, :] = small[:8]
        lows.append(small[8:])
    both_ref[:, width:] = col_ref[...].astype(BF16)
    weights = jnp.concatenate([left_w_ref[...], right_w_ref[...]], axis=1)
    part = 2 * width
    for k in range(both_ref.shape[0] // part):
        rows = pl.ds(k * part, part)
        emb_ref[rows, :] = lax.dot_general(
            both_ref[rows, :], weights, (((1,), (1,)), ((), ())), preferred_element_type=F32
        ).astype(BF16)
        leave(emb_ref.at[rows, :], emb_hbm.at[rows, :])
    for side, (grad_ref, grad_hbm) in enumerate(((left_ref, left_hbm), (right_ref, right_hbm))):
        for k in range(chips // 2):
            at = (side * chips // 2 + k) * width
            grad_ref[k * width : (k + 1) * width, :] = flat_ref[at : at + width, :].T
        leave(grad_ref, grad_hbm)
    vectors = lows[0] + lows[1]
    bias_ref[...] = vectors[:5]
    b_ref[...] = vectors[5:6]
    out_ref[...] = vectors[6:7]
    for source, target in ((w_ref, w_hbm), (bias_ref, bias_hbm), (b_ref, b_hbm), (out_ref, out_hbm)):
        leave(source, target)
    for chip in range(chips):
        for ref, side in ((pred_mine, core), (pred_other, 1 - core)):
            block = ref[chip].astype(F32)
            to = pl.multiple_of((2 * chip + side) * step, step)
            for slot in range(slots):
                flip_ref[slot, pl.ds(to, step), :] = block[slot * step : (slot + 1) * step]
    for slot in range(slots):
        pred_ref[slot] = flip_ref[slot].T.astype(BF16)
    leave(pred_ref, pred_hbm)
    for copy in copies:
        copy.wait()


def shape(*dims, dtype=F32):
    return jax.ShapeDtypeStruct(dims, dtype)


def call(kernel, outs, scratch, *args, out_space=VMEM, cost=None):
    return pl.pallas_call(
        kernel,
        out_shape=outs,
        in_specs=[VMEM] * len(args),
        out_specs=(out_space,) * len(outs),
        scratch_shapes=scratch,
        cost_estimate=cost,
        compiler_params=pltpu.CompilerParams(vmem_limit_bytes=32 * 1024 * 1024),
    )(*args)


def swapped(block, axis, bits):
    return lax.ppermute(block, axis, [(i, i ^ bits) for i in range(lax.axis_size(axis))])


def across(block, axis, groups=None):
    return lax.all_to_all(block, axis, 0, 0, axis_index_groups=groups, tiled=True)


def per_device(embeddings, w_left, w_right, pair_bias, w_pair, b_pair, w_out, tile_list, target):
    tile = place()
    core = lax.rem(tile, 2)
    slots, width = target.shape[2:4]
    rows, features = embeddings.shape
    blocks = rows // width
    pairs = width // 2
    shares = lax.axis_size("tile")
    chips = shares // 2
    step = width // shares
    part = rows // shares
    edge = part // 2
    target = target[0, 0]
    lists = jnp.transpose(tile_list, (0, 3, 1, 2)).reshape(3, 1, slots)

    emb_cols = lax.dynamic_slice_in_dim(
        embeddings.reshape(blocks, shares, step, features), tile, 1, 1
    ).reshape(part, features)
    target_other = swapped(target, "tile", 1)
    lists_other = swapped(lists, "tile", 1)
    bins = lax.axis_size("bin")
    emb_next = lax.ppermute(emb_cols[:edge], "bin", [(k + 1, k) for k in range(bins - 1)])
    consts = jnp.concatenate(
        [pair_bias, b_pair[None], w_out[None], jnp.zeros((1, width), F32)], axis=0
    )
    (target_send,) = call(
        split_kernel,
        (shape(chips, 2 * (slots + 1) * step, width, dtype=BF16),),
        [pltpu.VMEM((2 * slots, width, width), F32), pltpu.VMEM((2 * step, width), F32)],
        lists, lists_other, target, target_other,
    )
    groups = [list(range(k, shares, 2)) for k in range(2)]
    target_send, consts = lax.optimization_barrier((target_send, consts))
    target_all = across(target_send, "tile", groups)

    chunk = (BATCH * step * pairs, 2 * width)
    grouped = (slots * shares * step // width + 1, width, width)
    double = shape(2 * width, 2 * width, dtype=BF16)
    ready = call(
        ready_kernel,
        (
            shape(rows // 2, 2 * width),
            shape(part, width),
            double,
            double,
            double,
            shape(8, 2 * width),
        ),
        [pltpu.VMEM((rows, width), F32)],
        embeddings, w_left, w_right, consts, w_pair,
        cost=pl.CostEstimate(flops=1, bytes_accessed=1, transcendentals=0),
    )
    half = shape(chips, width + 16, width, dtype=BF16)
    sums, sums_send, pred, col, col_edge = call(
        pair_kernel,
        (
            half,
            half,
            shape(chips, 2 * slots * step, width, dtype=BF16),
            shape(part, width),
            shape(edge, width, dtype=BF16),
        ),
        [
            pltpu.SMEM((3, slots * shares + 2 * BATCH), jnp.int32),
            pltpu.SMEM((3, shares, width), jnp.int32),
            pltpu.SemaphoreType.DMA,
            pltpu.VMEM((3, shares, width), jnp.int32),
            pltpu.VMEM(grouped, F32),
            pltpu.VMEM(grouped, F32),
            pltpu.VMEM((rows // 2, 2 * width), F32),
            pltpu.VMEM((8 * (part + edge), 2 * width), F32),
            pltpu.VMEM((2 * width + 16, 2 * width), F32),
            pltpu.VMEM((64, 2 * width), F32),
            pltpu.VMEM((part + edge, width), F32),
            pltpu.VMEM(chunk, BF16),
            pltpu.VMEM(chunk, BF16),
            pltpu.VMEM(chunk, BF16),
            pltpu.VMEM(chunk, BF16),
        ],
        embeddings, emb_cols, emb_next, w_right, consts, target_all, w_pair, *ready,
    )
    sums = (sums.astype(F32) + swapped(sums_send, "tile", 1).astype(F32)).astype(BF16)
    sums = across(jnp.concatenate([sums, pred], axis=1), "tile", groups)
    row, weight, pred_mine, pred_send = call(
        share_kernel,
        (
            shape(pairs, width, dtype=BF16),
            shape(bins, pairs + 16 + edge, width, dtype=BF16),
            shape(chips, slots * step, width, dtype=BF16),
            shape(chips, slots * step, width, dtype=BF16),
        ),
        [], sums, col_edge,
    )
    weight = across(weight, "bin")
    (mine,) = call(
        total_kernel,
        (shape(chips, width + 16 + part, width, dtype=BF16),),
        [], weight, row, col,
    )
    mine = across(mine, "tile", groups)
    mine, pred_send = lax.optimization_barrier((mine, pred_send))
    pred_other = swapped(pred_send, "tile", 1)
    other = swapped(mine, "tile", 1)
    outs = (
        shape(slots, width, width, dtype=BF16),
        shape(rows, features, dtype=BF16),
        shape(features, width),
        shape(features, width),
        shape(5, width),
        shape(width, width),
        shape(1, width),
        shape(1, width),
    )
    outs = call(
        last_kernel,
        outs,
        [pltpu.VMEM(out.shape, out.dtype) for out in outs]
        + [
            pltpu.VMEM((rows, 2 * width), BF16),
            pltpu.VMEM((2 * features, width), F32),
            pltpu.VMEM((rows, width), F32),
            pltpu.VMEM((slots, width, width), F32),
            pltpu.SemaphoreType.DMA((rows // (2 * width) + 7,)),
        ],
        mine, other, pred_mine, pred_other, w_left, w_right, out_space=HBM,
    )
    return (outs[0][None, None], *outs[1:6], outs[6][0], outs[7][0])


def solution(mesh):
    return jax.shard_map(
        per_device,
        mesh=mesh,
        in_specs=(
            P("bin", None),
            P(),
            P(),
            P(),
            P(),
            P(),
            P(),
            P("bin", "tile", None, None),
            P("bin", "tile", None, None, None),
        ),
        out_specs=(
            P("bin", "tile", None, None, None),
            P("bin", None),
            P(),
            P(),
            P(),
            P(),
            P(),
            P(),
        ),
        check_vma=False,
    )
```

```python
import jax
import jax.numpy as jnp
from jax import lax
from jax.experimental import pallas as pl
from jax.experimental.pallas import tpu as pltpu
from jax.sharding import PartitionSpec as P

F32 = jnp.float32
BF16 = jnp.bfloat16
BATCH = 2
NEVER = -1e38
TINY = 1e-30
VMEM = pl.BlockSpec(memory_space=pltpu.VMEM)
HBM = pl.BlockSpec(memory_space=pl.ANY)


def place():
    return lax.axis_index("tile")


def split_kernel(
    list_mine, list_other, target_mine, target_other, send_ref, flip_ref, listed_ref
):
    core = place() & 1
    slots, width, _ = target_mine.shape
    chips = send_ref.shape[0]
    step = width // (2 * chips)
    listed_ref[...] = jnp.zeros_like(listed_ref)
    for side in range(2):
        mine = core == side
        for k in range(3):
            listed_ref[3 * side + k : 3 * side + k + 1, :slots] = jnp.where(
                mine, list_mine[k], list_other[k]
            ).astype(F32)
        for slot in range(slots):
            block = jnp.where(mine, target_mine[slot], target_other[slot]).astype(F32)
            flip_ref[side * slots + slot] = (block * (1.0 / width)).T
    listed = listed_ref[...].astype(BF16)
    for chip in range(chips):
        for side in range(2):
            at = (2 * chip + core) * step
            at = pl.multiple_of(at, step)
            pieces = [
                flip_ref[side * slots + slot, pl.ds(at, step), :] for slot in range(slots)
            ]
            send_ref[chip, side * slots * step : (side + 1) * slots * step, :] = jnp.concatenate(
                pieces, axis=0
            ).astype(BF16)
        send_ref[chip, 2 * slots * step :, :] = listed


def pair_kernel(
    emb_ref, cols_ref, next_ref, left_w_ref, right_w_ref, const_ref, target_ref, w_ref,
    keep_ref, send_ref, col_ref, edge_ref,
    table, lists, list_sem, list_all, left_ref, full_ref, right_all, target_all, pred_all, row_all, col_all,
    outer_all, bias_all, w_two, out_two, back_two, b_two, scale_two, first_0, first_1, slope_0, slope_1,
):
    tile = place()
    width = w_ref.shape[0]
    pairs = width // 2
    blocks = emb_ref.shape[0] // width
    chips = target_ref.shape[0]
    shares = 2 * chips
    step = width // shares
    slots = target_ref.shape[1] // (2 * step) - 1
    core = tile & 1
    groups = target_all.shape[0] - 1
    spread_bits = (width // step).bit_length() - 1

    for chip in range(chips):
        rows = target_ref[chip, 2 * slots * step :, :].astype(F32).astype(jnp.int32)
        for side in range(2):
            for k in range(3):
                at = 3 * side + k
                list_all[k, 2 * chip + side : 2 * chip + side + 1] = rows[at : at + 1]
    copy = pltpu.make_async_copy(list_all, lists, list_sem)
    copy.start()

    w = w_ref[...].astype(F32)
    w_out = const_ref[6:7, :]
    b_pair = const_ref[5:6, :]
    size = jnp.abs(w_out)
    power = jnp.exp2(jnp.floor(jnp.log2(jnp.maximum(size, TINY))))
    power = jnp.where(size < TINY, 0.0, power).astype(BF16).astype(F32)
    power = jnp.where(w_out < 0.0, -power, power)
    ratio = jnp.where(size < TINY, 1.0, w_out / jnp.where(size < TINY, 1.0, power))
    back = (w * w_out).T.astype(BF16)
    spread = jnp.broadcast_to(power * (1.0 / width), (width, width)).T.astype(BF16)
    for ref, block in ((w_two, w_ref[...]), (out_two, spread), (back_two, back)):
        ref[...] = jnp.zeros_like(ref)
        ref[:width, :width] = block
        ref[width:, width:] = block
    scale_two[:, :width] = ratio
    scale_two[:, width:] = ratio
    b_two[:, :width] = b_pair
    b_two[:, width:] = b_pair
    weights = jnp.concatenate([left_w_ref[...], right_w_ref[...]], axis=1)
    for block in range(0, blocks, 2):
        both = jnp.dot(
            emb_ref[block * width : (block + 2) * width, :],
            weights,
            preferred_element_type=F32,
        ).astype(BF16).astype(F32)
        for k in range(2):
            left = both[k * width : (k + 1) * width, :width]
            at = (block + k) * pairs
            left_ref[at : at + pairs, :width] = left[:pairs]
            left_ref[at : at + pairs, width:] = left[pairs:]
        full_ref[block * width : (block + 2) * width, :] = both[:, width:]
    own = blocks * step
    for block in range(blocks):
        at = pl.multiple_of(block * width + tile * step, step)
        right_all[block * step : (block + 1) * step, :] = full_ref[pl.ds(at, step), :]
    right_next = jnp.dot(next_ref[...], right_w_ref[...], preferred_element_type=F32)
    right_all[own:, :] = right_next.astype(BF16).astype(F32)
    rows = [target_ref[chip, : 2 * slots * step, :].astype(F32) for chip in range(chips)]
    rows = jnp.concatenate(rows, axis=0)
    for group in range(groups):
        target_all[group] = rows[group * width : (group + 1) * width].T
    target_all[groups] = jnp.zeros((width, width), F32)
    for ref in (pred_all, row_all, col_all, outer_all, bias_all, first_1, slope_1):
        ref[...] = jnp.zeros_like(ref)
    lane = lax.broadcasted_iota(jnp.int32, (width, width), 1)
    ones = jnp.ones((16, BATCH * step * pairs), BF16)

    copy.wait()
    count = jnp.int32(0)
    for share in range(shares):
        for slot in range(slots):
            offset = lists[2, share, slot]
            table[0, count] = lists[0, share, slot] & (blocks - 1)
            table[1, count] = offset
            table[2, count] = share * slots + slot
            count = count + jnp.where(offset >= 0, 1, 0)
    for spare in range(2 * BATCH):
        table[0, count + spare] = 0
        table[1, count + spare] = 0
        table[2, count + spare] = shares * slots

    def forward(turn, first_ref, slope_ref):
        pre = []
        wanted = []
        shifts = []
        floors = []
        for k in range(BATCH):
            job = turn * BATCH + k
            block, offset, slot = table[0, job], table[1, job], table[2, job]
            shift = (slot & (width // step - 1)) * step
            shifts.append((slot >> spread_bits, shift))
            at = pl.multiple_of(block * pairs, pairs)
            col_at = pl.multiple_of((block + offset) * step, step)
            right = right_all[pl.ds(col_at, step), :] + const_ref[pl.ds(offset, 1), :]
            right = jnp.concatenate([right, right], axis=1)
            left = left_ref[pl.ds(at, pairs), :]
            pre += [left + right[j : j + 1, :] for j in range(step)]
            target = pltpu.roll(
                target_all[slot >> spread_bits], (width - shift) & (width - 1), 1
            )
            for j in range(step):
                want = jnp.broadcast_to(target[:, j : j + 1], (width, width))
                wanted.append(jnp.concatenate([want[:pairs], want[pairs:]], axis=1))
            floor = jnp.where(job < count, b_two[...], jnp.full((1, 2 * width), NEVER, F32))
            floors.append(jnp.broadcast_to(floor, (step * pairs, 2 * width)))
        first = jnp.maximum(jnp.concatenate(pre, axis=0).astype(BF16), 0.0)
        first_ref[...] = first
        act = jnp.dot(first, w_two[...], preferred_element_type=F32)
        act = act + jnp.concatenate(floors, axis=0)
        second = jnp.maximum((act * scale_two[...]).astype(BF16), 0.0)
        contact = jnp.dot(second, out_two[...], preferred_element_type=F32)
        slope = (contact - jnp.concatenate(wanted, axis=0)).astype(BF16)
        slope_ref[...] = jnp.where(second > 0, slope, jnp.zeros_like(slope))
        for k, (group, shift) in enumerate(shifts):
            found = jnp.zeros((width, width), F32)
            for j in range(step):
                here = contact[(k * step + j) * pairs : (k * step + j + 1) * pairs]
                here = jnp.concatenate([here[:, :width], here[:, width:]], axis=0)
                found = jnp.where(lane == j, here, found)
            mine = (lane >= shift) & (lane < shift + step)
            pred_all[group] = jnp.where(mine, pltpu.roll(found, shift, 1), pred_all[group])

    def backward(turn, first_ref, slope_ref):
        first = first_ref[...]
        slope = slope_ref[...]
        back = jnp.dot(slope, back_two[...], preferred_element_type=F32)
        back = jnp.where(first.astype(F32) > 0.0, back, 0.0)
        for k in range(BATCH):
            job = turn * BATCH + k
            block, offset = table[0, job], table[1, job]
            at = pl.multiple_of(block * pairs, pairs)
            rows = jnp.zeros((pairs, 2 * width), F32)
            cols = []
            for j in range(step):
                here = back[(k * step + j) * pairs : (k * step + j + 1) * pairs]
                rows = rows + here
                cols.append(sum(here[g : g + 8] for g in range(0, pairs, 8)))
            row_all[pl.ds(at, pairs), :] += rows
            col_at = pl.multiple_of((block + offset) * (8 * step), 8 * step)
            col_all[pl.ds(col_at, 8 * step), :] += jnp.concatenate(cols, axis=0)
            bias_all[pl.ds(pl.multiple_of(offset * 8, 8), 8), :] += sum(cols)
        lhs = jnp.concatenate([first.T, ones], axis=0)
        outer_all[...] += jnp.dot(lhs, slope, preferred_element_type=F32)

    def body(pass_at, _):
        turn = 2 * pass_at
        backward(jnp.maximum(turn - 1, 0), first_1, slope_1)
        forward(turn, first_0, slope_0)
        backward(turn, first_0, slope_0)
        forward(turn + 1, first_1, slope_1)
        return 0

    passes = lax.div(count + 2 * BATCH - 1, 2 * BATCH)
    lax.fori_loop(0, passes, body, 0)
    backward(jnp.maximum(2 * passes - 1, 0), first_1, slope_1)

    flat = [(pred_all[group] * float(width)).T for group in range(groups)]
    flat = jnp.concatenate(flat, axis=0).astype(BF16)
    for chip in range(chips):
        at = chip * 2 * slots * step
        even = flat[at : at + slots * step]
        odd = flat[at + slots * step : at + 2 * slots * step]
        keep_ref[chip, width + 16 :, :] = jnp.where(core == 0, even, odd)
        send_ref[chip, width + 16 :, :] = jnp.where(core == 0, odd, even)
    def folded(ref, count):
        sums = [
            jnp.sum(ref[8 * k : 8 * k + 8, :], axis=0, keepdims=True) for k in range(count)
        ]
        sums = jnp.concatenate(sums, axis=0)
        return sums[:, :width] + sums[:, width:]

    col = folded(col_all, col_all.shape[0] // 8)
    bias = folded(bias_all, 8)
    outer = outer_all[:width, :width] + outer_all[width : 2 * width, width:]
    sum_d = outer_all[2 * width : 2 * width + 1, :width] + outer_all[2 * width : 2 * width + 1, width:]
    line = lax.broadcasted_iota(jnp.int32, bias.shape, 0)
    sum_out = jnp.sum(w * outer, axis=0, keepdims=True) + b_pair * sum_d
    vectors = jnp.where(line == 5, sum_d * w_out, bias)
    vectors = jnp.where(line == 6, sum_out, vectors)
    outer = outer * w_out
    high = vectors.astype(BF16).astype(F32)
    rest = (high, vectors - high)
    col_low = col.astype(BF16)
    rows = []
    for block in range(blocks):
        here = row_all[block * pairs : (block + 1) * pairs, :].astype(BF16)
        rows += [here[:, :width], here[:, width:]]
    embs = [cols_ref[...], next_ref[...]]
    contract = (((0,), (0,)), ((), ()))
    grads = (
        lax.dot_general(
            jnp.concatenate(rows, axis=0), emb_ref[...], contract, preferred_element_type=F32
        ).astype(BF16),
        lax.dot_general(
            col_low, jnp.concatenate(embs, axis=0), contract, preferred_element_type=F32
        ).astype(BF16),
    )
    def message(share):
        side, at = share // chips, share % chips
        grad = grads[side][:, at // 2 * width : (at // 2 + 1) * width]
        more = rest[share] if share < 2 else jnp.zeros_like(high)
        small = jnp.concatenate([outer[8 * share : 8 * share + 8], more], axis=0)
        return jnp.concatenate(
            [rows[share], grad[at % 2 * pairs : (at % 2 + 1) * pairs], small.astype(BF16)], axis=0
        )

    for chip in range(chips):
        even, odd = message(2 * chip), message(2 * chip + 1)
        keep_ref[chip, : width + 16, :] = jnp.where(core == 0, even, odd)
        send_ref[chip, : width + 16, :] = jnp.where(core == 0, odd, even)
    col_ref[...] = col[:own]
    edge_ref[...] = col_low[own:]


def share_kernel(sum_ref, edge_ref, row_ref, message_ref):
    chips, _, width = sum_ref.shape
    pairs = width // 2
    head = width + 16
    total = jnp.zeros((head, width), F32)
    for chip in range(chips):
        total = total + sum_ref[chip, :head, :].astype(F32)
    total = total.astype(BF16)
    row_ref[...] = total[:pairs]
    for bin_at in range(message_ref.shape[0]):
        message_ref[bin_at, : head - pairs, :] = total[pairs:]
        message_ref[bin_at, head - pairs :, :] = edge_ref[...]


def total_kernel(met_ref, row_ref, col_ref, message_ref):
    here = lax.axis_index("bin")
    bins = met_ref.shape[0]
    width = row_ref.shape[1]
    pairs = row_ref.shape[0]
    edge = col_ref.shape[0] // 2
    count = met_ref.shape[1] - edge
    total = jnp.zeros((count, width), F32)
    before = jnp.zeros((edge, width), F32)
    for bin_at in range(bins):
        total = total + met_ref[bin_at, :count, :].astype(F32)
        near = met_ref[bin_at, count:, :].astype(F32)
        before = jnp.where(here == bin_at + 1, near, before)
    total = total.astype(BF16)
    col = col_ref[...]
    top = (col[:edge] + before).astype(BF16)
    low = col[edge:].astype(BF16)
    for chip in range(message_ref.shape[0]):
        message_ref[chip, :pairs, :] = row_ref[...]
        message_ref[chip, pairs : pairs + count, :] = total
        message_ref[chip, pairs + count : pairs + count + edge, :] = top
        message_ref[chip, pairs + count + edge :, :] = low


def last_kernel(
    mine_ref, other_ref, sum_ref, left_w_ref, right_w_ref,
    pred_hbm, emb_hbm, left_hbm, right_hbm, bias_hbm, w_hbm, b_hbm, out_hbm,
    pred_ref, emb_ref, left_ref, right_ref, bias_ref, w_ref, b_ref, out_ref,
    both_ref, flat_ref, col_ref, flip_ref, sems,
):
    core = place() & 1
    width = left_w_ref.shape[1]
    pairs = width // 2
    chips = mine_ref.shape[0]
    slots = pred_ref.shape[0]
    step = width // (2 * chips)
    copies = []

    def leave(source, target):
        copies.append(pltpu.make_async_copy(source, target, sems.at[len(copies)]))
        copies[-1].start()

    lows = []
    for share in range(2 * chips):
        block = jnp.where(core == share % 2, mine_ref[share // 2], other_ref[share // 2])
        both_ref[share * pairs : (share + 1) * pairs, :width] = block[:pairs]
        block = block.astype(F32)
        for k in range(col_ref.shape[0] // width):
            to = k * width + share * step
            at = width + 16 + k * step
            col_ref[to : to + step, :] = block[at : at + step]
        flat_ref[share * pairs : (share + 1) * pairs, :] = block[pairs:width]
        small = block[width : width + 16]
        w_ref[8 * share : 8 * share + 8, :] = small[:8]
        lows.append(small[8:])
    both_ref[:, width:] = col_ref[...].astype(BF16)
    weights = jnp.concatenate([left_w_ref[...], right_w_ref[...]], axis=1)
    part = 2 * width
    for k in range(both_ref.shape[0] // part):
        rows = pl.ds(k * part, part)
        emb_ref[rows, :] = lax.dot_general(
            both_ref[rows, :], weights, (((1,), (1,)), ((), ())), preferred_element_type=F32
        ).astype(BF16)
        leave(emb_ref.at[rows, :], emb_hbm.at[rows, :])
    for side, (grad_ref, grad_hbm) in enumerate(((left_ref, left_hbm), (right_ref, right_hbm))):
        for k in range(chips // 2):
            at = (side * chips // 2 + k) * width
            grad_ref[k * width : (k + 1) * width, :] = flat_ref[at : at + width, :].T
        leave(grad_ref, grad_hbm)
    vectors = lows[0] + lows[1]
    bias_ref[...] = vectors[:5]
    b_ref[...] = vectors[5:6]
    out_ref[...] = vectors[6:7]
    for source, target in ((w_ref, w_hbm), (bias_ref, bias_hbm), (b_ref, b_hbm), (out_ref, out_hbm)):
        leave(source, target)
    for chip in range(chips):
        for part_at, side in enumerate((core, 1 - core)):
            at = width + 16 + part_at * slots * step
            block = sum_ref[chip, at : at + slots * step, :].astype(F32)
            to = pl.multiple_of((2 * chip + side) * step, step)
            for slot in range(slots):
                flip_ref[slot, pl.ds(to, step), :] = block[slot * step : (slot + 1) * step]
    for slot in range(slots):
        pred_ref[slot] = flip_ref[slot].T.astype(BF16)
    leave(pred_ref, pred_hbm)
    for copy in copies:
        copy.wait()


def shape(*dims, dtype=F32):
    return jax.ShapeDtypeStruct(dims, dtype)


def call(kernel, outs, scratch, *args, space=None, out_space=VMEM, limit=32):
    return pl.pallas_call(
        kernel,
        out_shape=outs,
        in_specs=space or [VMEM] * len(args),
        out_specs=(out_space,) * len(outs),
        scratch_shapes=scratch,
        compiler_params=pltpu.CompilerParams(vmem_limit_bytes=limit * 1024 * 1024),
    )(*args)


def swapped(block, axis, bits):
    return lax.ppermute(block, axis, [(i, i ^ bits) for i in range(lax.axis_size(axis))])


def across(block, axis, groups=None):
    return lax.all_to_all(block, axis, 0, 0, axis_index_groups=groups, tiled=True)


def per_device(embeddings, w_left, w_right, pair_bias, w_pair, b_pair, w_out, tile_list, target):
    tile = place()
    core = lax.rem(tile, 2)
    slots, width = target.shape[2:4]
    rows, features = embeddings.shape
    blocks = rows // width
    pairs = width // 2
    shares = lax.axis_size("tile")
    chips = shares // 2
    step = width // shares
    part = rows // shares
    edge = part // 2
    target = target[0, 0]
    lists = jnp.transpose(tile_list, (0, 3, 1, 2)).reshape(3, 1, slots)

    emb_cols = lax.dynamic_slice_in_dim(
        embeddings.reshape(blocks, shares, step, features), tile, 1, 1
    ).reshape(part, features)
    target_other = swapped(target, "tile", 1)
    lists_other = swapped(lists, "tile", 1)
    bins = lax.axis_size("bin")
    emb_next = lax.ppermute(emb_cols[:edge], "bin", [(k + 1, k) for k in range(bins - 1)])
    consts = jnp.concatenate(
        [pair_bias, b_pair[None], w_out[None], jnp.zeros((1, width), F32)], axis=0
    )
    (target_send,) = call(
        split_kernel,
        (shape(chips, 2 * (slots + 1) * step, width, dtype=BF16),),
        [pltpu.VMEM((2 * slots, width, width), F32), pltpu.VMEM((2 * step, width), F32)],
        lists, lists_other, target, target_other,
    )
    groups = [list(range(k, shares, 2)) for k in range(2)]
    target_all = across(target_send, "tile", groups)

    chunk = (BATCH * step * pairs, 2 * width)
    grouped = (slots * shares * step // width + 1, width, width)
    head = width + 16
    half = shape(chips, head + slots * step, width, dtype=BF16)
    sums, sums_send, col, col_edge = call(
        pair_kernel,
        (
            half,
            half,
            shape(part, width),
            shape(edge, width, dtype=BF16),
        ),
        [
            pltpu.SMEM((3, slots * shares + 2 * BATCH), jnp.int32),
            pltpu.SMEM((3, shares, width), jnp.int32),
            pltpu.SemaphoreType.DMA,
            pltpu.VMEM((3, shares, width), jnp.int32),
            pltpu.VMEM((rows // 2, 2 * width), F32),
            pltpu.VMEM((rows, width), F32),
            pltpu.VMEM((part + edge, width), F32),
            pltpu.VMEM(grouped, F32),
            pltpu.VMEM(grouped, F32),
            pltpu.VMEM((rows // 2, 2 * width), F32),
            pltpu.VMEM((8 * (part + edge), 2 * width), F32),
            pltpu.VMEM((2 * width + 16, 2 * width), F32),
            pltpu.VMEM((64, 2 * width), F32),
            pltpu.VMEM((2 * width, 2 * width), BF16),
            pltpu.VMEM((2 * width, 2 * width), BF16),
            pltpu.VMEM((2 * width, 2 * width), BF16),
            pltpu.VMEM((1, 2 * width), F32),
            pltpu.VMEM((1, 2 * width), F32),
            pltpu.VMEM(chunk, BF16),
            pltpu.VMEM(chunk, BF16),
            pltpu.VMEM(chunk, BF16),
            pltpu.VMEM(chunk, BF16),
        ],
        embeddings, emb_cols, emb_next, w_left, w_right, consts, target_all, w_pair,
    )
    met = swapped(sums_send, "tile", 1)
    both = (sums[:, :head].astype(F32) + met[:, :head].astype(F32)).astype(BF16)
    sums = across(
        jnp.concatenate([both, sums[:, head:], met[:, head:]], axis=1), "tile", groups
    )
    row, weight = call(
        share_kernel,
        (
            shape(pairs, width, dtype=BF16),
            shape(bins, pairs + 16 + edge, width, dtype=BF16),
        ),
        [], sums, col_edge,
    )
    weight = across(weight, "bin")
    (mine,) = call(
        total_kernel,
        (shape(chips, width + 16 + part, width, dtype=BF16),),
        [], weight, row, col,
    )
    mine = across(mine, "tile", groups)
    other = swapped(mine, "tile", 1)
    outs = (
        shape(slots, width, width, dtype=BF16),
        shape(rows, features, dtype=BF16),
        shape(features, width),
        shape(features, width),
        shape(5, width),
        shape(width, width),
        shape(1, width),
        shape(1, width),
    )
    outs = call(
        last_kernel,
        outs,
        [pltpu.VMEM(out.shape, out.dtype) for out in outs]
        + [
            pltpu.VMEM((rows, 2 * width), BF16),
            pltpu.VMEM((2 * features, width), F32),
            pltpu.VMEM((rows, width), F32),
            pltpu.VMEM((slots, width, width), F32),
            pltpu.SemaphoreType.DMA((rows // (2 * width) + 7,)),
        ],
        mine, other, sums, w_left, w_right, out_space=HBM,
    )
    return (outs[0][None, None], *outs[1:6], outs[6][0], outs[7][0])


def solution(mesh):
    return jax.shard_map(
        per_device,
        mesh=mesh,
        in_specs=(
            P("bin", None),
            P(),
            P(),
            P(),
            P(),
            P(),
            P(),
            P("bin", "tile", None, None),
            P("bin", "tile", None, None, None),
        ),
        out_specs=(
            P("bin", "tile", None, None, None),
            P("bin", None),
            P(),
            P(),
            P(),
            P(),
            P(),
            P(),
        ),
        check_vma=False,
    )
```

```python
import jax
import jax.numpy as jnp
from jax import lax
from jax.experimental import pallas as pl
from jax.experimental.pallas import tpu as pltpu
from jax.sharding import PartitionSpec as P

F32 = jnp.float32
BF16 = jnp.bfloat16
BATCH = 3
NEVER = -1e38
TINY = 1e-30
VMEM = pl.BlockSpec(memory_space=pltpu.VMEM)
HBM = pl.BlockSpec(memory_space=pl.ANY)


def place():
    return lax.axis_index("tile")


def split_kernel(
    list_mine, list_other, target_mine, target_other, send_ref, flip_ref, listed_ref
):
    core = place() & 1
    slots, width, _ = target_mine.shape
    chips = send_ref.shape[0]
    step = width // (2 * chips)
    listed_ref[...] = jnp.zeros_like(listed_ref)
    for side in range(2):
        mine = core == side
        for k in range(3):
            listed_ref[3 * side + k : 3 * side + k + 1, :slots] = jnp.where(
                mine, list_mine[k], list_other[k]
            ).astype(F32)
        for slot in range(slots):
            block = jnp.where(mine, target_mine[slot], target_other[slot]).astype(F32)
            flip_ref[side * slots + slot] = (block * (1.0 / width)).T
    listed = listed_ref[...].astype(BF16)
    for chip in range(chips):
        for side in range(2):
            at = (2 * chip + core) * step
            at = pl.multiple_of(at, step)
            pieces = [
                flip_ref[side * slots + slot, pl.ds(at, step), :] for slot in range(slots)
            ]
            send_ref[chip, side * slots * step : (side + 1) * slots * step, :] = jnp.concatenate(
                pieces, axis=0
            ).astype(BF16)
        send_ref[chip, 2 * slots * step :, :] = listed


def pair_kernel(
    emb_ref, cols_ref, next_ref, left_w_ref, right_w_ref, const_ref, target_ref, w_ref,
    keep_ref, send_ref, pred_ref, col_ref, edge_ref,
    table, lists, list_sem, list_all, left_ref, full_ref, right_all, target_all, pred_all, row_all, col_all,
    outer_all, bias_all, w_two, out_two, back_two, b_two, scale_two, first_0, first_1, slope_0, slope_1,
):
    tile = place()
    width = w_ref.shape[0]
    pairs = width // 2
    blocks = emb_ref.shape[0] // width
    chips = target_ref.shape[0]
    shares = 2 * chips
    step = width // shares
    slots = target_ref.shape[1] // (2 * step) - 1
    core = tile & 1
    groups = target_all.shape[0] - 1
    spread_bits = (width // step).bit_length() - 1

    for chip in range(chips):
        rows = target_ref[chip, 2 * slots * step :, :].astype(F32).astype(jnp.int32)
        for side in range(2):
            for k in range(3):
                at = 3 * side + k
                list_all[k, 2 * chip + side : 2 * chip + side + 1] = rows[at : at + 1]
    copy = pltpu.make_async_copy(list_all, lists, list_sem)
    copy.start()

    w = w_ref[...].astype(F32)
    w_out = const_ref[6:7, :]
    b_pair = const_ref[5:6, :]
    size = jnp.abs(w_out)
    power = jnp.exp2(jnp.floor(jnp.log2(jnp.maximum(size, TINY))))
    power = jnp.where(size < TINY, 0.0, power).astype(BF16).astype(F32)
    power = jnp.where(w_out < 0.0, -power, power)
    ratio = jnp.where(size < TINY, 1.0, w_out / jnp.where(size < TINY, 1.0, power))
    back = (w * w_out).T.astype(BF16)
    spread = jnp.broadcast_to(power * (1.0 / width), (width, width)).T.astype(BF16)
    for ref, block in ((w_two, w_ref[...]), (out_two, spread), (back_two, back)):
        ref[...] = jnp.zeros_like(ref)
        ref[:width, :width] = block
        ref[width:, width:] = block
    scale_two[:, :width] = ratio
    scale_two[:, width:] = ratio
    b_two[:, :width] = b_pair
    b_two[:, width:] = b_pair
    weights = jnp.concatenate([left_w_ref[...], right_w_ref[...]], axis=1)
    for block in range(0, blocks, 2):
        both = jnp.dot(
            emb_ref[block * width : (block + 2) * width, :],
            weights,
            preferred_element_type=F32,
        ).astype(BF16).astype(F32)
        for k in range(2):
            left = both[k * width : (k + 1) * width, :width]
            at = (block + k) * pairs
            left_ref[at : at + pairs, :width] = left[:pairs]
            left_ref[at : at + pairs, width:] = left[pairs:]
        full_ref[block * width : (block + 2) * width, :] = both[:, width:]
    own = blocks * step
    for block in range(blocks):
        at = pl.multiple_of(block * width + tile * step, step)
        right_all[block * step : (block + 1) * step, :] = full_ref[pl.ds(at, step), :]
    right_next = jnp.dot(next_ref[...], right_w_ref[...], preferred_element_type=F32)
    right_all[own:, :] = right_next.astype(BF16).astype(F32)
    rows = [target_ref[chip, : 2 * slots * step, :].astype(F32) for chip in range(chips)]
    rows = jnp.concatenate(rows, axis=0)
    for group in range(groups):
        target_all[group] = rows[group * width : (group + 1) * width].T
    target_all[groups] = jnp.zeros((width, width), F32)
    for ref in (pred_all, row_all, col_all, outer_all, bias_all, first_1, slope_1):
        ref[...] = jnp.zeros_like(ref)
    lane = lax.broadcasted_iota(jnp.int32, (width, width), 1)
    ones = jnp.ones((16, BATCH * step * pairs), BF16)

    copy.wait()
    count = jnp.int32(0)
    for share in range(shares):
        for slot in range(slots):
            offset = lists[2, share, slot]
            table[0, count] = lists[0, share, slot] & (blocks - 1)
            table[1, count] = offset
            table[2, count] = share * slots + slot
            count = count + jnp.where(offset >= 0, 1, 0)
    for spare in range(2 * BATCH):
        table[0, count + spare] = 0
        table[1, count + spare] = 0
        table[2, count + spare] = shares * slots

    def forward(turn, first_ref, slope_ref):
        pre = []
        wanted = []
        shifts = []
        floors = []
        for k in range(BATCH):
            job = turn * BATCH + k
            block, offset, slot = table[0, job], table[1, job], table[2, job]
            shift = (slot & (width // step - 1)) * step
            shifts.append((slot >> spread_bits, shift))
            at = pl.multiple_of(block * pairs, pairs)
            col_at = pl.multiple_of((block + offset) * step, step)
            right = right_all[pl.ds(col_at, step), :] + const_ref[pl.ds(offset, 1), :]
            right = jnp.concatenate([right, right], axis=1)
            left = left_ref[pl.ds(at, pairs), :]
            pre += [left + right[j : j + 1, :] for j in range(step)]
            target = pltpu.roll(
                target_all[slot >> spread_bits], (width - shift) & (width - 1), 1
            )
            for j in range(step):
                want = jnp.broadcast_to(target[:, j : j + 1], (width, width))
                wanted.append(jnp.concatenate([want[:pairs], want[pairs:]], axis=1))
            floor = jnp.where(job < count, b_two[...], jnp.full((1, 2 * width), NEVER, F32))
            floors.append(jnp.broadcast_to(floor, (step * pairs, 2 * width)))
        first = jnp.maximum(jnp.concatenate(pre, axis=0).astype(BF16), 0.0)
        first_ref[...] = first
        act = jnp.dot(first, w_two[...], preferred_element_type=F32)
        act = act + jnp.concatenate(floors, axis=0)
        second = jnp.maximum((act * scale_two[...]).astype(BF16), 0.0)
        contact = jnp.dot(second, out_two[...], preferred_element_type=F32)
        slope = (contact - jnp.concatenate(wanted, axis=0)).astype(BF16)
        slope_ref[...] = jnp.where(second > 0, slope, jnp.zeros_like(slope))
        for k, (group, shift) in enumerate(shifts):
            found = jnp.zeros((width, width), F32)
            for j in range(step):
                here = contact[(k * step + j) * pairs : (k * step + j + 1) * pairs]
                here = jnp.concatenate([here[:, :width], here[:, width:]], axis=0)
                found = jnp.where(lane == j, here, found)
            mine = (lane >= shift) & (lane < shift + step)
            pred_all[group] = jnp.where(mine, pltpu.roll(found, shift, 1), pred_all[group])

    def backward(turn, first_ref, slope_ref):
        first = first_ref[...]
        slope = slope_ref[...]
        back = jnp.dot(slope, back_two[...], preferred_element_type=F32)
        back = jnp.where(first.astype(F32) > 0.0, back, 0.0)
        for k in range(BATCH):
            job = turn * BATCH + k
            block, offset = table[0, job], table[1, job]
            at = pl.multiple_of(block * pairs, pairs)
            rows = jnp.zeros((pairs, 2 * width), F32)
            cols = []
            for j in range(step):
                here = back[(k * step + j) * pairs : (k * step + j + 1) * pairs]
                rows = rows + here
                cols.append(sum(here[g : g + 8] for g in range(0, pairs, 8)))
            row_all[pl.ds(at, pairs), :] += rows
            col_at = pl.multiple_of((block + offset) * (8 * step), 8 * step)
            col_all[pl.ds(col_at, 8 * step), :] += jnp.concatenate(cols, axis=0)
            bias_all[pl.ds(pl.multiple_of(offset * 8, 8), 8), :] += sum(cols)
        lhs = jnp.concatenate([first.T, ones], axis=0)
        outer_all[...] += jnp.dot(lhs, slope, preferred_element_type=F32)

    def body(pass_at, _):
        turn = 2 * pass_at
        backward(jnp.maximum(turn - 1, 0), first_1, slope_1)
        forward(turn, first_0, slope_0)
        backward(turn, first_0, slope_0)
        forward(turn + 1, first_1, slope_1)
        return 0

    passes = lax.div(count + 2 * BATCH - 1, 2 * BATCH)
    lax.fori_loop(0, passes, body, 0)
    backward(jnp.maximum(2 * passes - 1, 0), first_1, slope_1)

    flat = [(pred_all[group] * float(width)).T for group in range(groups)]
    flat = jnp.concatenate(flat, axis=0).astype(BF16)
    for chip in range(chips):
        pred_ref[chip] = flat[chip * 2 * slots * step : (chip + 1) * 2 * slots * step]
    def folded(ref, count):
        sums = [
            jnp.sum(ref[8 * k : 8 * k + 8, :], axis=0, keepdims=True) for k in range(count)
        ]
        sums = jnp.concatenate(sums, axis=0)
        return sums[:, :width] + sums[:, width:]

    col = folded(col_all, col_all.shape[0] // 8)
    bias = folded(bias_all, 8)
    outer = outer_all[:width, :width] + outer_all[width : 2 * width, width:]
    sum_d = outer_all[2 * width : 2 * width + 1, :width] + outer_all[2 * width : 2 * width + 1, width:]
    line = lax.broadcasted_iota(jnp.int32, bias.shape, 0)
    sum_out = jnp.sum(w * outer, axis=0, keepdims=True) + b_pair * sum_d
    vectors = jnp.where(line == 5, sum_d * w_out, bias)
    vectors = jnp.where(line == 6, sum_out, vectors)
    outer = outer * w_out
    high = vectors.astype(BF16).astype(F32)
    rest = (high, vectors - high)
    col_low = col.astype(BF16)
    rows = []
    for block in range(blocks):
        here = row_all[block * pairs : (block + 1) * pairs, :].astype(BF16)
        rows += [here[:, :width], here[:, width:]]
    embs = [cols_ref[...], next_ref[...]]
    contract = (((0,), (0,)), ((), ()))
    grads = (
        lax.dot_general(
            jnp.concatenate(rows, axis=0), emb_ref[...], contract, preferred_element_type=F32
        ).astype(BF16),
        lax.dot_general(
            col_low, jnp.concatenate(embs, axis=0), contract, preferred_element_type=F32
        ).astype(BF16),
    )
    def message(share):
        side, at = share // chips, share % chips
        grad = grads[side][:, at // 2 * width : (at // 2 + 1) * width]
        more = rest[share] if share < 2 else jnp.zeros_like(high)
        small = jnp.concatenate([outer[8 * share : 8 * share + 8], more], axis=0)
        return jnp.concatenate(
            [rows[share], grad[at % 2 * pairs : (at % 2 + 1) * pairs], small.astype(BF16)], axis=0
        )

    for chip in range(chips):
        even, odd = message(2 * chip), message(2 * chip + 1)
        keep_ref[chip] = jnp.where(core == 0, even, odd)
        send_ref[chip] = jnp.where(core == 0, odd, even)
    col_ref[...] = col[:own]
    edge_ref[...] = col_low[own:]


def share_kernel(sum_ref, edge_ref, row_ref, message_ref, mine_ref, send_ref):
    core = place() & 1
    chips, _, width = sum_ref.shape
    pairs = width // 2
    head = width + 16
    slot_rows = mine_ref.shape[1]
    total = jnp.zeros((head, width), F32)
    for chip in range(chips):
        total = total + sum_ref[chip, :head, :].astype(F32)
        first = sum_ref[chip, head : head + slot_rows, :]
        second = sum_ref[chip, head + slot_rows :, :]
        mine_ref[chip] = jnp.where(core == 0, first, second)
        send_ref[chip] = jnp.where(core == 0, second, first)
    total = total.astype(BF16)
    row_ref[...] = total[:pairs]
    for bin_at in range(message_ref.shape[0]):
        message_ref[bin_at, : head - pairs, :] = total[pairs:]
        message_ref[bin_at, head - pairs :, :] = edge_ref[...]


def total_kernel(met_ref, row_ref, col_ref, message_ref):
    here = lax.axis_index("bin")
    bins = met_ref.shape[0]
    width = row_ref.shape[1]
    pairs = row_ref.shape[0]
    edge = col_ref.shape[0] // 2
    count = met_ref.shape[1] - edge
    total = jnp.zeros((count, width), F32)
    before = jnp.zeros((edge, width), F32)
    for bin_at in range(bins):
        total = total + met_ref[bin_at, :count, :].astype(F32)
        near = met_ref[bin_at, count:, :].astype(F32)
        before = jnp.where(here == bin_at + 1, near, before)
    total = total.astype(BF16)
    col = col_ref[...]
    top = (col[:edge] + before).astype(BF16)
    low = col[edge:].astype(BF16)
    for chip in range(message_ref.shape[0]):
        message_ref[chip, :pairs, :] = row_ref[...]
        message_ref[chip, pairs : pairs + count, :] = total
        message_ref[chip, pairs + count : pairs + count + edge, :] = top
        message_ref[chip, pairs + count + edge :, :] = low


def last_kernel(
    mine_ref, other_ref, pred_mine, pred_other, left_w_ref, right_w_ref,
    pred_hbm, emb_hbm, left_hbm, right_hbm, bias_hbm, w_hbm, b_hbm, out_hbm,
    pred_ref, emb_ref, left_ref, right_ref, bias_ref, w_ref, b_ref, out_ref,
    both_ref, flat_ref, col_ref, flip_ref, sems,
):
    core = place() & 1
    width = left_w_ref.shape[1]
    pairs = width // 2
    chips = mine_ref.shape[0]
    slots = pred_ref.shape[0]
    step = width // (2 * chips)
    copies = []

    def leave(source, target):
        copies.append(pltpu.make_async_copy(source, target, sems.at[len(copies)]))
        copies[-1].start()

    lows = []
    for share in range(2 * chips):
        block = jnp.where(core == share % 2, mine_ref[share // 2], other_ref[share // 2])
        both_ref[share * pairs : (share + 1) * pairs, :width] = block[:pairs]
        block = block.astype(F32)
        for k in range(col_ref.shape[0] // width):
            to = k * width + share * step
            at = width + 16 + k * step
            col_ref[to : to + step, :] = block[at : at + step]
        flat_ref[share * pairs : (share + 1) * pairs, :] = block[pairs:width]
        small = block[width : width + 16]
        w_ref[8 * share : 8 * share + 8, :] = small[:8]
        lows.append(small[8:])
    both_ref[:, width:] = col_ref[...].astype(BF16)
    weights = jnp.concatenate([left_w_ref[...], right_w_ref[...]], axis=1)
    part = 2 * width
    for k in range(both_ref.shape[0] // part):
        rows = pl.ds(k * part, part)
        emb_ref[rows, :] = lax.dot_general(
            both_ref[rows, :], weights, (((1,), (1,)), ((), ())), preferred_element_type=F32
        ).astype(BF16)
        leave(emb_ref.at[rows, :], emb_hbm.at[rows, :])
    for side, (grad_ref, grad_hbm) in enumerate(((left_ref, left_hbm), (right_ref, right_hbm))):
        for k in range(chips // 2):
            at = (side * chips // 2 + k) * width
            grad_ref[k * width : (k + 1) * width, :] = flat_ref[at : at + width, :].T
        leave(grad_ref, grad_hbm)
    vectors = lows[0] + lows[1]
    bias_ref[...] = vectors[:5]
    b_ref[...] = vectors[5:6]
    out_ref[...] = vectors[6:7]
    for source, target in ((w_ref, w_hbm), (bias_ref, bias_hbm), (b_ref, b_hbm), (out_ref, out_hbm)):
        leave(source, target)
    for chip in range(chips):
        for ref, side in ((pred_mine, core), (pred_other, 1 - core)):
            block = ref[chip].astype(F32)
            to = pl.multiple_of((2 * chip + side) * step, step)
            for slot in range(slots):
                flip_ref[slot, pl.ds(to, step), :] = block[slot * step : (slot + 1) * step]
    for slot in range(slots):
        pred_ref[slot] = flip_ref[slot].T.astype(BF16)
    leave(pred_ref, pred_hbm)
    for copy in copies:
        copy.wait()


def shape(*dims, dtype=F32):
    return jax.ShapeDtypeStruct(dims, dtype)


def call(kernel, outs, scratch, *args, space=None, out_space=VMEM, limit=32):
    return pl.pallas_call(
        kernel,
        out_shape=outs,
        in_specs=space or [VMEM] * len(args),
        out_specs=(out_space,) * len(outs),
        scratch_shapes=scratch,
        compiler_params=pltpu.CompilerParams(vmem_limit_bytes=limit * 1024 * 1024),
    )(*args)


def swapped(block, axis, bits):
    return lax.ppermute(block, axis, [(i, i ^ bits) for i in range(lax.axis_size(axis))])


def across(block, axis, groups=None):
    return lax.all_to_all(block, axis, 0, 0, axis_index_groups=groups, tiled=True)


def per_device(embeddings, w_left, w_right, pair_bias, w_pair, b_pair, w_out, tile_list, target):
    tile = place()
    core = lax.rem(tile, 2)
    slots, width = target.shape[2:4]
    rows, features = embeddings.shape
    blocks = rows // width
    pairs = width // 2
    shares = lax.axis_size("tile")
    chips = shares // 2
    step = width // shares
    part = rows // shares
    edge = part // 2
    target = target[0, 0]
    lists = jnp.transpose(tile_list, (0, 3, 1, 2)).reshape(3, 1, slots)

    emb_cols = lax.dynamic_slice_in_dim(
        embeddings.reshape(blocks, shares, step, features), tile, 1, 1
    ).reshape(part, features)
    target_other = swapped(target, "tile", 1)
    lists_other = swapped(lists, "tile", 1)
    bins = lax.axis_size("bin")
    emb_next = lax.ppermute(emb_cols[:edge], "bin", [(k + 1, k) for k in range(bins - 1)])
    consts = jnp.concatenate(
        [pair_bias, b_pair[None], w_out[None], jnp.zeros((1, width), F32)], axis=0
    )
    (target_send,) = call(
        split_kernel,
        (shape(chips, 2 * (slots + 1) * step, width, dtype=BF16),),
        [pltpu.VMEM((2 * slots, width, width), F32), pltpu.VMEM((2 * step, width), F32)],
        lists, lists_other, target, target_other,
    )
    groups = [list(range(k, shares, 2)) for k in range(2)]
    target_all = across(target_send, "tile", groups)

    chunk = (BATCH * step * pairs, 2 * width)
    grouped = (slots * shares * step // width + 1, width, width)
    half = shape(chips, width + 16, width, dtype=BF16)
    sums, sums_send, pred, col, col_edge = call(
        pair_kernel,
        (
            half,
            half,
            shape(chips, 2 * slots * step, width, dtype=BF16),
            shape(part, width),
            shape(edge, width, dtype=BF16),
        ),
        [
            pltpu.SMEM((3, slots * shares + 2 * BATCH), jnp.int32),
            pltpu.SMEM((3, shares, width), jnp.int32),
            pltpu.SemaphoreType.DMA,
            pltpu.VMEM((3, shares, width), jnp.int32),
            pltpu.VMEM((rows // 2, 2 * width), F32),
            pltpu.VMEM((rows, width), F32),
            pltpu.VMEM((part + edge, width), F32),
            pltpu.VMEM(grouped, F32),
            pltpu.VMEM(grouped, F32),
            pltpu.VMEM((rows // 2, 2 * width), F32),
            pltpu.VMEM((8 * (part + edge), 2 * width), F32),
            pltpu.VMEM((2 * width + 16, 2 * width), F32),
            pltpu.VMEM((64, 2 * width), F32),
            pltpu.VMEM((2 * width, 2 * width), BF16),
            pltpu.VMEM((2 * width, 2 * width), BF16),
            pltpu.VMEM((2 * width, 2 * width), BF16),
            pltpu.VMEM((1, 2 * width), F32),
            pltpu.VMEM((1, 2 * width), F32),
            pltpu.VMEM(chunk, BF16),
            pltpu.VMEM(chunk, BF16),
            pltpu.VMEM(chunk, BF16),
            pltpu.VMEM(chunk, BF16),
        ],
        embeddings, emb_cols, emb_next, w_left, w_right, consts, target_all, w_pair,
    )
    sums = (sums.astype(F32) + swapped(sums_send, "tile", 1).astype(F32)).astype(BF16)
    sums = across(jnp.concatenate([sums, pred], axis=1), "tile", groups)
    row, weight, pred_mine, pred_send = call(
        share_kernel,
        (
            shape(pairs, width, dtype=BF16),
            shape(bins, pairs + 16 + edge, width, dtype=BF16),
            shape(chips, slots * step, width, dtype=BF16),
            shape(chips, slots * step, width, dtype=BF16),
        ),
        [], sums, col_edge,
    )
    weight = across(weight, "bin")
    (mine,) = call(
        total_kernel,
        (shape(chips, width + 16 + part, width, dtype=BF16),),
        [], weight, row, col,
    )
    mine = across(mine, "tile", groups)
    mine, pred_send = lax.optimization_barrier((mine, pred_send))
    pred_other = swapped(pred_send, "tile", 1)
    other = swapped(mine, "tile", 1)
    outs = (
        shape(slots, width, width, dtype=BF16),
        shape(rows, features, dtype=BF16),
        shape(features, width),
        shape(features, width),
        shape(5, width),
        shape(width, width),
        shape(1, width),
        shape(1, width),
    )
    outs = call(
        last_kernel,
        outs,
        [pltpu.VMEM(out.shape, out.dtype) for out in outs]
        + [
            pltpu.VMEM((rows, 2 * width), BF16),
            pltpu.VMEM((2 * features, width), F32),
            pltpu.VMEM((rows, width), F32),
            pltpu.VMEM((slots, width, width), F32),
            pltpu.SemaphoreType.DMA((rows // (2 * width) + 7,)),
        ],
        mine, other, pred_mine, pred_other, w_left, w_right, out_space=HBM,
    )
    return (outs[0][None, None], *outs[1:6], outs[6][0], outs[7][0])


def solution(mesh):
    return jax.shard_map(
        per_device,
        mesh=mesh,
        in_specs=(
            P("bin", None),
            P(),
            P(),
            P(),
            P(),
            P(),
            P(),
            P("bin", "tile", None, None),
            P("bin", "tile", None, None, None),
        ),
        out_specs=(
            P("bin", "tile", None, None, None),
            P("bin", None),
            P(),
            P(),
            P(),
            P(),
            P(),
            P(),
        ),
        check_vma=False,
    )
```
